256 devices in a mesh: ctx: 16 (over z, core), vocab: 16 (over x, y).
Axes of the slice: x: 4, y: 4, z: 8, core: 2. Of those that a mesh axis runs over, the one named last changes fastest.
Arguments:
- hidden_states: bfloat16 [2048, 3584], P('ctx'), may hold values from -40 to 40, as said below
- head_weight: bfloat16 [3584, 81920], P(None, ('ctx', 'vocab')), may hold values from -3 to 3, as said below
- token_ids: int32 [2048], P('ctx'), may hold values from 0 to 81919
- response_mask: int32 [2048], P('ctx'), may hold values 0 or 1
- teacher_logprob: float32 [2048], P('ctx'), may hold values from -18 to -8
Outputs:
- hidden_grad: bfloat16 [2048, 3584], P('ctx', 'vocab')
- head_grad: bfloat16 [3584, 81920], P(None, ('ctx', 'vocab'))
The draws below stay inside these ranges and needn't reach their ends.
Inputs may be any that keep to these rules, and one draw needn't show every extreme that they name: `hidden_states`: rows of scale about 1 to 4; a few rows may be strongly aligned with head columns. `head_weight`: head entries of order 3 / sqrt(3584).
All inputs are finite; a program needn't handle non-finite values. No bound on the sum of `response_mask` on one device may be relied on, other than what follows from the above.
Results may differ from the reference program's by a relative error of at most 0.02.
Values may be sent and summed in bfloat16 or wider, within the bound.
No kernel may reach another device: no remote copies, remote signals or barrier semaphores. Data moves between devices by JAX's collectives and lax.ppermute only.
A program may use at most 128 MiB of HBM per device.

```python
import math
import jax
import jax.numpy as jnp
import numpy as np
from jax import lax

D = 3584
VOC_DEV = 320
TOKENS = 2048
VOCAB = 81920


def shared_head(source):
    values = jax.random.truncated_normal(source, -6.0, 6.0, (D, VOCAB), jnp.float32)
    return values * (3.0 / math.sqrt(D))


def draw_head_weight(key, part):
    return shared_head(key).astype(jnp.bfloat16)


def draw_hidden_states(key, part):
    key = jax.random.fold_in(key, 11)
    keys = jax.random.split(key, 1)
    normal_rows = jax.random.truncated_normal(keys[0], -6.0, 6.0, (TOKENS, D), jnp.float32)
    return jnp.clip(normal_rows, -40.0, 40.0).astype(jnp.bfloat16)


def with_ends(array, rng, least, high):
    dims = array.shape
    index_at = [jax.random.randint(jax.random.fold_in(rng, axis), (), 0, dims[axis]) for axis in range(len(dims))]
    array = array.at[tuple(index_at)].set(least)
    longest = dims.index(max(dims))
    index_at[longest] = (index_at[longest] + 1) % dims[longest]
    return array.at[tuple(index_at)].set(high)


def level_of(own_key, shape, pieces, smallest, largest):
    factor_of = 1.0
    for dim, blocks in pieces:
        draws = jax.random.uniform(jax.random.fold_in(jax.random.fold_in(own_key, 6), dim), (blocks,), jnp.float32, smallest / len(pieces), largest / len(pieces))
        factor_of = factor_of * jnp.repeat(jnp.exp(draws), shape[dim] // blocks).reshape((-1,) + (1,) * (len(shape) - 1 - dim))
    return factor_of


def ranked_wide(stream_key, shape, number_of, skew):
    weights = [min(1 << octave, number_of + 1 - (1 << octave)) * (1 << 20) // math.isqrt((1 << octave) ** skew) + 1 for octave in range((number_of + 1).bit_length()) if 1 << octave <= number_of]
    scale = 1 + sum(weights) // (1 << 30)
    table = np.cumsum(np.array([max(1, weight // scale) for weight in weights]))
    ticket = jax.random.randint(jax.random.fold_in(stream_key, 1), shape, 0, int(table[len(weights) - 1]))
    start = jnp.left_shift(1, jnp.searchsorted(jnp.asarray(table, jnp.int32), ticket, side="right").astype(jnp.int32))
    grade = start - 1 + jax.random.randint(jax.random.fold_in(stream_key, 4), shape, 0, 1 << 30) % jnp.minimum(start, number_of + 1 - start)
    return jax.random.permutation(jax.random.fold_in(stream_key, 2), number_of)[grade].astype(jnp.int32)


def setup_inputs(seed: int = 0) -> dict:
    splits = jax.random.split(jax.random.key(seed), 6)
    return {
        "hidden_states": draw_hidden_states(jax.random.fold_in(splits[5], 71), 0),
        "head_weight": draw_head_weight(jax.random.fold_in(splits[5], 71), 0),
        "token_ids": with_ends(ranked_wide(splits[2], (TOKENS,), VOCAB, 2), jax.random.fold_in(splits[2], 3), 0, VOCAB - 1).astype(jnp.int32),
        "response_mask": with_ends((jax.random.randint(splits[3], (TOKENS,), 0, 8) < 7).astype(jnp.int32), jax.random.fold_in(splits[3], 1), 0, 1),
        "teacher_logprob": jnp.clip(-18.0 + 10.0 * jax.random.uniform(splits[4], (TOKENS,), jnp.float32) ** level_of(splits[4], (TOKENS,), ((0, 16),), -0.2, 0.2), -18.0, -8.0),
    }


def combine_stats(left, right):
    left_max, left_sum, left_pick = left
    right_max, right_sum, right_pick = right
    merged = jnp.maximum(left_max, right_max)
    joined = left_sum * jnp.exp(left_max - merged) + right_sum * jnp.exp(right_max - merged)
    return (merged, joined, left_pick + right_pick)


def block_stats(logits, matches):
    row_max = jnp.max(logits, axis=1)
    exp_sum = jnp.sum(jnp.exp(logits - row_max[:, None]), axis=1)
    picked = jnp.sum(jnp.where(matches, logits, jnp.float32(0.0)), axis=1)
    return (row_max, exp_sum, picked)


def reverse_cumsum(values):
    return jnp.flip(jnp.cumsum(jnp.flip(values)))


def reference(hidden_states, head_weight, token_ids, response_mask, teacher_logprob):
    blocks = VOCAB // VOC_DEV

    def block_logits(index):
        column_start = (index * VOC_DEV).astype(jnp.int32)
        weights = lax.dynamic_slice_in_dim(head_weight, column_start, VOC_DEV, 1)
        logits = jnp.dot(hidden_states, weights, preferred_element_type=jnp.float32)
        columns = column_start + jnp.arange(VOC_DEV, dtype=jnp.int32)
        matches = token_ids.astype(jnp.int32)[:, None] == columns[None, :]
        return weights, logits, matches

    def stats_step(carry, index):
        weights, logits, matches = block_logits(index)
        return combine_stats(carry, block_stats(logits, matches)), None

    starting = (jnp.full((TOKENS,), -jnp.inf, jnp.float32), jnp.zeros((TOKENS,), jnp.float32), jnp.zeros((TOKENS,), jnp.float32))
    indices = jnp.arange(blocks, dtype=jnp.int32)
    (row_max, exp_sum, picked), unused = lax.scan(stats_step, starting, indices)
    log_norm = row_max + jnp.log(exp_sum)
    mask = response_mask.astype(jnp.float32)
    ratio = mask * (picked - log_norm - teacher_logprob)
    token_weight = mask * reverse_cumsum(ratio) / float(TOKENS)

    def grad_step(feature_grad, index):
        weights, logits, matches = block_logits(index)
        softmax_part = jnp.exp(logits - log_norm[:, None])
        logit_grad = (token_weight[:, None] * (matches.astype(jnp.float32) - softmax_part)).astype(jnp.bfloat16)
        partial_sum = lax.dot_general(logit_grad, weights, (((1,), (1,)), ((), ())), preferred_element_type=jnp.float32)
        rounded = lax.optimization_barrier(partial_sum.astype(jnp.bfloat16)).astype(jnp.float32)
        head_block = lax.dot_general(hidden_states, logit_grad, (((0,), (0,)), ((), ())), preferred_element_type=jnp.float32)
        return feature_grad + rounded, head_block.astype(jnp.bfloat16)

    feature_grad, head_blocks = lax.scan(grad_step, jnp.zeros((TOKENS, D), jnp.float32), indices)
    head_grad = jnp.transpose(head_blocks, (1, 0, 2)).reshape(D, VOCAB)
    return (feature_grad.astype(jnp.bfloat16), head_grad)
```

```python
import jax
import jax.numpy as jnp
from jax import lax
from jax.sharding import Mesh, PartitionSpec as P

F32 = jnp.float32
BF16 = jnp.bfloat16
Z, CORES, X, Y = 8, 2, 4, 4
PLANE = X * Y
SWAP = [(0, 1), (1, 0)]


def broadcast_gather(part, axes, count):
    copies = jnp.broadcast_to(part[None], (count,) + part.shape)
    return lax.all_to_all(copies, axes, 0, 0, tiled=True)


def merge_stats(parts):
    top = jnp.max(parts[:, 0], axis=0)
    total = jnp.sum(parts[:, 1] * jnp.exp(parts[:, 0] - top[None]), axis=0)
    return jnp.stack([top, total, jnp.sum(parts[:, 2], axis=0)])


def on_device(hidden, weight, token_ids, response_mask, teacher_logprob):
    own_rows, features = hidden.shape
    columns_here = weight.shape[1]
    core, z = lax.axis_index("core"), lax.axis_index("z")
    rows = Z * own_rows
    tokens = rows * CORES

    other_weight = lax.ppermute(weight, "core", SWAP)
    both = jnp.concatenate([weight, other_weight], axis=1)
    gathered = lax.all_gather(hidden, "z", axis=0, tiled=True)
    facts = jnp.stack(
        [token_ids.astype(F32), response_mask.astype(F32), teacher_logprob]
    )
    facts = lax.all_gather(facts, ("z", "core"), axis=0).reshape(Z, CORES, 3, own_rows)
    mine = lax.dynamic_index_in_dim(facts, core, 1, False)
    ids = mine[:, 0].astype(jnp.int32).reshape(rows)

    place = lax.axis_index("x") * Y + lax.axis_index("y")
    first = ((z * CORES + core) * PLANE + place) * columns_here
    second = ((z * CORES + 1 - core) * PLANE + place) * columns_here
    span = jnp.arange(columns_here, dtype=jnp.int32)
    columns = jnp.concatenate([first + span, second + span])

    logits = jnp.dot(gathered, both, preferred_element_type=F32)
    matches = ids[:, None] == columns[None, :]
    top = jnp.max(logits, axis=1)
    total = jnp.sum(jnp.exp(logits - top[:, None]), axis=1)
    picked = jnp.sum(jnp.where(matches, logits, F32(0.0)), axis=1)
    stats = jnp.stack([top, total, picked])

    share = rows // PLANE
    stats = stats.reshape(3, PLANE, share).transpose(1, 0, 2)
    stats = merge_stats(lax.all_to_all(stats, ("x", "y"), 0, 0, tiled=True))
    stats = merge_stats(broadcast_gather(stats, "z", Z))
    final = jnp.stack([stats[0] + jnp.log(stats[1]), stats[2]])
    final = broadcast_gather(final, ("core", "x", "y"), CORES * PLANE)
    final = final.reshape(CORES, PLANE, 2, share).transpose(0, 2, 1, 3)
    final = final.reshape(CORES, 2, Z, own_rows)

    mask = facts[:, :, 1]
    norms, picks = final[:, 0].transpose(1, 0, 2), final[:, 1].transpose(1, 0, 2)
    ratio = (mask * (picks - norms - facts[:, :, 2])).reshape(Z * CORES, own_rows)
    place_in = jnp.arange(own_rows, dtype=jnp.int32)
    later = (place_in[None, :] >= place_in[:, None]).astype(F32)
    within = jnp.sum(ratio[:, None, :] * later[None], axis=2)
    shard = jnp.arange(Z * CORES, dtype=jnp.int32)
    after = (shard[None, :] > shard[:, None]).astype(F32)
    beyond = jnp.sum(jnp.sum(ratio, axis=1)[None, :] * after, axis=1)
    weights = mask * (within + beyond[:, None]).reshape(Z, CORES, own_rows) / float(tokens)
    weights = lax.dynamic_index_in_dim(weights, core, 1, False).reshape(rows)
    norm = lax.dynamic_index_in_dim(norms, core, 1, False).reshape(rows)

    grad = weights[:, None] * (matches.astype(F32) - jnp.exp(logits - norm[:, None]))
    grad = grad.astype(BF16)

    partial = lax.dot_general(
        grad, both, (((1,), (1,)), ((), ())), preferred_element_type=F32
    ).astype(BF16)
    mine = lax.psum_scatter(partial, "z", scatter_dimension=0, tiled=True)
    cut = features // PLANE
    blocks = mine.reshape(own_rows, PLANE, cut).transpose(1, 0, 2)
    blocks = lax.all_to_all(blocks, ("x", "y"), 0, 0, tiled=True)
    hidden_grad = jnp.sum(blocks.astype(F32), axis=0).astype(BF16)

    far = lax.dot_general(
        gathered, grad[:, columns_here:], (((0,), (0,)), ((), ())), preferred_element_type=F32
    ).astype(BF16)
    far = lax.ppermute(far, "core", SWAP)
    near = lax.dot_general(
        gathered, grad[:, :columns_here], (((0,), (0,)), ((), ())), preferred_element_type=F32
    )
    head_grad = (near + far.astype(F32)).astype(BF16)
    return hidden_grad, head_grad


def solution(mesh):
    fine = Mesh(mesh.devices.reshape(Z, CORES, X, Y), ("z", "core", "x", "y"))
    by_token = ("z", "core")
    by_column = P(None, ("z", "core", "x", "y"))
    return jax.shard_map(
        on_device,
        mesh=fine,
        in_specs=(P(by_token, None), by_column, P(by_token), P(by_token), P(by_token)),
        out_specs=(P(by_token, ("x", "y")), by_column),
        check_vma=False,
    )
```

```python
import jax
import jax.numpy as jnp
from jax import lax
from jax.sharding import Mesh, PartitionSpec as P

F32 = jnp.float32
BF16 = jnp.bfloat16
Z, CORES, X, Y = 8, 2, 4, 4
PLANE = X * Y
SWAP = [(0, 1), (1, 0)]
HALVES, GROUPS = 2, 8


def broadcast_gather(part, axes, count):
    copies = jnp.broadcast_to(part[None], (count,) + part.shape)
    return lax.all_to_all(copies, axes, 0, 0, tiled=True)


def merge_stats(parts):
    top = jnp.max(parts[:, 0], axis=0)
    total = jnp.sum(parts[:, 1] * jnp.exp(parts[:, 0] - top[None]), axis=0)
    return jnp.stack([top, total, jnp.sum(parts[:, 2], axis=0)])


def block_stats(logits, matches):
    top = jnp.max(logits, axis=1)
    total = jnp.sum(jnp.exp(logits - top[:, None]), axis=1)
    picked = jnp.sum(jnp.where(matches, logits, F32(0.0)), axis=1)
    return jnp.stack([top, total, picked])


def dot(left, right, contract):
    return lax.dot_general(left, right, (contract, ((), ())), preferred_element_type=F32)


def on_device(hidden, weight, token_ids, response_mask, teacher_logprob):
    own_rows, features = hidden.shape
    columns_here = weight.shape[1]
    core, z = lax.axis_index("core"), lax.axis_index("z")
    place = lax.axis_index("x") * Y + lax.axis_index("y")
    split = own_rows // 2
    group = split // GROUPS
    wide = features // HALVES
    half = Z * split
    tokens = own_rows * Z * CORES

    other_weight = lax.ppermute(weight, "core", SWAP)
    both = jnp.concatenate([weight, other_weight], axis=1)

    late = lax.all_gather(hidden[split:], "z", axis=0, tiled=True)
    piece = lax.dynamic_slice(
        hidden, (place % GROUPS * group, place // GROUPS * wide), (group, wide)
    )
    pieces = broadcast_gather(piece, "z", Z).reshape(Z * group, wide)
    early = broadcast_gather(pieces, ("x", "y"), PLANE).reshape(HALVES, half, wide)

    facts = jnp.stack([token_ids.astype(F32), response_mask.astype(F32), teacher_logprob])
    facts = broadcast_gather(facts, ("z", "core"), Z * CORES)

    def local_order(values):
        first = values[:, :split].reshape(Z, GROUPS, group).transpose(1, 0, 2)
        return first.reshape(half), values[:, split:].reshape(half)

    def whole_order(first, second):
        first = first.reshape(GROUPS, Z, group).transpose(1, 0, 2).reshape(Z, split)
        return jnp.concatenate([first, second.reshape(Z, split)], axis=1)

    own_facts = lax.dynamic_index_in_dim(facts.reshape(Z, CORES, 3, own_rows), core, 1, False)
    ids = [part.astype(jnp.int32) for part in local_order(own_facts[:, 0])]

    first = ((z * CORES + core) * PLANE + place) * columns_here
    second = ((z * CORES + 1 - core) * PLANE + place) * columns_here
    span = jnp.arange(columns_here, dtype=jnp.int32)
    columns = jnp.concatenate([first + span, second + span])
    matches = [part[:, None] == columns[None, :] for part in ids]

    logits = [
        dot(early[0], both[:wide], ((1,), (0,))) + dot(early[1], both[wide:], ((1,), (0,))),
        dot(late, both, ((1,), (0,))),
    ]
    stats = jnp.concatenate([block_stats(l, m) for l, m in zip(logits, matches)], axis=1)
    stats = merge_stats(broadcast_gather(stats, "z", Z))
    stats = merge_stats(broadcast_gather(stats, ("x", "y"), PLANE))
    norm = stats[0] + jnp.log(stats[1])
    norms = [norm[:half], norm[half:]]

    change = [
        m.astype(F32) - jnp.exp(l - n[:, None]) for l, m, n in zip(logits, matches, norms)
    ]
    change_low = [part.astype(BF16) for part in change]

    partial = dot(change_low[1], both, ((1,), (1,))).astype(BF16)
    late_sum = lax.psum_scatter(partial, "z", scatter_dimension=0, tiled=True)
    cut = features // PLANE
    partial = dot(both, change_low[0], ((1,), (1,))).astype(BF16)
    shared = lax.all_to_all(partial.reshape(PLANE, cut, half), ("x", "y"), 0, 0, tiled=True)
    early_sum = jnp.sum(shared.astype(F32), axis=0).astype(BF16).T
    early_sum = early_sum.reshape(GROUPS, Z, group, cut).transpose(1, 0, 2, 3)
    early_sum = lax.all_to_all(early_sum.reshape(Z, split, cut), "z", 0, 0, tiled=True)
    early_sum = jnp.sum(early_sum.astype(F32), axis=0)
    late_sum = late_sum.reshape(split, PLANE, cut).transpose(1, 0, 2)
    late_sum = lax.all_to_all(late_sum, ("x", "y"), 0, 0, tiled=True)
    late_sum = jnp.sum(late_sum.astype(F32), axis=0)

    picks = whole_order(stats[2, :half], stats[2, half:])
    known = whole_order(norms[0], norms[1])
    ratio = own_facts[:, 1] * (picks - known - own_facts[:, 2])
    other = lax.ppermute(jnp.sum(ratio, axis=1), "core", SWAP)
    steps = jnp.arange(own_rows, dtype=jnp.int32)
    later = (steps[None, :] >= steps[:, None]).astype(F32)
    within = jnp.sum(ratio[:, None, :] * later[None], axis=2)
    shard = jnp.arange(Z, dtype=jnp.int32)
    after = (shard[None, :] > shard[:, None]).astype(F32)
    at_or_after = jnp.where(core == 0, (shard[None, :] >= shard[:, None]).astype(F32), after)
    beyond = jnp.sum(jnp.sum(ratio, axis=1)[None, :] * after + other[None, :] * at_or_after, axis=1)
    weights = own_facts[:, 1] * (within + beyond[:, None]) / float(tokens)

    own_weight = lax.dynamic_index_in_dim(weights, z, 0, False)
    hidden_grad = jnp.concatenate([early_sum, late_sum]) * own_weight[:, None]

    grads = [(w[:, None] * part).astype(BF16) for w, part in zip(local_order(weights), change)]

    def head_part(low, high):
        first = dot(early, grads[0][:, low:high], ((1,), (0,))).reshape(features, high - low)
        return first + dot(late, grads[1][:, low:high], ((0,), (0,)))

    far = lax.ppermute(head_part(columns_here, 2 * columns_here).astype(BF16), "core", SWAP)
    head_grad = head_part(0, columns_here) + far.astype(F32)
    return hidden_grad.astype(BF16), head_grad.astype(BF16)


def solution(mesh):
    fine = Mesh(mesh.devices.reshape(Z, CORES, X, Y), ("z", "core", "x", "y"))
    by_token = ("z", "core")
    by_column = P(None, ("z", "core", "x", "y"))
    return jax.shard_map(
        on_device,
        mesh=fine,
        in_specs=(P(by_token, None), by_column, P(by_token), P(by_token), P(by_token)),
        out_specs=(P(by_token, ("x", "y")), by_column),
        check_vma=False,
    )
```

```python
import jax
import jax.numpy as jnp
from jax import lax
from jax.experimental import pallas as pl
from jax.experimental.pallas import tpu as pltpu
from jax.sharding import Mesh, PartitionSpec as P

F32 = jnp.float32
BF16 = jnp.bfloat16
Z, CORES, X, Y = 8, 2, 4, 4
PLANE = X * Y
SWAP = [(0, 1), (1, 0)]
WIDE, GROUPS = 4, 4
EARLY = 48
LANES = 128


def broadcast_gather(part, axes, count):
    copies = jnp.broadcast_to(part[None], (count,) + part.shape)
    return lax.all_to_all(copies, axes, 0, 0, tiled=True)


def merge_stats(parts):
    top = jnp.max(parts[:, 0], axis=0)
    total = jnp.sum(parts[:, 1] * jnp.exp(parts[:, 0] - top[None]), axis=0)
    return jnp.stack([top, total, jnp.sum(parts[:, 2], axis=0)])


def dot(left, right, contract):
    return lax.dot_general(left, right, (contract, ((), ())), preferred_element_type=F32)


def params(megabytes):
    return pltpu.CompilerParams(vmem_limit_bytes=megabytes << 20)


def cost(flops, nbytes):
    return pl.CostEstimate(flops=flops, bytes_accessed=nbytes, transcendentals=0)


SMEM = pl.BlockSpec(memory_space=pltpu.SMEM)


def whole(shape):
    return pl.BlockSpec(shape, lambda *_: (0,) * len(shape))


def column_of(starts_ref, shape, low, half):
    row = lax.broadcasted_iota(jnp.int32, shape, 0) + low
    return row + jnp.where(row < half, starts_ref[0], starts_ref[1] - half)


def logits_and_stats(starts, ids, hidden, weight_t):
    columns, features = weight_t.shape
    tokens = hidden.shape[-2]
    block = features // WIDE
    if hidden.ndim == 3:
        spec = pl.BlockSpec((None, tokens, block), lambda k: (k, 0, 0))
    else:
        spec = pl.BlockSpec((tokens, block), lambda k: (0, k))

    def body(starts_ref, ids_ref, h_ref, w_ref, logits_ref, stats_ref):
        step = pl.program_id(0)
        part = dot(w_ref[...], h_ref[...], ((1,), (1,)))

        @pl.when(step == 0)
        def _():
            logits_ref[...] = part

        @pl.when(step > 0)
        def _():
            logits_ref[...] += part

        @pl.when(step == WIDE - 1)
        def _():
            logits = logits_ref[...]
            match = column_of(starts_ref, logits.shape, 0, columns // 2) == ids_ref[...]
            top = jnp.max(logits, axis=0, keepdims=True)
            total = jnp.sum(jnp.exp(logits - top), axis=0, keepdims=True)
            picked = jnp.sum(jnp.where(match, logits, 0.0), axis=0, keepdims=True)
            stats_ref[...] = jnp.concatenate([top, total, picked] + [jnp.zeros_like(top)] * 5)

    return pl.pallas_call(
        body,
        grid=(WIDE,),
        in_specs=[SMEM, whole((1, tokens)), spec, pl.BlockSpec((columns, block), lambda k: (0, k))],
        out_specs=[whole((columns, tokens)), whole((8, tokens))],
        out_shape=[
            jax.ShapeDtypeStruct((columns, tokens), F32),
            jax.ShapeDtypeStruct((8, tokens), F32),
        ],
        compiler_params=params(20),
        cost_estimate=cost(
            2 * columns * tokens * features, 2 * features * (columns + tokens) + 4 * columns * tokens
        ),
    )(starts, ids, hidden, weight_t)


def change_of(starts_ref, logits, norm, ids, low, half):
    match = column_of(starts_ref, logits.shape, low, half) == ids
    return jnp.where(match, 1.0, 0.0) - jnp.exp(logits - norm)


def partial_product(starts, ids, logits_t, norm, weight, by_feature):
    columns, tokens = logits_t.shape
    features = weight.shape[0] if by_feature else weight.shape[1]
    block = features // 7

    def body(starts_ref, ids_ref, logits_ref, norm_ref, w_ref, out_ref, held):
        @pl.when(pl.program_id(0) == 0)
        def _():
            change = change_of(
                starts_ref, logits_ref[...], norm_ref[...], ids_ref[...], 0, columns // 2
            )
            held[...] = (change if by_feature else change.T).astype(BF16)

        if by_feature:
            out = dot(w_ref[...], held[...], ((1,), (0,)))
        else:
            out = dot(held[...], w_ref[...], ((1,), (0,)))
        out_ref[...] = out.astype(BF16)

    if by_feature:
        w_spec = pl.BlockSpec((block, columns), lambda k: (k, 0))
        out_spec, out_dims = pl.BlockSpec((block, tokens), lambda k: (k, 0)), (features, tokens)
        held = (columns, tokens)
    else:
        w_spec = pl.BlockSpec((columns, block), lambda k: (0, k))
        out_spec, out_dims = pl.BlockSpec((tokens, block), lambda k: (0, k)), (tokens, features)
        held = (tokens, columns)
    return pl.pallas_call(
        body,
        grid=(7,),
        in_specs=[SMEM, whole((1, tokens)), whole((columns, tokens)), whole((1, tokens)), w_spec],
        out_specs=out_spec,
        out_shape=jax.ShapeDtypeStruct(out_dims, BF16),
        scratch_shapes=[pltpu.VMEM(held, BF16)],
        compiler_params=params(20),
        cost_estimate=cost(
            2 * columns * tokens * features, 2 * features * (columns + tokens) + 4 * columns * tokens
        ),
    )(starts, ids, logits_t, norm, weight)


def head_half(starts, early, late, low, high, added):
    columns = early[1].shape[0]
    here = high - low
    sizes = [early[1].shape[1], late[1].shape[1]]
    features = late[4].shape[1]
    block = features // WIDE

    def body(starts_ref, *refs):
        sides = [refs[0:5], refs[5:10]]
        rest = refs[10:]
        held = rest[-2:]
        out_ref = rest[-3]

        @pl.when(pl.program_id(0) == 0)
        def _():
            for (ids, logits, norm, scale, _), into in zip(sides, held):
                change = change_of(
                    starts_ref, logits[low:high], norm[...], ids[...], low, columns // 2
                )
                into[...] = (change * scale[...]).astype(BF16)

        total = dot(held[0][...], sides[0][4][...], ((1,), (0,)))
        total += dot(held[1][...], sides[1][4][...], ((1,), (0,)))
        total = total.T
        if added is not None:
            total += rest[0][...].astype(F32)
        out_ref[...] = total.astype(BF16)

    specs = [SMEM]
    for size, spec in zip(
        sizes,
        (
            pl.BlockSpec((None, sizes[0], block), lambda k: (k, 0, 0)),
            pl.BlockSpec((sizes[1], block), lambda k: (0, k)),
        ),
    ):
        specs += [whole((1, size)), whole((columns, size)), whole((1, size)), whole((1, size)), spec]
    out_spec = pl.BlockSpec((block, here), lambda k: (k, 0))
    operands = list(early) + list(late)
    if added is not None:
        specs.append(out_spec)
        operands.append(added)
    return pl.pallas_call(
        body,
        grid=(WIDE,),
        in_specs=specs,
        out_specs=out_spec,
        out_shape=jax.ShapeDtypeStruct((features, here), BF16),
        scratch_shapes=[pltpu.VMEM((here, size), BF16) for size in sizes],
        compiler_params=params(28),
        cost_estimate=cost(
            2 * here * sum(sizes) * features, 2 * features * (here + sum(sizes)) + 4 * columns * sum(sizes)
        ),
    )(starts, *operands)


def pack_facts(token_ids, response_mask, teacher_logprob):
    high = lax.reduce_precision(teacher_logprob, 8, 7)
    rest = teacher_logprob - high
    middle = lax.reduce_precision(rest, 8, 7)
    rows = [
        token_ids // 16384,
        token_ids // 128 % 128,
        token_ids % 128,
        response_mask,
        high,
        middle,
        rest - middle,
        jnp.zeros_like(high),
    ]
    return jnp.stack([row.astype(F32) for row in rows]).astype(BF16)


def unpack_facts(rows):
    rows = rows.astype(F32)
    ids = (rows[:, 0] * 16384.0 + rows[:, 1] * 128.0 + rows[:, 2]).astype(jnp.int32)
    return ids, rows[:, 3], rows[:, 4] + rows[:, 5] + rows[:, 6]


def on_device(hidden, weight, token_ids, response_mask, teacher_logprob):
    own_rows, features = hidden.shape
    columns_here = weight.shape[1]
    core, z = lax.axis_index("core"), lax.axis_index("z")
    place = lax.axis_index("x") * Y + lax.axis_index("y")
    group = EARLY // GROUPS
    wide = features // WIDE
    first_half, second_half = Z * EARLY, Z * (own_rows - EARLY)
    all_rows = first_half + second_half
    tokens = all_rows * CORES

    other_weight = lax.ppermute(weight, "core", SWAP)
    both = jnp.concatenate([weight, other_weight], axis=1)
    both_t = both.T

    late = lax.all_gather(hidden[EARLY:], "z", axis=0, tiled=True)
    piece = lax.dynamic_slice(
        hidden, (place % GROUPS * group, place // GROUPS * wide), (group, wide)
    )
    facts = pack_facts(token_ids, response_mask, teacher_logprob)
    facts = jnp.pad(facts, ((0, group - facts.shape[0]), (0, 0)))
    pieces = broadcast_gather(jnp.concatenate([piece, facts], axis=1), "z", Z)
    ids, mask, teacher = unpack_facts(pieces[:, :8, wide:])
    pieces = pieces[:, :, :wide].reshape(Z * group, wide)
    early = broadcast_gather(pieces, ("x", "y"), PLANE).reshape(WIDE, first_half, wide)

    def local_order(values):
        first = values[:, :EARLY].reshape(Z, GROUPS, group).transpose(1, 0, 2)
        return first.reshape(1, first_half), values[:, EARLY:].reshape(1, second_half)

    def whole_order(values):
        first = values[:first_half].reshape(GROUPS, Z, group).transpose(1, 0, 2)
        second = values[first_half:].reshape(Z, own_rows - EARLY)
        return jnp.concatenate([first.reshape(Z, EARLY), second], axis=1)

    ids = local_order(ids)
    starts = jnp.stack(
        [((z * CORES + c) * PLANE + place) * columns_here for c in (core, 1 - core)]
    ).astype(jnp.int32)

    early_logits, early_stats = logits_and_stats(starts, ids[0], early, both_t)
    late_logits, late_stats = logits_and_stats(starts, ids[1], late, both_t)
    stats = jnp.concatenate([early_stats[:3], late_stats[:3]], axis=1)
    stats = stats.reshape(3 * all_rows // LANES, LANES)

    def merged(stats, axes, count):
        parts = broadcast_gather(stats, axes, count)
        merged = merge_stats(parts.reshape(count, 3, all_rows // LANES, LANES))
        return merged.reshape(3 * all_rows // LANES, LANES)

    stats = merged(stats, "z", Z)
    stats = merged(stats, ("x", "y"), PLANE).reshape(3, all_rows)
    norm = stats[0] + jnp.log(stats[1])
    norms = norm[None, :first_half], norm[None, first_half:]

    partial = partial_product(starts, ids[1], late_logits, norms[1], both_t, False)
    late_sum = lax.psum_scatter(partial, "z", scatter_dimension=0, tiled=True)
    cut = features // PLANE
    partial = partial_product(starts, ids[0], early_logits, norms[0], both, True)
    shared = lax.all_to_all(
        partial.reshape(PLANE, cut, first_half), ("x", "y"), 0, 0, tiled=True
    )
    early_sum = jnp.sum(shared.astype(F32), axis=0).astype(BF16).T
    early_sum = early_sum.reshape(GROUPS, Z, group, cut).transpose(1, 0, 2, 3)
    early_sum = lax.all_to_all(early_sum.reshape(Z, EARLY, cut), "z", 0, 0, tiled=True)
    early_sum = jnp.sum(early_sum.astype(F32), axis=0)
    late_sum = late_sum.reshape(own_rows - EARLY, PLANE, cut).transpose(1, 0, 2)
    late_sum = lax.all_to_all(late_sum, ("x", "y"), 0, 0, tiled=True)
    late_sum = jnp.sum(late_sum.astype(F32), axis=0)

    ratio = mask * (whole_order(stats[2]) - whole_order(norm) - teacher)
    shard_sums = jnp.sum(ratio, axis=1)
    other_sums = lax.ppermute(shard_sums, "core", SWAP)
    steps = jnp.arange(own_rows, dtype=jnp.int32)
    later = (steps[None, :] >= steps[:, None]).astype(F32)
    within = jnp.sum(ratio[:, None, :] * later[None], axis=2)
    shard = jnp.arange(Z, dtype=jnp.int32)
    after = (shard[None, :] > shard[:, None]).astype(F32)
    from_here = (shard[None, :] >= shard[:, None]).astype(F32)
    beyond = shard_sums[None, :] * after
    beyond += other_sums[None, :] * jnp.where(core == 0, from_here, after)
    weights = mask * (within + jnp.sum(beyond, axis=1)[:, None]) / float(tokens)

    own_weight = lax.dynamic_index_in_dim(weights, z, 0, False)
    hidden_grad = jnp.concatenate([early_sum, late_sum]) * own_weight[:, None]

    weights = local_order(weights)
    sides = (
        (ids[0], early_logits, norms[0], weights[0], early),
        (ids[1], late_logits, norms[1], weights[1], late),
    )
    far = head_half(starts, *sides, columns_here, 2 * columns_here, None)
    far = lax.ppermute(far, "core", SWAP)
    head_grad = head_half(starts, *sides, 0, columns_here, far)
    return hidden_grad.astype(BF16), head_grad


def solution(mesh):
    fine = Mesh(mesh.devices.reshape(Z, CORES, X, Y), ("z", "core", "x", "y"))
    by_token = ("z", "core")
    by_column = P(None, ("z", "core", "x", "y"))
    return jax.shard_map(
        on_device,
        mesh=fine,
        in_specs=(P(by_token, None), by_column, P(by_token), P(by_token), P(by_token)),
        out_specs=(P(by_token, ("x", "y")), by_column),
        check_vma=False,
    )
```

```python
import jax
import jax.numpy as jnp
from jax import lax
from jax.experimental import pallas as pl
from jax.experimental.pallas import tpu as pltpu
from jax.sharding import Mesh, PartitionSpec as P

F32 = jnp.float32
BF16 = jnp.bfloat16
Z, CORES, X, Y = 8, 2, 4, 4
PLANE = X * Y
SWAP = [(0, 1), (1, 0)]
WIDE, GROUPS = 4, 4
EARLY = 48
LANES = 128
PARAMS = pltpu.CompilerParams(vmem_limit_bytes=56 << 20)


def broadcast_gather(part, axes, count):
    copies = jnp.broadcast_to(part[None], (count,) + part.shape)
    return lax.all_to_all(copies, axes, 0, 0, tiled=True)


def merge_stats(parts):
    top = jnp.max(parts[:, 0], axis=0)
    total = jnp.sum(parts[:, 1] * jnp.exp(parts[:, 0] - top[None]), axis=0)
    return jnp.stack([top, total, jnp.sum(parts[:, 2], axis=0)])


def dot(left, right, contract):
    return lax.dot_general(left, right, (contract, ((), ())), preferred_element_type=F32)


def cost(flops, nbytes):
    return pl.CostEstimate(flops=flops, bytes_accessed=nbytes, transcendentals=0)


SMEM = pl.BlockSpec(memory_space=pltpu.SMEM)


def whole(shape):
    return pl.BlockSpec(shape, lambda *_: (0,) * len(shape))


def column_of(starts_ref, shape, low, half):
    row = lax.broadcasted_iota(jnp.int32, shape, 0) + low
    return row + jnp.where(row < half, starts_ref[0], starts_ref[1] - half)


def logits_and_stats(starts, ids, hidden, weight_t):
    columns, features = weight_t.shape
    tokens = hidden.shape[-2]
    block = features // WIDE
    if hidden.ndim == 3:
        spec = pl.BlockSpec((None, tokens, block), lambda k: (k, 0, 0))
    else:
        spec = pl.BlockSpec((tokens, block), lambda k: (0, k))

    def body(starts_ref, ids_ref, h_ref, w_ref, logits_ref, stats_ref):
        step = pl.program_id(0)
        part = dot(w_ref[...], h_ref[...], ((1,), (1,)))

        @pl.when(step == 0)
        def _():
            logits_ref[...] = part

        @pl.when(step > 0)
        def _():
            logits_ref[...] += part

        @pl.when(step == WIDE - 1)
        def _():
            logits = logits_ref[...]
            match = column_of(starts_ref, logits.shape, 0, columns // 2) == ids_ref[...]
            top = jnp.max(logits, axis=0, keepdims=True)
            total = jnp.sum(jnp.exp(logits - top), axis=0, keepdims=True)
            picked = jnp.sum(jnp.where(match, logits, 0.0), axis=0, keepdims=True)
            stats_ref[...] = jnp.concatenate([top, total, picked] + [jnp.zeros_like(top)] * 5)

    return pl.pallas_call(
        body,
        grid=(WIDE,),
        in_specs=[SMEM, whole((1, tokens)), spec, pl.BlockSpec((columns, block), lambda k: (0, k))],
        out_specs=[whole((columns, tokens)), whole((8, tokens))],
        out_shape=[
            jax.ShapeDtypeStruct((columns, tokens), F32),
            jax.ShapeDtypeStruct((8, tokens), F32),
        ],
        compiler_params=PARAMS,
        cost_estimate=cost(
            2 * columns * tokens * features, 2 * features * (columns + tokens) + 4 * columns * tokens
        ),
    )(starts, ids, hidden, weight_t)


def change_of(starts_ref, logits, norm, ids, low, half):
    match = column_of(starts_ref, logits.shape, low, half) == ids
    return jnp.where(match, 1.0, 0.0) - jnp.exp(logits - norm)


def partial_product(starts, ids, logits_t, norm, weight_t, by_feature):
    columns, tokens = logits_t.shape
    features = weight_t.shape[1]
    block = features // 7

    def body(starts_ref, ids_ref, logits_ref, norm_ref, w_ref, out_ref, held):
        @pl.when(pl.program_id(0) == 0)
        def _():
            change = change_of(
                starts_ref, logits_ref[...], norm_ref[...], ids_ref[...], 0, columns // 2
            )
            held[...] = (change if by_feature else change.T).astype(BF16)

        if by_feature:
            out = dot(w_ref[...], held[...], ((0,), (0,)))
        else:
            out = dot(held[...], w_ref[...], ((1,), (0,)))
        out_ref[...] = out.astype(BF16)

    if by_feature:
        out_spec, out_dims = pl.BlockSpec((block, tokens), lambda k: (k, 0)), (features, tokens)
        held = (columns, tokens)
    else:
        out_spec, out_dims = pl.BlockSpec((tokens, block), lambda k: (0, k)), (tokens, features)
        held = (tokens, columns)
    return pl.pallas_call(
        body,
        grid=(7,),
        in_specs=[
            SMEM,
            whole((1, tokens)),
            whole((columns, tokens)),
            whole((1, tokens)),
            pl.BlockSpec((columns, block), lambda k: (0, k)),
        ],
        out_specs=out_spec,
        out_shape=jax.ShapeDtypeStruct(out_dims, BF16),
        scratch_shapes=[pltpu.VMEM(held, BF16)],
        compiler_params=PARAMS,
        cost_estimate=cost(
            2 * columns * tokens * features, 2 * features * (columns + tokens) + 4 * columns * tokens
        ),
    )(starts, ids, logits_t, norm, weight_t)


def head_half(starts, early, late, low, high, added):
    columns = early[1].shape[0]
    here = high - low
    sizes = [early[1].shape[1], late[1].shape[1]]
    features = late[4].shape[1]
    block = features // WIDE

    def body(starts_ref, *refs):
        sides = [refs[0:5], refs[5:10]]
        rest = refs[10:]
        held = rest[-2:]
        out_ref = rest[-3]

        @pl.when(pl.program_id(0) == 0)
        def _():
            for (ids, logits, norm, scale, _), into in zip(sides, held):
                change = change_of(
                    starts_ref, logits[low:high], norm[...], ids[...], low, columns // 2
                )
                into[...] = (change * scale[...]).astype(BF16)

        total = dot(held[0][...], sides[0][4][...], ((1,), (0,)))
        total += dot(held[1][...], sides[1][4][...], ((1,), (0,)))
        if added is not None:
            total += rest[0][...].astype(F32)
        out_ref[...] = total.astype(BF16)

    specs = [SMEM]
    for size, spec in zip(
        sizes,
        (
            pl.BlockSpec((None, sizes[0], block), lambda k: (k, 0, 0)),
            pl.BlockSpec((sizes[1], block), lambda k: (0, k)),
        ),
    ):
        specs += [whole((1, size)), whole((columns, size)), whole((1, size)), whole((1, size)), spec]
    out_spec = pl.BlockSpec((here, block), lambda k: (0, k))
    operands = list(early) + list(late)
    if added is not None:
        specs.append(out_spec)
        operands.append(added)
    return pl.pallas_call(
        body,
        grid=(WIDE,),
        in_specs=specs,
        out_specs=out_spec,
        out_shape=jax.ShapeDtypeStruct((here, features), BF16),
        scratch_shapes=[pltpu.VMEM((here, size), BF16) for size in sizes],
        compiler_params=PARAMS,
        cost_estimate=cost(
            2 * here * sum(sizes) * features, 2 * features * (here + sum(sizes)) + 4 * columns * sum(sizes)
        ),
    )(starts, *operands)


def pack_facts(token_ids, response_mask, teacher_logprob):
    high = lax.reduce_precision(teacher_logprob, 8, 7)
    rest = teacher_logprob - high
    middle = lax.reduce_precision(rest, 8, 7)
    rows = [
        token_ids // 16384,
        token_ids // 128 % 128,
        token_ids % 128,
        response_mask,
        high,
        middle,
        rest - middle,
        jnp.zeros_like(high),
    ]
    return jnp.stack([row.astype(F32) for row in rows]).astype(BF16)


def unpack_facts(rows):
    rows = rows.astype(F32)
    ids = (rows[:, 0] * 16384.0 + rows[:, 1] * 128.0 + rows[:, 2]).astype(jnp.int32)
    return ids, rows[:, 3], rows[:, 4] + rows[:, 5] + rows[:, 6]


def on_device(hidden, weight, token_ids, response_mask, teacher_logprob):
    own_rows, features = hidden.shape
    columns_here = weight.shape[1]
    core, z = lax.axis_index("core"), lax.axis_index("z")
    place = lax.axis_index("x") * Y + lax.axis_index("y")
    group = EARLY // GROUPS
    wide = features // WIDE
    first_half, second_half = Z * EARLY, Z * (own_rows - EARLY)
    all_rows = first_half + second_half
    tokens = all_rows * CORES

    weight_t = weight.T
    both_t = jnp.concatenate([weight_t, lax.ppermute(weight_t, "core", SWAP)])

    late = lax.all_gather(hidden[EARLY:], "z", axis=0, tiled=True)
    piece = lax.dynamic_slice(
        hidden, (place % GROUPS * group, place // GROUPS * wide), (group, wide)
    )
    facts = pack_facts(token_ids, response_mask, teacher_logprob)
    facts = jnp.pad(facts, ((0, group - facts.shape[0]), (0, 0)))
    pieces = broadcast_gather(jnp.concatenate([piece, facts], axis=1), "z", Z)
    ids, mask, teacher = unpack_facts(pieces[:, :8, wide:])
    pieces = pieces[:, :, :wide].reshape(Z * group, wide)
    early = broadcast_gather(pieces, ("x", "y"), PLANE).reshape(WIDE, first_half, wide)

    def local_order(values):
        first = values[:, :EARLY].reshape(Z, GROUPS, group).transpose(1, 0, 2)
        return first.reshape(1, first_half), values[:, EARLY:].reshape(1, second_half)

    def whole_order(values):
        first = values[:first_half].reshape(GROUPS, Z, group).transpose(1, 0, 2)
        second = values[first_half:].reshape(Z, own_rows - EARLY)
        return jnp.concatenate([first.reshape(Z, EARLY), second], axis=1)

    ids = local_order(ids)
    starts = jnp.stack(
        [((z * CORES + c) * PLANE + place) * columns_here for c in (core, 1 - core)]
    ).astype(jnp.int32)

    early_logits, early_stats = logits_and_stats(starts, ids[0], early, both_t)
    late_logits, late_stats = logits_and_stats(starts, ids[1], late, both_t)
    stats = jnp.concatenate([early_stats[:3], late_stats[:3]], axis=1)
    stats = stats.reshape(3 * all_rows // LANES, LANES)

    def merged(stats, axes, count):
        parts = broadcast_gather(stats, axes, count)
        merged = merge_stats(parts.reshape(count, 3, all_rows // LANES, LANES))
        return merged.reshape(3 * all_rows // LANES, LANES)

    stats = merged(stats, "z", Z)
    stats = merged(stats, ("x", "y"), PLANE).reshape(3, all_rows)
    norm = stats[0] + jnp.log(stats[1])
    norms = norm[None, :first_half], norm[None, first_half:]

    partial = partial_product(starts, ids[1], late_logits, norms[1], both_t, False)
    late_sum = lax.psum_scatter(partial, "z", scatter_dimension=0, tiled=True)
    cut = features // PLANE
    partial = partial_product(starts, ids[0], early_logits, norms[0], both_t, True)
    shared = lax.all_to_all(
        partial.reshape(PLANE, cut, first_half), ("x", "y"), 0, 0, tiled=True
    )
    early_sum = jnp.sum(shared.astype(F32), axis=0).astype(BF16).T
    early_sum = early_sum.reshape(GROUPS, Z, group, cut).transpose(1, 0, 2, 3)
    early_sum = lax.all_to_all(early_sum.reshape(Z, EARLY, cut), "z", 0, 0, tiled=True)
    early_sum = jnp.sum(early_sum.astype(F32), axis=0)
    late_sum = late_sum.reshape(own_rows - EARLY, PLANE, cut).transpose(1, 0, 2)
    late_sum = lax.all_to_all(late_sum, ("x", "y"), 0, 0, tiled=True)
    late_sum = jnp.sum(late_sum.astype(F32), axis=0)

    ratio = mask * (whole_order(stats[2]) - whole_order(norm) - teacher)
    shard_sums = jnp.sum(ratio, axis=1)
    other_sums = lax.ppermute(shard_sums, "core", SWAP)
    steps = jnp.arange(own_rows, dtype=jnp.int32)
    later = (steps[None, :] >= steps[:, None]).astype(F32)
    within = jnp.sum(ratio[:, None, :] * later[None], axis=2)
    shard = jnp.arange(Z, dtype=jnp.int32)
    after = (shard[None, :] > shard[:, None]).astype(F32)
    from_here = (shard[None, :] >= shard[:, None]).astype(F32)
    beyond = shard_sums[None, :] * after
    beyond += other_sums[None, :] * jnp.where(core == 0, from_here, after)
    weights = mask * (within + jnp.sum(beyond, axis=1)[:, None]) / float(tokens)

    own_weight = lax.dynamic_index_in_dim(weights, z, 0, False)
    hidden_grad = jnp.concatenate([early_sum, late_sum]) * own_weight[:, None]

    weights = local_order(weights)
    sides = (
        (ids[0], early_logits, norms[0], weights[0], early),
        (ids[1], late_logits, norms[1], weights[1], late),
    )
    far = head_half(starts, *sides, columns_here, 2 * columns_here, None)
    far = lax.ppermute(far, "core", SWAP)
    head_grad = head_half(starts, *sides, 0, columns_here, far)
    return hidden_grad.astype(BF16), head_grad.T


def solution(mesh):
    fine = Mesh(mesh.devices.reshape(Z, CORES, X, Y), ("z", "core", "x", "y"))
    by_token = ("z", "core")
    by_column = P(None, ("z", "core", "x", "y"))
    return jax.shard_map(
        on_device,
        mesh=fine,
        in_specs=(P(by_token, None), by_column, P(by_token), P(by_token), P(by_token)),
        out_specs=(P(by_token, ("x", "y")), by_column),
        check_vma=False,
    )
```

```python
import jax
import jax.numpy as jnp
from jax import lax
from jax.experimental import pallas as pl
from jax.experimental.pallas import tpu as pltpu
from jax.sharding import Mesh, PartitionSpec as P

F32 = jnp.float32
BF16 = jnp.bfloat16
Z, CORES, X, Y = 8, 2, 4, 4
PLANE = X * Y
SWAP = [(0, 1), (1, 0)]
WIDE, GROUPS = 4, 4
EARLY = 48
LANES = 128
LIMIT = 28
PARAMS = pltpu.CompilerParams(vmem_limit_bytes=LIMIT << 20)


def broadcast_gather(part, axes, count):
    copies = jnp.broadcast_to(part[None], (count,) + part.shape)
    return lax.all_to_all(copies, axes, 0, 0, tiled=True)


def merge_stats(parts):
    top = jnp.max(parts[:, 0], axis=0)
    total = jnp.sum(parts[:, 1] * jnp.exp(parts[:, 0] - top[None]), axis=0)
    return jnp.stack([top, total, jnp.sum(parts[:, 2], axis=0)])


def dot(left, right, contract):
    return lax.dot_general(left, right, (contract, ((), ())), preferred_element_type=F32)


def cost(flops, nbytes):
    return pl.CostEstimate(flops=flops, bytes_accessed=nbytes, transcendentals=0)


SMEM = pl.BlockSpec(memory_space=pltpu.SMEM)


VMEM = pl.BlockSpec(memory_space=pltpu.VMEM)
ANY = pl.BlockSpec(memory_space=pl.ANY)
HBM = pl.BlockSpec(memory_space=pltpu.HBM)


def column_of(starts_ref, shape, low, half):
    row = lax.broadcasted_iota(jnp.int32, shape, 0) + low
    return row + jnp.where(row < half, starts_ref[0], starts_ref[1] - half)


def feature_block(hidden_ref, k, block):
    if len(hidden_ref.shape) == 3:
        return hidden_ref.at[k]
    return hidden_ref.at[:, pl.ds(k * block, block)]


def logits_and_stats(starts, ids, hidden, weight_t):
    columns, features = weight_t.shape
    tokens = hidden.shape[-2]
    block = features // WIDE

    def body(starts_ref, ids_ref, h_ref, w_ref, logits_ref, stats_ref, held, sems):
        copies = [
            pltpu.make_async_copy(feature_block(h_ref, k, block), held.at[k], sems.at[k])
            for k in range(WIDE)
        ]
        for copy in copies:
            copy.start()
        for k in range(WIDE):
            copies[k].wait()
            part = dot(w_ref[:, k * block : (k + 1) * block], held[k], ((1,), (1,)))
            logits_ref[...] = part if k == 0 else logits_ref[...] + part
        logits = logits_ref[...]
        match = column_of(starts_ref, logits.shape, 0, columns // 2) == ids_ref[...]
        top = jnp.max(logits, axis=0, keepdims=True)
        total = jnp.sum(jnp.exp(logits - top), axis=0, keepdims=True)
        picked = jnp.sum(jnp.where(match, logits, 0.0), axis=0, keepdims=True)
        stats_ref[...] = jnp.concatenate([top, total, picked] + [jnp.zeros_like(top)] * 5)

    return pl.pallas_call(
        body,
        in_specs=[SMEM, VMEM, ANY if hidden.ndim == 3 else HBM, VMEM],
        out_specs=[VMEM, VMEM],
        out_shape=[
            jax.ShapeDtypeStruct((columns, tokens), F32),
            jax.ShapeDtypeStruct((8, tokens), F32),
        ],
        scratch_shapes=[
            pltpu.VMEM((WIDE, tokens, block), BF16),
            pltpu.SemaphoreType.DMA((WIDE,)),
        ],
        compiler_params=PARAMS,
        cost_estimate=cost(
            2 * columns * tokens * features, 2 * features * tokens
        ),
    )(starts, ids, hidden, weight_t)


def change_of(starts_ref, logits, norm, ids, low, half):
    match = column_of(starts_ref, logits.shape, low, half) == ids
    return jnp.where(match, 1.0, 0.0) - jnp.exp(logits - norm)


def partial_product(starts, ids, logits_t, norm, weight_t, by_feature):
    columns, tokens = logits_t.shape
    features = weight_t.shape[1]
    steps = 7
    block = features // steps

    def body(starts_ref, ids_ref, logits_ref, norm_ref, w_ref, out_ref, held, ready, sems):
        change = change_of(
            starts_ref, logits_ref[...], norm_ref[...], ids_ref[...], 0, columns // 2
        )
        held[...] = (change if by_feature else change.T).astype(BF16)

        def send(k):
            span = pl.ds(k * block, block)
            into = out_ref.at[span] if by_feature else out_ref.at[:, span]
            return pltpu.make_async_copy(ready.at[k % 2], into, sems.at[k % 2])

        for k in range(steps):
            weights = w_ref[:, k * block : (k + 1) * block]
            if by_feature:
                out = dot(weights, held[...], ((0,), (0,)))
            else:
                out = dot(held[...], weights, ((1,), (0,)))
            if k >= 2:
                send(k - 2).wait()
            ready[k % 2] = out.astype(BF16)
            send(k).start()
        send(steps - 2).wait()
        send(steps - 1).wait()

    if by_feature:
        out_dims, out_block, held = (features, tokens), (block, tokens), (columns, tokens)
    else:
        out_dims, out_block, held = (tokens, features), (tokens, block), (tokens, columns)
    return pl.pallas_call(
        body,
        in_specs=[SMEM, VMEM, VMEM, VMEM, VMEM],
        out_specs=ANY,
        out_shape=jax.ShapeDtypeStruct(out_dims, BF16),
        scratch_shapes=[
            pltpu.VMEM(held, BF16),
            pltpu.VMEM((2,) + out_block, BF16),
            pltpu.SemaphoreType.DMA((2,)),
        ],
        compiler_params=PARAMS,
        cost_estimate=cost(2 * columns * tokens * features, 2 * features * tokens),
    )(starts, ids, logits_t, norm, weight_t)


def head_parts(starts, early, late):
    columns = early[1].shape[0]
    half = columns // 2
    sizes = [early[1].shape[1], late[1].shape[1]]
    features = late[4].shape[1]
    block = features // WIDE

    def body(starts_ref, *refs):
        sides = [refs[0:5], refs[5:10]]
        near_ref, far_ref = refs[10:12]
        held, blocks = refs[12:14], refs[14:16]
        sems = refs[16]
        copies = [
            [
                pltpu.make_async_copy(
                    feature_block(side[4], k, block), into.at[k], sems.at[number, k]
                )
                for number, (side, into) in enumerate(zip(sides, blocks))
            ]
            for k in range(WIDE)
        ]
        for pair in copies:
            for copy in pair:
                copy.start()
        for (ids, logits, norm, scale, _), into in zip(sides, held):
            change = change_of(starts_ref, logits[...], norm[...], ids[...], 0, half)
            into[...] = (change * scale[...]).astype(BF16)
        for k in range(WIDE):
            total = None
            for copy, grad, hidden in zip(copies[k], held, blocks):
                copy.wait()
                part = dot(grad[...], hidden[k], ((1,), (0,)))
                total = part if total is None else total + part
            near_ref[:, k * block : (k + 1) * block] = total[:half]
            far_ref[:, k * block : (k + 1) * block] = total[half:].astype(BF16)

    return pl.pallas_call(
        body,
        in_specs=[SMEM, VMEM, VMEM, VMEM, VMEM, ANY, VMEM, VMEM, VMEM, VMEM, HBM],
        out_specs=[VMEM, VMEM],
        out_shape=[
            jax.ShapeDtypeStruct((half, features), F32),
            jax.ShapeDtypeStruct((half, features), BF16),
        ],
        scratch_shapes=[pltpu.VMEM((columns, size), BF16) for size in sizes]
        + [pltpu.VMEM((WIDE, size, block), BF16) for size in sizes]
        + [pltpu.SemaphoreType.DMA((2, WIDE))],
        compiler_params=PARAMS,
        cost_estimate=cost(2 * columns * sum(sizes) * features, 2 * features * sum(sizes)),
    )(starts, *early, *late)


def pack_facts(token_ids, response_mask, teacher_logprob):
    high = lax.reduce_precision(teacher_logprob, 8, 7)
    rest = teacher_logprob - high
    middle = lax.reduce_precision(rest, 8, 7)
    rows = [
        token_ids // 16384,
        token_ids // 128 % 128,
        token_ids % 128,
        response_mask,
        high,
        middle,
        rest - middle,
        jnp.zeros_like(high),
    ]
    return jnp.stack([row.astype(F32) for row in rows]).astype(BF16)


def unpack_facts(rows):
    rows = rows.astype(F32)
    ids = (rows[:, 0] * 16384.0 + rows[:, 1] * 128.0 + rows[:, 2]).astype(jnp.int32)
    return ids, rows[:, 3], rows[:, 4] + rows[:, 5] + rows[:, 6]


def on_device(hidden, weight, token_ids, response_mask, teacher_logprob):
    own_rows, features = hidden.shape
    columns_here = weight.shape[1]
    core, z = lax.axis_index("core"), lax.axis_index("z")
    place = lax.axis_index("x") * Y + lax.axis_index("y")
    group = EARLY // GROUPS
    wide = features // WIDE
    first_half, second_half = Z * EARLY, Z * (own_rows - EARLY)
    all_rows = first_half + second_half
    tokens = all_rows * CORES

    weight_t = weight.T
    both_t = jnp.concatenate([weight_t, lax.ppermute(weight_t, "core", SWAP)])

    late = lax.all_gather(hidden[EARLY:], "z", axis=0, tiled=True)
    piece = lax.dynamic_slice(
        hidden, (place % GROUPS * group, place // GROUPS * wide), (group, wide)
    )
    facts = pack_facts(token_ids, response_mask, teacher_logprob)
    facts = jnp.pad(facts, ((0, group - facts.shape[0]), (0, 0)))
    pieces = broadcast_gather(jnp.concatenate([piece, facts], axis=1), "z", Z)
    ids, mask, teacher = unpack_facts(pieces[:, :8, wide:])
    pieces = pieces[:, :, :wide].reshape(Z * group, wide)
    early = broadcast_gather(pieces, ("x", "y"), PLANE).reshape(WIDE, first_half, wide)

    def local_order(values):
        first = values[:, :EARLY].reshape(Z, GROUPS, group).transpose(1, 0, 2)
        return first.reshape(1, first_half), values[:, EARLY:].reshape(1, second_half)

    def whole_order(values):
        first = values[:first_half].reshape(GROUPS, Z, group).transpose(1, 0, 2)
        second = values[first_half:].reshape(Z, own_rows - EARLY)
        return jnp.concatenate([first.reshape(Z, EARLY), second], axis=1)

    ids = local_order(ids)
    starts = jnp.stack(
        [((z * CORES + c) * PLANE + place) * columns_here for c in (core, 1 - core)]
    ).astype(jnp.int32)

    early_logits, early_stats = logits_and_stats(starts, ids[0], early, both_t)
    late_logits, late_stats = logits_and_stats(starts, ids[1], late, both_t)
    stats = jnp.concatenate([early_stats[:3], late_stats[:3]], axis=1)
    stats = stats.reshape(3 * all_rows // LANES, LANES)

    def merged(stats, axes, count):
        parts = broadcast_gather(stats, axes, count)
        merged = merge_stats(parts.reshape(count, 3, all_rows // LANES, LANES))
        return merged.reshape(3 * all_rows // LANES, LANES)

    stats = merged(stats, "z", Z)
    stats = merged(stats, ("x", "y"), PLANE).reshape(3, all_rows)
    norm = stats[0] + jnp.log(stats[1])
    norms = norm[None, :first_half], norm[None, first_half:]

    partial = partial_product(starts, ids[1], late_logits, norms[1], both_t, False)
    late_sum = lax.psum_scatter(partial, "z", scatter_dimension=0, tiled=True)
    cut = features // PLANE
    partial = partial_product(starts, ids[0], early_logits, norms[0], both_t, True)
    shared = lax.all_to_all(
        partial.reshape(PLANE, cut, first_half), ("x", "y"), 0, 0, tiled=True
    )
    early_sum = jnp.sum(shared.astype(F32), axis=0).astype(BF16).T
    early_sum = early_sum.reshape(GROUPS, Z, group, cut).transpose(1, 0, 2, 3)
    early_sum = lax.all_to_all(early_sum.reshape(Z, EARLY, cut), "z", 0, 0, tiled=True)
    early_sum = jnp.sum(early_sum.astype(F32), axis=0)
    late_sum = late_sum.reshape(own_rows - EARLY, PLANE, cut).transpose(1, 0, 2)
    late_sum = lax.all_to_all(late_sum, ("x", "y"), 0, 0, tiled=True)
    late_sum = jnp.sum(late_sum.astype(F32), axis=0)

    ratio = mask * (whole_order(stats[2]) - whole_order(norm) - teacher)
    shard_sums = jnp.sum(ratio, axis=1)
    other_sums = lax.ppermute(shard_sums, "core", SWAP)
    steps = jnp.arange(own_rows, dtype=jnp.int32)
    later = (steps[None, :] >= steps[:, None]).astype(F32)
    within = jnp.sum(ratio[:, None, :] * later[None], axis=2)
    shard = jnp.arange(Z, dtype=jnp.int32)
    after = (shard[None, :] > shard[:, None]).astype(F32)
    from_here = (shard[None, :] >= shard[:, None]).astype(F32)
    beyond = shard_sums[None, :] * after
    beyond += other_sums[None, :] * jnp.where(core == 0, from_here, after)
    weights = mask * (within + jnp.sum(beyond, axis=1)[:, None]) / float(tokens)

    own_weight = lax.dynamic_index_in_dim(weights, z, 0, False)
    hidden_grad = jnp.concatenate([early_sum, late_sum]) * own_weight[:, None]

    weights = local_order(weights)
    sides = (
        (ids[0], early_logits, norms[0], weights[0], early),
        (ids[1], late_logits, norms[1], weights[1], late),
    )
    near, far = head_parts(starts, *sides)
    head_grad = near + lax.ppermute(far, "core", SWAP).astype(F32)
    return hidden_grad.astype(BF16), head_grad.astype(BF16).T


def solution(mesh):
    fine = Mesh(mesh.devices.reshape(Z, CORES, X, Y), ("z", "core", "x", "y"))
    by_token = ("z", "core")
    by_column = P(None, ("z", "core", "x", "y"))
    return jax.shard_map(
        on_device,
        mesh=fine,
        in_specs=(P(by_token, None), by_column, P(by_token), P(by_token), P(by_token)),
        out_specs=(P(by_token, ("x", "y")), by_column),
        check_vma=False,
    )
```

```python
import jax
import jax.numpy as jnp
from jax import lax
from jax.experimental import pallas as pl
from jax.experimental.pallas import tpu as pltpu
from jax.sharding import Mesh, PartitionSpec as P

F32 = jnp.float32
BF16 = jnp.bfloat16
Z, CORES, X, Y = 8, 2, 4, 4
PLANE = X * Y
SWAP = [(0, 1), (1, 0)]
WIDE, GROUPS = 4, 4
EARLY = 48
LANES = 128
LIMIT = 56
PARAMS = pltpu.CompilerParams(vmem_limit_bytes=LIMIT << 20)


def broadcast_gather(part, axes, count):
    copies = jnp.broadcast_to(part[None], (count,) + part.shape)
    return lax.all_to_all(copies, axes, 0, 0, tiled=True)


def merge_stats(parts):
    top = jnp.max(parts[:, 0], axis=0)
    total = jnp.sum(parts[:, 1] * jnp.exp(parts[:, 0] - top[None]), axis=0)
    return jnp.stack([top, total, jnp.sum(parts[:, 2], axis=0)])


def dot(left, right, contract):
    return lax.dot_general(left, right, (contract, ((), ())), preferred_element_type=F32)


def cost(flops, nbytes):
    return pl.CostEstimate(flops=flops, bytes_accessed=nbytes, transcendentals=0)


SMEM = pl.BlockSpec(memory_space=pltpu.SMEM)


VMEM = pl.BlockSpec(memory_space=pltpu.VMEM)
ANY = pl.BlockSpec(memory_space=pl.ANY)


def column_of(starts_ref, shape, low, half):
    row = lax.broadcasted_iota(jnp.int32, shape, 0) + low
    return row + jnp.where(row < half, starts_ref[0], starts_ref[1] - half)


def logits_and_stats(starts, ids, early, late, weight_t):
    columns, features = weight_t.shape
    sizes = early.shape[1], late.shape[0]
    tokens = sum(sizes)
    spans = (0, sizes[0]), (sizes[0], tokens)
    block = features // WIDE

    def body(starts_ref, ids_ref, e_ref, l_ref, w_ref, logits_ref, stats_ref, w, e, l, held, sems, out):
        def span(k):
            return pl.ds(k * block, block)

        copies = [
            (
                pltpu.make_async_copy(w_ref.at[:, span(k)], w.at[k], sems.at[k, 0]),
                pltpu.make_async_copy(e_ref.at[k], e.at[k], sems.at[k, 1]),
                pltpu.make_async_copy(l_ref.at[:, span(k)], l.at[k], sems.at[k, 2]),
            )
            for k in range(WIDE)
        ]
        for copy in copies[0] + copies[1]:
            copy.start()
        sends = []
        for k in range(WIDE):
            for copy in copies[k]:
                copy.wait()
            if k + 2 < WIDE:
                for copy in copies[k + 2]:
                    copy.start()
            for side, (hidden, (low, high)) in enumerate(zip((e, l), spans)):
                part = dot(w[k], hidden[k], ((1,), (1,)))
                held[:, low:high] = part if k == 0 else held[:, low:high] + part
                if k == WIDE - 1:
                    send = pltpu.make_async_copy(
                        held.at[:, pl.ds(low, high - low)],
                        logits_ref.at[:, pl.ds(low, high - low)],
                        out.at[side],
                    )
                    send.start()
                    sends.append(send)
        for low, high in spans:
            logits = held[:, low:high]
            match = column_of(starts_ref, logits.shape, 0, columns // 2) == ids_ref[:, low:high]
            top = jnp.max(logits, axis=0, keepdims=True)
            total = jnp.sum(jnp.exp(logits - top), axis=0, keepdims=True)
            picked = jnp.sum(jnp.where(match, logits, 0.0), axis=0, keepdims=True)
            stats_ref[:, low:high] = jnp.concatenate(
                [top, total, picked] + [jnp.zeros_like(top)] * 5
            )
        for send in sends:
            send.wait()

    return pl.pallas_call(
        body,
        in_specs=[SMEM, VMEM, ANY, ANY, ANY],
        out_specs=[ANY, VMEM],
        out_shape=[
            jax.ShapeDtypeStruct((columns, tokens), F32),
            jax.ShapeDtypeStruct((8, tokens), F32),
        ],
        scratch_shapes=[
            pltpu.VMEM((WIDE, columns, block), BF16),
            pltpu.VMEM((WIDE, sizes[0], block), BF16),
            pltpu.VMEM((WIDE, sizes[1], block), BF16),
            pltpu.VMEM((columns, tokens), F32),
            pltpu.SemaphoreType.DMA((WIDE, 3)),
            pltpu.SemaphoreType.DMA((2,)),
        ],
        compiler_params=PARAMS,
        cost_estimate=cost(
            2 * columns * tokens * features, 2 * features * (columns + tokens) + 4 * columns * tokens
        ),
    )(starts, ids, early, late, weight_t)


def change_of(starts_ref, logits, norm, ids, low, half):
    match = column_of(starts_ref, logits.shape, low, half) == ids
    return jnp.where(match, 1.0, 0.0) - jnp.exp(logits - norm)


def partial_product(starts, ids, logits_t, norm, weight_t, low, high, by_feature):
    columns = logits_t.shape[0]
    tokens = high - low
    features = weight_t.shape[1]
    steps = 7
    block = features // steps

    def body(starts_ref, ids_ref, logits_ref, norm_ref, w_ref, out_ref, logits, w, held, ready, w_sems, sems):
        fetch = pltpu.make_async_copy(
            logits_ref.at[:, pl.ds(low, tokens)], logits, w_sems.at[steps]
        )
        fetch.start()
        loads = [
            pltpu.make_async_copy(w_ref.at[:, pl.ds(k * block, block)], w.at[k], w_sems.at[k])
            for k in range(steps)
        ]
        for load in loads:
            load.start()
        fetch.wait()
        change = change_of(
            starts_ref, logits[...], norm_ref[:, low:high], ids_ref[:, low:high], 0, columns // 2
        )
        held[...] = (change if by_feature else change.T).astype(BF16)

        def send(k):
            span = pl.ds(k * block, block)
            into = out_ref.at[span] if by_feature else out_ref.at[:, span]
            return pltpu.make_async_copy(ready.at[k % 2], into, sems.at[k % 2])

        for k in range(steps):
            loads[k].wait()
            if by_feature:
                out = dot(w[k], held[...], ((0,), (0,)))
            else:
                out = dot(held[...], w[k], ((1,), (0,)))
            if k >= 2:
                send(k - 2).wait()
            ready[k % 2] = out.astype(BF16)
            send(k).start()
        send(steps - 2).wait()
        send(steps - 1).wait()

    if by_feature:
        out_dims, out_block, held = (features, tokens), (block, tokens), (columns, tokens)
    else:
        out_dims, out_block, held = (tokens, features), (tokens, block), (tokens, columns)
    return pl.pallas_call(
        body,
        in_specs=[SMEM, VMEM, ANY, VMEM, ANY],
        out_specs=ANY,
        out_shape=jax.ShapeDtypeStruct(out_dims, BF16),
        scratch_shapes=[
            pltpu.VMEM((columns, tokens), F32),
            pltpu.VMEM((steps, columns, block), BF16),
            pltpu.VMEM(held, BF16),
            pltpu.VMEM((2,) + out_block, BF16),
            pltpu.SemaphoreType.DMA((steps + 1,)),
            pltpu.SemaphoreType.DMA((2,)),
        ],
        compiler_params=PARAMS,
        cost_estimate=cost(
            2 * columns * tokens * features, 2 * features * (columns + tokens) + 4 * columns * tokens
        ),
    )(starts, ids, logits_t, norm, weight_t)


def head_parts(starts, ids, logits_t, norm, scale, early, late):
    columns, tokens = logits_t.shape
    half = columns // 2
    sizes = early.shape[1], late.shape[0]
    spans = (0, sizes[0]), (sizes[0], tokens)
    features = late.shape[1]
    block = features // WIDE

    def body(starts_ref, ids_ref, logits_ref, norm_ref, scale_ref, e_ref, l_ref, near_ref, far_ref,
             logits, e, l, held, near, far, sems, out):
        fetch = pltpu.make_async_copy(logits_ref, logits, sems.at[WIDE, 0])
        fetch.start()
        copies = [
            (
                pltpu.make_async_copy(e_ref.at[k], e.at[k], sems.at[k, 0]),
                pltpu.make_async_copy(
                    l_ref.at[:, pl.ds(k * block, block)], l.at[k], sems.at[k, 1]
                ),
            )
            for k in range(WIDE)
        ]
        for pair in copies:
            for copy in pair:
                copy.start()
        fetch.wait()
        for low, high in spans:
            change = change_of(
                starts_ref, logits[:, low:high], norm_ref[:, low:high], ids_ref[:, low:high], 0, half
            )
            held[:, low:high] = (change * scale_ref[:, low:high]).astype(BF16)

        def sends(k):
            span = pl.ds(k * block, block)
            return (
                pltpu.make_async_copy(far.at[k % 2], far_ref.at[:, span], out.at[k % 2, 0]),
                pltpu.make_async_copy(near.at[k % 2], near_ref.at[:, span], out.at[k % 2, 1]),
            )

        for k in range(WIDE):
            total = None
            for copy, (low, high), hidden in zip(copies[k], spans, (e, l)):
                copy.wait()
                part = dot(held[:, low:high], hidden[k], ((1,), (0,)))
                total = part if total is None else total + part
            if k >= 2:
                for send in sends(k - 2):
                    send.wait()
            near[k % 2] = total[:half]
            far[k % 2] = total[half:].astype(BF16)
            for send in sends(k):
                send.start()
        for k in (WIDE - 2, WIDE - 1):
            for send in sends(k):
                send.wait()

    return pl.pallas_call(
        body,
        in_specs=[SMEM, VMEM, ANY, VMEM, VMEM, ANY, ANY],
        out_specs=[ANY, ANY],
        out_shape=[
            jax.ShapeDtypeStruct((half, features), F32),
            jax.ShapeDtypeStruct((half, features), BF16),
        ],
        scratch_shapes=[
            pltpu.VMEM((columns, tokens), F32),
            pltpu.VMEM((WIDE, sizes[0], block), BF16),
            pltpu.VMEM((WIDE, sizes[1], block), BF16),
            pltpu.VMEM((columns, tokens), BF16),
            pltpu.VMEM((2, half, block), F32),
            pltpu.VMEM((2, half, block), BF16),
            pltpu.SemaphoreType.DMA((WIDE + 1, 2)),
            pltpu.SemaphoreType.DMA((2, 2)),
        ],
        compiler_params=PARAMS,
        cost_estimate=cost(
            2 * columns * tokens * features, 2 * features * (columns + tokens) + 4 * columns * tokens
        ),
    )(starts, ids, logits_t, norm, scale, early, late)


def pack_facts(token_ids, response_mask, teacher_logprob):
    high = lax.reduce_precision(teacher_logprob, 8, 7)
    rest = teacher_logprob - high
    middle = lax.reduce_precision(rest, 8, 7)
    rows = [
        token_ids // 16384,
        token_ids // 128 % 128,
        token_ids % 128,
        response_mask,
        high,
        middle,
        rest - middle,
        jnp.zeros_like(high),
    ]
    return jnp.stack([row.astype(F32) for row in rows]).astype(BF16)


def unpack_facts(rows):
    rows = rows.astype(F32)
    ids = (rows[:, 0] * 16384.0 + rows[:, 1] * 128.0 + rows[:, 2]).astype(jnp.int32)
    return ids, rows[:, 3], rows[:, 4] + rows[:, 5] + rows[:, 6]


def on_device(hidden, weight, token_ids, response_mask, teacher_logprob):
    own_rows, features = hidden.shape
    columns_here = weight.shape[1]
    core, z = lax.axis_index("core"), lax.axis_index("z")
    place = lax.axis_index("x") * Y + lax.axis_index("y")
    group = EARLY // GROUPS
    wide = features // WIDE
    first_half, second_half = Z * EARLY, Z * (own_rows - EARLY)
    all_rows = first_half + second_half
    tokens = all_rows * CORES

    weight_t = weight.T
    both_t = jnp.concatenate([weight_t, lax.ppermute(weight_t, "core", SWAP)])

    late = lax.all_gather(hidden[EARLY:], "z", axis=0, tiled=True)
    piece = lax.dynamic_slice(
        hidden, (place % GROUPS * group, place // GROUPS * wide), (group, wide)
    )
    facts = pack_facts(token_ids, response_mask, teacher_logprob)
    facts = jnp.pad(facts, ((0, group - facts.shape[0]), (0, 0)))
    pieces = broadcast_gather(jnp.concatenate([piece, facts], axis=1), "z", Z)
    ids, mask, teacher = unpack_facts(pieces[:, :8, wide:])
    pieces = pieces[:, :, :wide].reshape(Z * group, wide)
    early = broadcast_gather(pieces, ("x", "y"), PLANE).reshape(WIDE, first_half, wide)

    def local_order(values):
        first = values[:, :EARLY].reshape(Z, GROUPS, group).transpose(1, 0, 2)
        second = values[:, EARLY:].reshape(second_half)
        return jnp.concatenate([first.reshape(first_half), second])[None]

    def whole_order(values):
        first = values[:first_half].reshape(GROUPS, Z, group).transpose(1, 0, 2)
        second = values[first_half:].reshape(Z, own_rows - EARLY)
        return jnp.concatenate([first.reshape(Z, EARLY), second], axis=1)

    ids = local_order(ids)
    starts = jnp.stack(
        [((z * CORES + c) * PLANE + place) * columns_here for c in (core, 1 - core)]
    ).astype(jnp.int32)

    logits, stats = logits_and_stats(starts, ids, early, late, both_t)
    stats = stats[:3]
    stats = stats.reshape(3 * all_rows // LANES, LANES)

    def merged(stats, axes, count):
        parts = broadcast_gather(stats, axes, count)
        merged = merge_stats(parts.reshape(count, 3, all_rows // LANES, LANES))
        return merged.reshape(3 * all_rows // LANES, LANES)

    stats = merged(stats, "z", Z)
    stats = merged(stats, ("x", "y"), PLANE).reshape(3, all_rows)
    norm = stats[0] + jnp.log(stats[1])
    norm_row = norm[None]

    partial = partial_product(
        starts, ids, logits, norm_row, both_t, first_half, all_rows, False
    )
    late_sum = lax.psum_scatter(partial, "z", scatter_dimension=0, tiled=True)
    cut = features // PLANE
    partial = partial_product(starts, ids, logits, norm_row, both_t, 0, first_half, True)
    shared = lax.all_to_all(
        partial.reshape(PLANE, cut, first_half), ("x", "y"), 0, 0, tiled=True
    )
    early_sum = jnp.sum(shared.astype(F32), axis=0).astype(BF16).T
    early_sum = early_sum.reshape(GROUPS, Z, group, cut).transpose(1, 0, 2, 3)
    early_sum = lax.all_to_all(early_sum.reshape(Z, EARLY, cut), "z", 0, 0, tiled=True)
    early_sum = jnp.sum(early_sum.astype(F32), axis=0)
    late_sum = late_sum.reshape(own_rows - EARLY, PLANE, cut).transpose(1, 0, 2)
    late_sum = lax.all_to_all(late_sum, ("x", "y"), 0, 0, tiled=True)
    late_sum = jnp.sum(late_sum.astype(F32), axis=0)

    ratio = mask * (whole_order(stats[2]) - whole_order(norm) - teacher)
    shard_sums = jnp.sum(ratio, axis=1)
    other_sums = lax.ppermute(shard_sums, "core", SWAP)
    steps = jnp.arange(own_rows, dtype=jnp.int32)
    later = (steps[None, :] >= steps[:, None]).astype(F32)
    within = jnp.sum(ratio[:, None, :] * later[None], axis=2)
    shard = jnp.arange(Z, dtype=jnp.int32)
    after = (shard[None, :] > shard[:, None]).astype(F32)
    from_here = (shard[None, :] >= shard[:, None]).astype(F32)
    beyond = shard_sums[None, :] * after
    beyond += other_sums[None, :] * jnp.where(core == 0, from_here, after)
    weights = mask * (within + jnp.sum(beyond, axis=1)[:, None]) / float(tokens)

    own_weight = lax.dynamic_index_in_dim(weights, z, 0, False)
    hidden_grad = jnp.concatenate([early_sum, late_sum]) * own_weight[:, None]

    near, far = head_parts(starts, ids, logits, norm_row, local_order(weights), early, late)
    head_grad = near + lax.ppermute(far, "core", SWAP).astype(F32)
    return hidden_grad.astype(BF16), head_grad.astype(BF16).T


def solution(mesh):
    fine = Mesh(mesh.devices.reshape(Z, CORES, X, Y), ("z", "core", "x", "y"))
    by_token = ("z", "core")
    by_column = P(None, ("z", "core", "x", "y"))
    return jax.shard_map(
        on_device,
        mesh=fine,
        in_specs=(P(by_token, None), by_column, P(by_token), P(by_token), P(by_token)),
        out_specs=(P(by_token, ("x", "y")), by_column),
        check_vma=False,
    )
```

```python
import jax
import jax.numpy as jnp
from jax import lax
from jax.experimental import pallas as pl
from jax.experimental.pallas import tpu as pltpu
from jax.sharding import Mesh, PartitionSpec as P

F32 = jnp.float32
BF16 = jnp.bfloat16
Z, CORES, XH, XL, Y = 8, 2, 2, 2, 4
PLANE = XH * XL * Y
SWAP = [(0, 1), (1, 0)]
LANES = 128
STEPS = 7
PARAMS = pltpu.CompilerParams(vmem_limit_bytes=56 << 20)
SMEM = pl.BlockSpec(memory_space=pltpu.SMEM)
VMEM = pl.BlockSpec(memory_space=pltpu.VMEM)
ANY = pl.BlockSpec(memory_space=pl.ANY)


def broadcast_gather(part, axes, count):
    copies = jnp.broadcast_to(part[None], (count,) + part.shape)
    return lax.all_to_all(copies, axes, 0, 0, tiled=True)


def dot(left, right, contract):
    return lax.dot_general(left, right, (contract, ((), ())), preferred_element_type=F32)


def cost(flops, nbytes):
    return pl.CostEstimate(flops=flops, bytes_accessed=nbytes, transcendentals=0)


def matches_of(starts_ref, number, rows, ids):
    row = lax.broadcasted_iota(jnp.int32, (rows, ids.shape[1]), 0)
    return row + starts_ref[number] == ids


def logits_and_stats(starts, ids, hidden, weights):
    rows, features = weights[0].shape
    count = len(weights)
    columns, tokens = rows * count, hidden.shape[0]
    block = features // STEPS

    def body(starts_ref, ids_ref, h_ref, *refs):
        w_refs = refs[:count]
        logits_ref, stats_ref, w, h, held, sems, out = refs[count:]

        def loads(k):
            span = pl.ds(k * block, block)
            return [pltpu.make_async_copy(h_ref.at[:, span], h.at[k], sems.at[k, count])] + [
                pltpu.make_async_copy(
                    w_refs[i].at[:, span], w.at[k, pl.ds(i * rows, rows)], sems.at[k, i]
                )
                for i in range(count)
            ]

        copies = [loads(k) for k in range(STEPS)]
        for copy in copies[0] + copies[1]:
            copy.start()
        for k in range(STEPS):
            for copy in copies[k]:
                copy.wait()
            if k + 2 < STEPS:
                for copy in copies[k + 2]:
                    copy.start()
            part = dot(w[k], h[k], ((1,), (1,)))
            held[...] = part if k == 0 else held[...] + part
        send = pltpu.make_async_copy(held, logits_ref, out)
        send.start()
        ids = ids_ref[...]
        top = jnp.max(held[...], axis=0, keepdims=True)
        total, picked = jnp.zeros_like(top), jnp.zeros_like(top)
        for i in range(count):
            logits = held[i * rows : (i + 1) * rows]
            total += jnp.sum(jnp.exp(logits - top), axis=0, keepdims=True)
            match = matches_of(starts_ref, i, rows, ids)
            picked += jnp.sum(jnp.where(match, logits, 0.0), axis=0, keepdims=True)
        stats_ref[...] = jnp.concatenate([top, total, picked] + [jnp.zeros_like(top)] * 5)
        send.wait()

    return pl.pallas_call(
        body,
        in_specs=[SMEM, VMEM, ANY] + [ANY] * count,
        out_specs=[ANY, VMEM],
        out_shape=[
            jax.ShapeDtypeStruct((columns, tokens), F32),
            jax.ShapeDtypeStruct((8, tokens), F32),
        ],
        scratch_shapes=[
            pltpu.VMEM((STEPS, columns, block), BF16),
            pltpu.VMEM((STEPS, tokens, block), BF16),
            pltpu.VMEM((columns, tokens), F32),
            pltpu.SemaphoreType.DMA((STEPS, count + 1)),
            pltpu.SemaphoreType.DMA,
        ],
        compiler_params=PARAMS,
        cost_estimate=cost(
            2 * columns * tokens * features, 2 * features * (columns + tokens) + 4 * columns * tokens
        ),
    )(starts, ids, hidden, *weights)


def fetch_changes(starts_ref, ids_ref, norm_ref, logits_ref, logits, held, sems, numbers, rows, scale_ref):
    copies = [
        pltpu.make_async_copy(
            logits_ref.at[pl.ds(number * rows, rows)], logits.at[pl.ds(i * rows, rows)], sems.at[i]
        )
        for i, number in enumerate(numbers)
    ]

    def fill():
        ids, norm = ids_ref[...], norm_ref[...]
        for i, (copy, number) in enumerate(zip(copies, numbers)):
            copy.wait()
            span = slice(i * rows, (i + 1) * rows)
            match = matches_of(starts_ref, number, rows, ids)
            change = jnp.where(match, 1.0, 0.0) - jnp.exp(logits[span] - norm)
            if scale_ref is not None:
                change = change * scale_ref[...]
            held[span] = change.astype(BF16)

    return copies, fill


def partial_product(starts, ids, logits_t, norm, weights):
    columns, tokens = logits_t.shape
    rows, features = weights[0].shape
    count = len(weights)
    block = features // STEPS

    def body(starts_ref, ids_ref, logits_ref, norm_ref, *refs):
        w_refs = refs[:count]
        out_ref, logits, w, held, ready, l_sems, w_sems, sems = refs[count:]
        first, fill = fetch_changes(
            starts_ref, ids_ref, norm_ref, logits_ref, logits, held, l_sems, range(count), rows, None
        )
        loads = [
            [
                pltpu.make_async_copy(
                    w_refs[i].at[:, pl.ds(k * block, block)],
                    w.at[k, pl.ds(i * rows, rows)],
                    w_sems.at[k, i],
                )
                for i in range(count)
            ]
            for k in range(STEPS)
        ]
        for copy in first:
            copy.start()
        for load in loads:
            for copy in load:
                copy.start()
        fill()

        def send(k):
            return pltpu.make_async_copy(
                ready.at[k % 2], out_ref.at[:, pl.ds(k * block, block)], sems.at[k % 2]
            )

        for k in range(STEPS):
            for copy in loads[k]:
                copy.wait()
            out = dot(held[...], w[k], ((0,), (0,)))
            if k >= 2:
                send(k - 2).wait()
            ready[k % 2] = out.astype(BF16)
            send(k).start()
        send(STEPS - 2).wait()
        send(STEPS - 1).wait()

    return pl.pallas_call(
        body,
        in_specs=[SMEM, VMEM, ANY, VMEM] + [ANY] * count,
        out_specs=ANY,
        out_shape=jax.ShapeDtypeStruct((tokens, features), BF16),
        scratch_shapes=[
            pltpu.VMEM((columns, tokens), F32),
            pltpu.VMEM((STEPS, columns, block), BF16),
            pltpu.VMEM((columns, tokens), BF16),
            pltpu.VMEM((2, tokens, block), BF16),
            pltpu.SemaphoreType.DMA((count,)),
            pltpu.SemaphoreType.DMA((STEPS, count)),
            pltpu.SemaphoreType.DMA((2,)),
        ],
        compiler_params=PARAMS,
        cost_estimate=cost(
            2 * columns * tokens * features, 2 * features * (columns + tokens) + 4 * columns * tokens
        ),
    )(starts, ids, logits_t, norm, *weights)


def head_parts(starts, ids, logits_t, norm, scale, hidden, numbers, rows):
    tokens, features = hidden.shape
    block = features // STEPS
    columns = 2 * rows

    def body(starts_ref, ids_ref, logits_ref, norm_ref, scale_ref, h_ref, keep_ref, give_ref,
             logits, h, held, keep, give, l_sems, h_sems, sems):
        first, fill = fetch_changes(
            starts_ref, ids_ref, norm_ref, logits_ref, logits, held, l_sems, numbers, rows, scale_ref
        )
        loads = [
            pltpu.make_async_copy(h_ref.at[:, pl.ds(k * block, block)], h.at[k], h_sems.at[k])
            for k in range(STEPS)
        ]
        for copy in first + loads:
            copy.start()
        fill()

        def sends(k):
            span = pl.ds(k * block, block)
            return (
                pltpu.make_async_copy(keep.at[k % 2], keep_ref.at[:, span], sems.at[k % 2, 0]),
                pltpu.make_async_copy(give.at[k % 2], give_ref.at[:, span], sems.at[k % 2, 1]),
            )

        for k in range(STEPS):
            loads[k].wait()
            out = dot(held[...], h[k], ((1,), (0,)))
            if k >= 2:
                for send in sends(k - 2):
                    send.wait()
            keep[k % 2] = out[:rows]
            give[k % 2] = out[rows:].astype(BF16)
            for send in sends(k):
                send.start()
        for k in (STEPS - 2, STEPS - 1):
            for send in sends(k):
                send.wait()

    return pl.pallas_call(
        body,
        in_specs=[SMEM, VMEM, ANY, VMEM, VMEM, ANY],
        out_specs=[ANY, ANY],
        out_shape=[
            jax.ShapeDtypeStruct((rows, features), F32),
            jax.ShapeDtypeStruct((rows, features), BF16),
        ],
        scratch_shapes=[
            pltpu.VMEM((columns, tokens), F32),
            pltpu.VMEM((STEPS, tokens, block), BF16),
            pltpu.VMEM((columns, tokens), BF16),
            pltpu.VMEM((2, rows, block), F32),
            pltpu.VMEM((2, rows, block), BF16),
            pltpu.SemaphoreType.DMA((2,)),
            pltpu.SemaphoreType.DMA((STEPS,)),
            pltpu.SemaphoreType.DMA((2, 2)),
        ],
        compiler_params=PARAMS,
        cost_estimate=cost(
            2 * columns * tokens * features, 2 * features * (columns + tokens) + 4 * columns * tokens
        ),
    )(starts, ids, logits_t, norm, scale, hidden)


def pick_one(values, *places):
    for place in places:
        values = lax.dynamic_index_in_dim(values, place, 0, False)
    return values


def on_device(hidden, weight, token_ids, response_mask, teacher_logprob):
    own_rows, features = hidden.shape
    columns_here = weight.shape[1]
    core, z = lax.axis_index("core"), lax.axis_index("z")
    xh, side, y = lax.axis_index("xh"), lax.axis_index("xl"), lax.axis_index("y")
    rows = own_rows // 2
    here = Z * rows
    lines = here // LANES
    tokens = own_rows * Z * CORES

    own = weight.T
    across = lax.ppermute(own, "xl", SWAP)
    gathered = lax.all_gather(
        lax.dynamic_slice_in_dim(hidden, side * rows, rows, 0), "z", axis=0, tiled=True
    )
    weights = [own, lax.ppermute(own, "core", SWAP), across, lax.ppermute(across, "core", SWAP)]
    starts = jnp.stack(
        [
            (((z * CORES + c) * XH + xh) * XL + s) * Y * columns_here + y * columns_here
            for s in (side, 1 - side)
            for c in (core, 1 - core)
        ]
    ).astype(jnp.int32)

    facts = jnp.stack([token_ids.astype(F32), response_mask.astype(F32), teacher_logprob])
    facts = broadcast_gather(facts, ("z", "core"), Z * CORES)
    facts = facts.reshape(Z, CORES, 3, XL, rows).transpose(2, 1, 3, 0, 4)
    ids = pick_one(facts[0], core, side).astype(jnp.int32).reshape(1, here)

    logits, stats = logits_and_stats(starts, ids, gathered, weights)
    stats = broadcast_gather(stats[:3].reshape(3 * lines, LANES), "z", Z)
    stats = stats.reshape(Z, 3, lines, LANES)
    top = jnp.max(stats[:, 0], axis=0)
    total = jnp.sum(stats[:, 1] * jnp.exp(stats[:, 0] - top[None]), axis=0)
    stats = jnp.concatenate([top, total, jnp.sum(stats[:, 2], axis=0)])
    stats = broadcast_gather(stats, ("core", "xh", "xl", "y"), CORES * PLANE)
    stats = stats.reshape(CORES, XH, XL, Y, 3, lines, LANES)
    top = jnp.max(stats[:, :, :, :, 0], axis=(1, 3))
    shrink = jnp.exp(stats[:, :, :, :, 0] - top[:, None, :, None])
    total = jnp.sum(stats[:, :, :, :, 1] * shrink, axis=(1, 3))
    picked = jnp.sum(stats[:, :, :, :, 2], axis=(1, 3))
    norms = top + jnp.log(total)
    norm = pick_one(norms, core, side).reshape(1, here)

    partial = partial_product(starts, ids, logits, norm, weights)
    summed = lax.psum_scatter(partial, "z", scatter_dimension=0, tiled=True)
    cut = features // PLANE
    summed = summed.reshape(rows, PLANE, cut).transpose(1, 0, 2)
    summed = lax.all_to_all(summed, ("xh", "xl", "y"), 0, 0, tiled=True)
    summed = summed.reshape(XH, XL, Y, rows, cut).astype(F32)
    summed = jnp.sum(summed, axis=(0, 2)).reshape(own_rows, cut)

    by_shard = (CORES, XL, Z, rows)
    ratio = facts[1] * (picked.reshape(by_shard) - norms.reshape(by_shard) - facts[2])
    steps = jnp.arange(rows, dtype=jnp.int32)
    later = (steps[None, :] >= steps[:, None]).astype(F32)
    within = jnp.sum(ratio[..., None, :] * later, axis=-1)
    parts = jnp.sum(ratio, axis=-1).transpose(2, 0, 1).reshape(-1)
    order = jnp.arange(parts.shape[0], dtype=jnp.int32)
    after = (order[None, :] > order[:, None]).astype(F32)
    beyond = jnp.sum(parts[None, :] * after, axis=1).reshape(Z, CORES, XL).transpose(1, 2, 0)
    scales = facts[1] * (within + beyond[..., None]) / float(tokens)

    own_scale = lax.dynamic_index_in_dim(pick_one(scales, core), z, 1, False).reshape(own_rows)
    hidden_grad = summed * own_scale[:, None]

    scale = pick_one(scales, core, side).reshape(1, here)
    keep, give = head_parts(starts, ids, logits, norm, scale, gathered, (2, 3), columns_here)
    theirs = (keep + lax.ppermute(give, "core", SWAP).astype(F32)).astype(BF16)
    from_across = lax.ppermute(theirs, "xl", SWAP)
    keep, give = head_parts(starts, ids, logits, norm, scale, gathered, (0, 1), columns_here)
    head_grad = keep + lax.ppermute(give, "core", SWAP).astype(F32) + from_across.astype(F32)
    return hidden_grad.astype(BF16), head_grad.astype(BF16).T


def solution(mesh):
    names = ("z", "core", "xh", "xl", "y")
    fine = Mesh(mesh.devices.reshape(Z, CORES, XH, XL, Y), names)
    by_token, by_column = ("z", "core"), P(None, names)
    return jax.shard_map(
        on_device,
        mesh=fine,
        in_specs=(P(by_token, None), by_column, P(by_token), P(by_token), P(by_token)),
        out_specs=(P(by_token, names[2:]), by_column),
        check_vma=False,
    )
```

```python
import jax
import jax.numpy as jnp
from jax import lax
from jax.experimental import pallas as pl
from jax.experimental.pallas import tpu as pltpu
from jax.sharding import Mesh, PartitionSpec as P

F32 = jnp.float32
BF16 = jnp.bfloat16
Z, CORES, XH, XL, Y = 8, 2, 2, 2, 4
PLANE = XH * XL * Y
SWAP = [(0, 1), (1, 0)]
LANES = 128
STEPS = 7
PARAMS = pltpu.CompilerParams(vmem_limit_bytes=56 << 20)
SMEM = pl.BlockSpec(memory_space=pltpu.SMEM)
VMEM = pl.BlockSpec(memory_space=pltpu.VMEM)
ANY = pl.BlockSpec(memory_space=pl.ANY)


def broadcast_gather(part, axes, count):
    copies = jnp.broadcast_to(part[None], (count,) + part.shape)
    return lax.all_to_all(copies, axes, 0, 0, tiled=True)


def dot(left, right, contract):
    return lax.dot_general(left, right, (contract, ((), ())), preferred_element_type=F32)


def cost(flops, nbytes):
    return pl.CostEstimate(flops=flops, bytes_accessed=nbytes, transcendentals=0)


def matches_of(starts_ref, low, rows, columns_here, ids):
    number = low // columns_here
    row = lax.broadcasted_iota(jnp.int32, (rows, ids.shape[1]), 0) + (low - number * columns_here)
    return row + starts_ref[number] == ids


def logits_and_stats(starts, hidden, weights, columns_here):
    features = weights[0].shape[1]
    count = len(weights)
    sizes = [piece.shape[0] for piece in weights]
    offsets = [sum(sizes[:i]) for i in range(count)]
    columns, tokens = sum(sizes), hidden.shape[0]
    block = features // STEPS
    blocks = columns // columns_here

    def body(starts_ref, h_ref, *refs):
        w_refs = refs[:count]
        exps_ref, stats_ref, facts_ref, w, h, f, held, exps, sems, out = refs[count:]

        def loads(k):
            span = pl.ds(k * block, block)
            return [pltpu.make_async_copy(h_ref.at[:, span], h.at[k], sems.at[k, count])] + [
                pltpu.make_async_copy(
                    w_refs[i].at[:, span], w.at[k, pl.ds(offsets[i], sizes[i])], sems.at[k, i]
                )
                for i in range(count)
            ]

        copies = [loads(k) for k in range(STEPS)]
        facts_copy = pltpu.make_async_copy(
            h_ref.at[:, pl.ds(features, LANES)], f, sems.at[STEPS, 0]
        )
        for copy in copies[0] + copies[1] + [facts_copy]:
            copy.start()
        for k in range(STEPS):
            for copy in copies[k]:
                copy.wait()
            if k + 2 < STEPS:
                for copy in copies[k + 2]:
                    copy.start()
            part = dot(w[k], h[k], ((1,), (1,)))
            held[...] = part if k == 0 else held[...] + part
        facts_copy.wait()
        facts = f[...].astype(F32).T
        token_id = facts[0:1] * 16384.0 + facts[1:2] * 128.0 + facts[2:3]
        teacher = facts[4:5] + facts[5:6] + facts[6:7]
        ids = token_id.astype(jnp.int32)
        top = jnp.max(held[...], axis=0, keepdims=True)
        total, picked = jnp.zeros_like(top), jnp.zeros_like(top)
        sends = []
        for i in range(blocks):
            low = i * columns_here
            logits = held[low : low + columns_here]
            grown = jnp.exp(logits - top)
            total += jnp.sum(grown, axis=0, keepdims=True)
            exps[low : low + columns_here] = grown.astype(BF16)
            span = pl.ds(low, columns_here)
            sends.append(pltpu.make_async_copy(exps.at[span], exps_ref.at[span], out.at[i]))
            sends[-1].start()
            match = matches_of(starts_ref, low, columns_here, columns_here, ids)
            picked += jnp.sum(jnp.where(match, logits, 0.0), axis=0, keepdims=True)
        zero = jnp.zeros_like(top)
        stats_ref[...] = jnp.concatenate([top, total, picked, facts[3:4], teacher] + [zero] * 3)
        facts_ref[...] = jnp.concatenate([token_id, facts[3:4], teacher] + [zero] * 5)
        for send in sends:
            send.wait()

    return pl.pallas_call(
        body,
        in_specs=[SMEM, ANY] + [ANY] * count,
        out_specs=[ANY, VMEM, VMEM],
        out_shape=[
            jax.ShapeDtypeStruct((columns, tokens), BF16),
            jax.ShapeDtypeStruct((8, tokens), F32),
            jax.ShapeDtypeStruct((8, tokens), F32),
        ],
        scratch_shapes=[
            pltpu.VMEM((STEPS, columns, block), BF16),
            pltpu.VMEM((STEPS, tokens, block), BF16),
            pltpu.VMEM((tokens, LANES), BF16),
            pltpu.VMEM((columns, tokens), F32),
            pltpu.VMEM((columns, tokens), BF16),
            pltpu.SemaphoreType.DMA((STEPS + 1, count + 1)),
            pltpu.SemaphoreType.DMA((blocks,)),
        ],
        compiler_params=PARAMS,
        cost_estimate=cost(
            2 * columns * tokens * features, 2 * features * (columns + tokens) + 2 * columns * tokens
        ),
    )(starts, hidden, *weights)


def fill_changes(starts_ref, facts_ref, stats_ref, norm_ref, copies, exps, held, spans, columns_here, scale_ref):
    ids = facts_ref[0:1].astype(jnp.int32)
    shrink = jnp.exp(stats_ref[0:1] - norm_ref[...])
    at = 0
    for copy, (low, rows) in zip(copies, spans):
        copy.wait()
        match = matches_of(starts_ref, low, rows, columns_here, ids)
        change = jnp.where(match, 1.0, 0.0) - exps[at : at + rows].astype(F32) * shrink
        if scale_ref is not None:
            change = change * scale_ref[...]
        held[at : at + rows] = change.astype(BF16)
        at += rows


def partial_product(starts, facts, exps_t, stats, norm, weights, columns_here):
    columns, tokens = exps_t.shape
    features = weights[0].shape[1]
    count = len(weights)
    sizes = [piece.shape[0] for piece in weights]
    offsets = [sum(sizes[:i]) for i in range(count)]
    spans = [(low, columns_here) for low in range(0, columns, columns_here)]
    block = features // STEPS

    def body(starts_ref, facts_ref, exps_ref, stats_ref, norm_ref, *refs):
        w_refs = refs[:count]
        out_ref, exps, w, held, ready, e_sems, w_sems, sems = refs[count:]
        first = [
            pltpu.make_async_copy(
                exps_ref.at[pl.ds(low, rows)], exps.at[pl.ds(low, rows)], e_sems.at[i]
            )
            for i, (low, rows) in enumerate(spans)
        ]
        loads = [
            [
                pltpu.make_async_copy(
                    w_refs[i].at[:, pl.ds(k * block, block)],
                    w.at[k, pl.ds(offsets[i], sizes[i])],
                    w_sems.at[k, i],
                )
                for i in range(count)
            ]
            for k in range(STEPS)
        ]
        for copy in first + loads[0] + loads[1]:
            copy.start()
        fill_changes(
            starts_ref, facts_ref, stats_ref, norm_ref, first, exps, held, spans, columns_here, None
        )

        def send(k):
            return pltpu.make_async_copy(
                ready.at[k % 2], out_ref.at[:, pl.ds(k * block, block)], sems.at[k % 2]
            )

        for k in range(STEPS):
            for copy in loads[k]:
                copy.wait()
            if k + 2 < STEPS:
                for copy in loads[k + 2]:
                    copy.start()
            out = dot(held[...], w[k], ((0,), (0,)))
            if k >= 2:
                send(k - 2).wait()
            ready[k % 2] = out.astype(BF16)
            send(k).start()
        send(STEPS - 2).wait()
        send(STEPS - 1).wait()

    return pl.pallas_call(
        body,
        in_specs=[SMEM, VMEM, ANY, VMEM, VMEM] + [ANY] * count,
        out_specs=ANY,
        out_shape=jax.ShapeDtypeStruct((tokens, features), BF16),
        scratch_shapes=[
            pltpu.VMEM((columns, tokens), BF16),
            pltpu.VMEM((STEPS, columns, block), BF16),
            pltpu.VMEM((columns, tokens), BF16),
            pltpu.VMEM((2, tokens, block), BF16),
            pltpu.SemaphoreType.DMA((len(spans),)),
            pltpu.SemaphoreType.DMA((STEPS, count)),
            pltpu.SemaphoreType.DMA((2,)),
        ],
        compiler_params=PARAMS,
        cost_estimate=cost(
            2 * columns * tokens * features, 2 * features * (columns + tokens) + 2 * columns * tokens
        ),
    )(starts, facts, exps_t, stats, norm, *weights)


def head_parts(starts, facts, exps_t, stats, norm, scale, hidden, after, lows, rows, columns_here, features):
    tokens = hidden.shape[0]
    block = features // STEPS
    spans = [(low, rows) for low in lows]

    def body(starts_ref, facts_ref, exps_ref, stats_ref, norm_ref, scale_ref, h_ref, _, keep_ref, give_ref,
             exps, h, held, keep, give, e_sems, h_sems, sems):
        first = [
            pltpu.make_async_copy(
                exps_ref.at[pl.ds(low, rows)], exps.at[pl.ds(i * rows, rows)], e_sems.at[i]
            )
            for i, low in enumerate(lows)
        ]
        loads = [
            pltpu.make_async_copy(h_ref.at[:, pl.ds(k * block, block)], h.at[k], h_sems.at[k])
            for k in range(STEPS)
        ]
        for copy in first + loads:
            copy.start()
        fill_changes(
            starts_ref, facts_ref, stats_ref, norm_ref, first, exps, held, spans, columns_here, scale_ref
        )

        def sends(k):
            span = pl.ds(k * block, block)
            return (
                pltpu.make_async_copy(keep.at[k % 2], keep_ref.at[:, span], sems.at[k % 2, 0]),
                pltpu.make_async_copy(give.at[k % 2], give_ref.at[:, span], sems.at[k % 2, 1]),
            )

        for k in range(STEPS):
            loads[k].wait()
            out = dot(held[...], h[k], ((1,), (0,)))
            if k >= 2:
                for send in sends(k - 2):
                    send.wait()
            keep[k % 2] = out[:rows]
            give[k % 2] = out[rows:].astype(BF16)
            for send in sends(k):
                send.start()
        for k in (STEPS - 2, STEPS - 1):
            for send in sends(k):
                send.wait()

    return pl.pallas_call(
        body,
        in_specs=[SMEM, VMEM, ANY, VMEM, VMEM, VMEM, ANY, ANY],
        out_specs=[ANY, ANY],
        out_shape=[
            jax.ShapeDtypeStruct((rows, features), F32),
            jax.ShapeDtypeStruct((rows, features), BF16),
        ],
        scratch_shapes=[
            pltpu.VMEM((2 * rows, tokens), BF16),
            pltpu.VMEM((STEPS, tokens, block), BF16),
            pltpu.VMEM((2 * rows, tokens), BF16),
            pltpu.VMEM((2, rows, block), F32),
            pltpu.VMEM((2, rows, block), BF16),
            pltpu.SemaphoreType.DMA((2,)),
            pltpu.SemaphoreType.DMA((STEPS,)),
            pltpu.SemaphoreType.DMA((2, 2)),
        ],
        compiler_params=PARAMS,
        cost_estimate=cost(
            4 * rows * tokens * features, 2 * features * (5 * rows + tokens) + 4 * rows * tokens
        ),
    )(starts, facts, exps_t, stats, norm, scale, hidden, after)


def pack_facts(token_ids, response_mask, teacher_logprob):
    high = lax.reduce_precision(teacher_logprob, 8, 7)
    rest = teacher_logprob - high
    middle = lax.reduce_precision(rest, 8, 7)
    fields = [
        token_ids // 16384,
        token_ids // 128 % 128,
        token_ids % 128,
        response_mask,
        high,
        middle,
        rest - middle,
    ]
    fields = jnp.stack([field.astype(F32) for field in fields], axis=1).astype(BF16)
    return jnp.pad(fields, ((0, 0), (0, LANES - fields.shape[1])))


def pick_one(values, *places):
    for place in places:
        values = lax.dynamic_index_in_dim(values, place, 0, False)
    return values


def on_device(hidden, weight, token_ids, response_mask, teacher_logprob):
    own_rows, features = hidden.shape
    columns_here = weight.shape[1]
    core, z = lax.axis_index("core"), lax.axis_index("z")
    xh, side, y = lax.axis_index("xh"), lax.axis_index("xl"), lax.axis_index("y")
    rows = own_rows // 2
    here = Z * rows
    lines = here // LANES
    tokens = own_rows * Z * CORES

    own = weight.T
    cut_rows = columns_here // 2
    own_other = lax.ppermute(own, "core", SWAP)
    across = [lax.ppermute(part, "xl", SWAP) for part in (own[:cut_rows], own[cut_rows:])]
    facts = pack_facts(token_ids, response_mask, teacher_logprob)
    gathered = lax.all_gather(
        lax.dynamic_slice_in_dim(jnp.concatenate([hidden, facts], axis=1), side * rows, rows, 0),
        "z",
        axis=0,
        tiled=True,
    )
    weights = [own, own_other] + across + [lax.ppermute(part, "core", SWAP) for part in across]
    starts = jnp.stack(
        [
            (((z * CORES + c) * XH + xh) * XL + s) * Y * columns_here + y * columns_here
            for s in (side, 1 - side)
            for c in (core, 1 - core)
        ]
    ).astype(jnp.int32)

    exps, stats, facts = logits_and_stats(starts, gathered, weights, columns_here)
    shared = broadcast_gather(stats[:3].reshape(3 * lines, LANES), "z", Z)
    shared = shared.reshape(Z, 3, lines, LANES)
    top = jnp.max(shared[:, 0], axis=0)
    total = jnp.sum(shared[:, 1] * jnp.exp(shared[:, 0] - top[None]), axis=0)
    known = stats[3:5].reshape(2 * lines, LANES)
    shared = jnp.concatenate([top, total, jnp.sum(shared[:, 2], axis=0), known])
    shared = broadcast_gather(shared, ("xh", "xl", "y"), PLANE)
    shared = shared.reshape(XH, XL, Y, 5, lines, LANES)
    top = jnp.max(shared[:, :, :, 0], axis=(0, 2))
    shrink = jnp.exp(shared[:, :, :, 0] - top[None, :, None])
    total = jnp.sum(shared[:, :, :, 1] * shrink, axis=(0, 2))
    picked = jnp.sum(shared[:, :, :, 2], axis=(0, 2))
    norms = top + jnp.log(total)
    norm = pick_one(norms, side).reshape(1, here)

    partial = partial_product(starts, facts, exps, stats, norm, weights, columns_here)
    summed = lax.psum_scatter(partial, "z", scatter_dimension=0, tiled=True)
    cut = features // PLANE
    summed = summed.reshape(rows, PLANE, cut).transpose(1, 0, 2)
    summed = lax.all_to_all(summed, ("xh", "xl", "y"), 0, 0, tiled=True)
    summed = summed.reshape(XH, XL, Y, rows, cut).astype(F32)
    summed = jnp.sum(summed, axis=(0, 2)).reshape(own_rows, cut)

    mask, teacher = shared[0, :, 0, 3], shared[0, :, 0, 4]
    mask, ratio = (
        part.reshape(XL, Z, rows) for part in (mask, mask * (picked - norms - teacher))
    )
    steps = jnp.arange(rows, dtype=jnp.int32)
    later = (steps[None, :] >= steps[:, None]).astype(F32)
    within = jnp.sum(ratio[..., None, :] * later, axis=-1)
    parts = jnp.sum(ratio, axis=-1).reshape(XL * Z)
    other_parts = lax.ppermute(parts, "core", SWAP)
    number = jnp.arange(XL * Z, dtype=jnp.int32)
    order = number % Z * (CORES * XL) + number // Z
    after = order[None, :] + core * XL
    far_after = order[None, :] + (1 - core) * XL
    here_order = order[:, None] + core * XL
    beyond = parts[None, :] * (after > here_order) + other_parts[None, :] * (far_after > here_order)
    beyond = jnp.sum(beyond, axis=1).reshape(XL, Z, 1)
    scales = mask * (within + beyond) / float(tokens)

    own_scale = lax.dynamic_index_in_dim(scales, z, 1, False).reshape(own_rows)
    hidden_grad = summed * own_scale[:, None]

    scale = pick_one(scales, side).reshape(1, here)

    def parts_of(low, count, after):
        lows = (low, low + columns_here)
        keep, give = head_parts(
            starts, facts, exps, stats, norm, scale, gathered, after, lows, count, columns_here, features
        )
        return (keep + lax.ppermute(give, "core", SWAP).astype(F32)).astype(BF16)

    from_across, after = [], partial
    for low in (0, cut_rows):
        after = parts_of(2 * columns_here + low, cut_rows, after)
        from_across.append(lax.ppermute(after, "xl", SWAP))
    head_grad = parts_of(0, columns_here, after).astype(F32)
    head_grad += jnp.concatenate(from_across).astype(F32)
    return hidden_grad.astype(BF16), head_grad.astype(BF16).T


def solution(mesh):
    names = ("z", "core", "xh", "xl", "y")
    fine = Mesh(mesh.devices.reshape(Z, CORES, XH, XL, Y), names)
    by_token, by_column = ("z", "core"), P(None, names)
    return jax.shard_map(
        on_device,
        mesh=fine,
        in_specs=(P(by_token, None), by_column, P(by_token), P(by_token), P(by_token)),
        out_specs=(P(by_token, names[2:]), by_column),
        check_vma=False,
    )
```

```python
import jax
import jax.numpy as jnp
from jax import lax
from jax.experimental import pallas as pl
from jax.experimental.pallas import tpu as pltpu
from jax.sharding import Mesh, PartitionSpec as P

F32 = jnp.float32
BF16 = jnp.bfloat16
Z, CORES, XH, XL, Y = 8, 2, 2, 2, 4
PLANE = XH * XL * Y
SWAP = [(0, 1), (1, 0)]
LANES = 128
STEPS = 7
PARAMS = pltpu.CompilerParams(vmem_limit_bytes=56 << 20)
SMEM = pl.BlockSpec(memory_space=pltpu.SMEM)
VMEM = pl.BlockSpec(memory_space=pltpu.VMEM)
ANY = pl.BlockSpec(memory_space=pl.ANY)


def broadcast_gather(part, axes, count):
    copies = jnp.broadcast_to(part[None], (count,) + part.shape)
    return lax.all_to_all(copies, axes, 0, 0, tiled=True)


def dot(left, right, contract):
    return lax.dot_general(left, right, (contract, ((), ())), preferred_element_type=F32)


def cost(flops, nbytes):
    return pl.CostEstimate(flops=flops, bytes_accessed=nbytes, transcendentals=0)


def matches_of(starts_ref, low, rows, columns_here, ids):
    number = low // columns_here
    row = lax.broadcasted_iota(jnp.int32, (rows, ids.shape[1]), 0) + (low - number * columns_here)
    return row + starts_ref[number] == ids


def logits_and_stats(starts, hidden, weights, columns_here):
    features = weights[0].shape[1]
    count = len(weights)
    sizes = [piece.shape[0] for piece in weights]
    offsets = [sum(sizes[:i]) for i in range(count)]
    columns, tokens = sum(sizes), hidden.shape[0]
    block = features // STEPS
    blocks = columns // columns_here

    def body(starts_ref, h_ref, *refs):
        w_refs = refs[:count]
        *exps_refs, stats_ref, w, h, f, held, exps, sems, out = refs[count:]

        def loads(k):
            span = pl.ds(k * block, block)
            return [pltpu.make_async_copy(h_ref.at[:, span], h.at[k], sems.at[k, count])] + [
                pltpu.make_async_copy(
                    w_refs[i].at[:, span], w.at[k, pl.ds(offsets[i], sizes[i])], sems.at[k, i]
                )
                for i in range(count)
            ]

        copies = [loads(k) for k in range(STEPS)]
        facts_copy = pltpu.make_async_copy(
            h_ref.at[:, pl.ds(features, LANES)], f, sems.at[STEPS, 0]
        )
        for copy in copies[0] + copies[1] + [facts_copy]:
            copy.start()
        for k in range(STEPS):
            for copy in copies[k]:
                copy.wait()
            if k + 2 < STEPS:
                for copy in copies[k + 2]:
                    copy.start()
            part = dot(w[k], h[k], ((1,), (1,)))
            held[...] = part if k == 0 else held[...] + part
        facts_copy.wait()
        facts = f[...].astype(F32).T
        token_id = facts[0:1] * 16384.0 + facts[1:2] * 128.0 + facts[2:3]
        teacher = facts[4:5] + facts[5:6] + facts[6:7]
        ids = token_id.astype(jnp.int32)
        top = jnp.max(held[...], axis=0, keepdims=True)
        total, picked = jnp.zeros_like(top), jnp.zeros_like(top)
        sends = []
        for i in range(blocks):
            low = i * columns_here
            logits = held[low : low + columns_here]
            grown = jnp.exp(logits - top)
            total += jnp.sum(grown, axis=0, keepdims=True)
            exps[low : low + columns_here] = grown.astype(BF16)
            into = exps_refs[2 * i // blocks].at[pl.ds(low % (columns // 2), columns_here)]
            sends.append(
                pltpu.make_async_copy(exps.at[pl.ds(low, columns_here)], into, out.at[i])
            )
            sends[-1].start()
            match = matches_of(starts_ref, low, columns_here, columns_here, ids)
            picked += jnp.sum(jnp.where(match, logits, 0.0), axis=0, keepdims=True)
        zero = jnp.zeros_like(top)
        stats_ref[...] = jnp.concatenate(
            [top, total, picked, facts[3:4], teacher, token_id, zero, zero]
        )
        for send in sends:
            send.wait()

    return pl.pallas_call(
        body,
        in_specs=[SMEM, ANY] + [ANY] * count,
        out_specs=[ANY, ANY, VMEM],
        out_shape=[jax.ShapeDtypeStruct((columns // 2, tokens), BF16)] * 2
        + [jax.ShapeDtypeStruct((8, tokens), F32)],
        scratch_shapes=[
            pltpu.VMEM((STEPS, columns, block), BF16),
            pltpu.VMEM((STEPS, tokens, block), BF16),
            pltpu.VMEM((tokens, LANES), BF16),
            pltpu.VMEM((columns, tokens), F32),
            pltpu.VMEM((columns, tokens), BF16),
            pltpu.SemaphoreType.DMA((STEPS + 1, count + 1)),
            pltpu.SemaphoreType.DMA((blocks,)),
        ],
        compiler_params=PARAMS,
        cost_estimate=cost(
            2 * columns * tokens * features, 2 * features * (columns + tokens) + 2 * columns * tokens
        ),
    )(starts, hidden, *weights)


def change_of(starts_ref, rows_ref, exps, low, columns_here, scaled):
    ids = rows_ref[0:1].astype(jnp.int32)
    match = matches_of(starts_ref, low, exps.shape[0], columns_here, ids)
    change = jnp.where(match, 1.0, 0.0) - exps.astype(F32) * rows_ref[1:2]
    return (change * rows_ref[2:3] if scaled else change).astype(BF16)


def partial_product(starts, token_rows, exps_t, weights, columns_here):
    half, tokens = exps_t[0].shape
    columns = 2 * half
    features = weights[0].shape[1]
    count = len(weights)
    sizes = [piece.shape[0] for piece in weights]
    offsets = [sum(sizes[:i]) for i in range(count)]
    block = features // STEPS

    def body(starts_ref, rows_ref, first_ref, last_ref, *refs):
        w_refs = refs[:count]
        out_ref, exps, w, held, ready, e_sems, w_sems, sems = refs[count:]
        first = [
            pltpu.make_async_copy(ref, exps.at[pl.ds(i * half, half)], e_sems.at[i])
            for i, ref in enumerate((first_ref, last_ref))
        ]
        loads = [
            [
                pltpu.make_async_copy(
                    w_refs[i].at[:, pl.ds(k * block, block)],
                    w.at[k, pl.ds(offsets[i], sizes[i])],
                    w_sems.at[k, i],
                )
                for i in range(count)
            ]
            for k in range(STEPS)
        ]
        for copy in first + loads[0] + loads[1]:
            copy.start()
        for low in range(0, columns, columns_here):
            if low % half == 0:
                first[low // half].wait()
            held[low : low + columns_here] = change_of(
                starts_ref, rows_ref, exps[low : low + columns_here], low, columns_here, False
            )

        def send(k):
            return pltpu.make_async_copy(
                ready.at[k % 2], out_ref.at[:, pl.ds(k * block, block)], sems.at[k % 2]
            )

        for k in range(STEPS):
            for copy in loads[k]:
                copy.wait()
            if k + 2 < STEPS:
                for copy in loads[k + 2]:
                    copy.start()
            out = dot(held[...], w[k], ((0,), (0,)))
            if k >= 2:
                send(k - 2).wait()
            ready[k % 2] = out.astype(BF16)
            send(k).start()
        send(STEPS - 2).wait()
        send(STEPS - 1).wait()

    return pl.pallas_call(
        body,
        in_specs=[SMEM, VMEM, ANY, ANY] + [ANY] * count,
        out_specs=ANY,
        out_shape=jax.ShapeDtypeStruct((tokens, features), BF16),
        scratch_shapes=[
            pltpu.VMEM((columns, tokens), BF16),
            pltpu.VMEM((STEPS, columns, block), BF16),
            pltpu.VMEM((columns, tokens), BF16),
            pltpu.VMEM((2, tokens, block), BF16),
            pltpu.SemaphoreType.DMA((2,)),
            pltpu.SemaphoreType.DMA((STEPS, count)),
            pltpu.SemaphoreType.DMA((2,)),
        ],
        compiler_params=PARAMS,
        cost_estimate=cost(
            2 * columns * tokens * features, 2 * features * (columns + tokens) + 2 * columns * tokens
        ),
    )(starts, token_rows, *exps_t, *weights)


def head_block(starts, sides, low, columns_here, features, after):
    tokens = sides[0][2].shape[0]
    block = features // STEPS
    count = len(sides)

    def body(starts_ref, *refs):
        rows_refs, exps_refs, h_refs = refs[0 : 3 * count : 3], refs[1 : 3 * count : 3], refs[2 : 3 * count : 3]
        out_ref, exps, h, held, ready, e_sems, h_sems, sems = refs[3 * count + 1 :]
        first = [
            pltpu.make_async_copy(ref.at[pl.ds(low, columns_here)], exps.at[i], e_sems.at[i])
            for i, ref in enumerate(exps_refs)
        ]
        loads = [
            [
                pltpu.make_async_copy(
                    ref.at[:, pl.ds(k * block, block)], h.at[k, i], h_sems.at[k, i]
                )
                for i, ref in enumerate(h_refs)
            ]
            for k in range(STEPS)
        ]
        for copy in first + loads[0] + loads[1]:
            copy.start()
        for i in range(count):
            first[i].wait()
            held[i] = change_of(starts_ref, rows_refs[i], exps[i], low, columns_here, True)

        def send(k):
            return pltpu.make_async_copy(
                ready.at[k % 2], out_ref.at[:, pl.ds(k * block, block)], sems.at[k % 2]
            )

        for k in range(STEPS):
            if k + 2 < STEPS:
                for copy in loads[k + 2]:
                    copy.start()
            out = None
            for i in range(count):
                loads[k][i].wait()
                part = dot(held[i], h[k, i], ((1,), (0,)))
                out = part if out is None else out + part
            if k >= 2:
                send(k - 2).wait()
            ready[k % 2] = out.astype(BF16)
            send(k).start()
        send(STEPS - 2).wait()
        send(STEPS - 1).wait()

    return pl.pallas_call(
        body,
        in_specs=[SMEM] + [VMEM, ANY, ANY] * count + [ANY],
        out_specs=ANY,
        out_shape=jax.ShapeDtypeStruct((columns_here, features), BF16),
        scratch_shapes=[
            pltpu.VMEM((count, columns_here, tokens), BF16),
            pltpu.VMEM((STEPS, count, tokens, block), BF16),
            pltpu.VMEM((count, columns_here, tokens), BF16),
            pltpu.VMEM((2, columns_here, block), BF16),
            pltpu.SemaphoreType.DMA((count,)),
            pltpu.SemaphoreType.DMA((STEPS, count)),
            pltpu.SemaphoreType.DMA((2,)),
        ],
        compiler_params=PARAMS,
        cost_estimate=cost(
            2 * count * columns_here * tokens * features, 2 * features * (columns_here + count * tokens)
        ),
    )(starts, *(operand for side in sides for operand in side), after)


def cut_features(values, width):
    rows, features = values.shape
    count = features // width

    def body(in_ref, out_ref):
        values = in_ref[...]
        for i in range(count):
            out_ref[i] = values[:, i * width : (i + 1) * width]

    return pl.pallas_call(
        body,
        in_specs=[VMEM],
        out_specs=VMEM,
        out_shape=jax.ShapeDtypeStruct((count, rows, width), values.dtype),
        compiler_params=PARAMS,
        cost_estimate=cost(0, 4 * rows * features),
    )(values)


def pack_facts(token_ids, response_mask, teacher_logprob):
    high = lax.reduce_precision(teacher_logprob, 8, 7)
    rest = teacher_logprob - high
    middle = lax.reduce_precision(rest, 8, 7)
    fields = [
        token_ids // 16384,
        token_ids // 128 % 128,
        token_ids % 128,
        response_mask,
        high,
        middle,
        rest - middle,
    ]
    fields = jnp.stack([field.astype(F32) for field in fields], axis=1).astype(BF16)
    return jnp.pad(fields, ((0, 0), (0, LANES - fields.shape[1])))


def pick_one(values, *places):
    for place in places:
        values = lax.dynamic_index_in_dim(values, place, 0, False)
    return values


def on_device(hidden, weight, token_ids, response_mask, teacher_logprob):
    own_rows, features = hidden.shape
    columns_here = weight.shape[1]
    core, z = lax.axis_index("core"), lax.axis_index("z")
    xh, side, y = lax.axis_index("xh"), lax.axis_index("xl"), lax.axis_index("y")
    rows = own_rows // 2
    here = Z * rows
    lines = here // LANES
    tokens = own_rows * Z * CORES

    own = weight.T
    across = lax.ppermute(own, "xl", SWAP)
    own_other = lax.ppermute(own, "core", SWAP)
    facts = pack_facts(token_ids, response_mask, teacher_logprob)
    gathered = lax.all_gather(
        lax.dynamic_slice_in_dim(jnp.concatenate([hidden, facts], axis=1), side * rows, rows, 0),
        "z",
        axis=0,
        tiled=True,
    )
    weights = [own, across, own_other, lax.ppermute(across, "core", SWAP)]
    starts = jnp.stack(
        [
            (((z * CORES + c) * XH + xh) * XL + s) * Y * columns_here + y * columns_here
            for c in (core, 1 - core)
            for s in (side, 1 - side)
        ]
    ).astype(jnp.int32)

    mine, theirs, stats = logits_and_stats(starts, gathered, weights, columns_here)
    far_gathered = lax.ppermute(gathered, "core", SWAP)
    far_exps = lax.ppermute(theirs, "core", SWAP)
    shared = broadcast_gather(stats[:5].reshape(5 * lines, LANES), "z", Z)
    shared = shared.reshape(Z, 5, lines, LANES)
    top = jnp.max(shared[:, 0], axis=0)
    total = jnp.sum(shared[:, 1] * jnp.exp(shared[:, 0] - top[None]), axis=0)
    known = shared[0, 3:].reshape(2 * lines, LANES)
    shared = jnp.concatenate([top, total, jnp.sum(shared[:, 2], axis=0), known])
    shared = broadcast_gather(shared, ("xh", "xl", "y"), PLANE)
    shared = shared.reshape(XH, XL, Y, 5, lines, LANES)
    top = jnp.max(shared[:, :, :, 0], axis=(0, 2))
    shrink = jnp.exp(shared[:, :, :, 0] - top[None, :, None])
    total = jnp.sum(shared[:, :, :, 1] * shrink, axis=(0, 2))
    picked = jnp.sum(shared[:, :, :, 2], axis=(0, 2))
    norms = top + jnp.log(total)
    factor = jnp.exp(stats[0] - pick_one(norms, side).reshape(here))
    token_rows = jnp.stack([stats[5], factor])

    partial = partial_product(starts, token_rows, (mine, theirs), weights, columns_here)
    summed = lax.psum_scatter(partial, "z", scatter_dimension=0, tiled=True)
    cut = features // PLANE
    shares = cut_features(summed, cut)
    summed = lax.all_to_all(shares, ("xh", "xl", "y"), 0, 0, tiled=True)
    summed = summed.reshape(XH, XL, Y, rows, cut).astype(F32)
    summed = jnp.sum(summed, axis=(0, 2)).reshape(own_rows, cut)

    mask, teacher = shared[0, :, 0, 3], shared[0, :, 0, 4]
    ratio = mask * (picked - norms - teacher)
    known = jnp.concatenate([part.reshape(XL, here) for part in (mask, ratio)] + [token_rows])
    known = jnp.stack([known, lax.ppermute(known, "core", SWAP)])
    mask, ratio = (
        part.reshape(CORES, XL, Z, rows) for part in (known[:, :XL], known[:, XL : 2 * XL])
    )
    steps = jnp.arange(rows, dtype=jnp.int32)
    later = (steps[None, :] >= steps[:, None]).astype(F32)
    within = jnp.sum(ratio[..., None, :] * later, axis=-1)
    parts = jnp.sum(ratio, axis=-1).reshape(-1)
    number = jnp.arange(XL * Z, dtype=jnp.int32)
    order = number % Z * (CORES * XL) + number // Z
    order = jnp.concatenate([order + core * XL, order + (1 - core) * XL])
    beyond = jnp.sum(parts[None, :] * (order[None, :] > order[:, None]), axis=1)
    scales = mask * (within + beyond.reshape(CORES, XL, Z, 1)) / float(tokens)

    own_scale = lax.dynamic_index_in_dim(scales[0], z, 1, False).reshape(own_rows)
    hidden_grad = summed * own_scale[:, None]

    scale = lax.dynamic_index_in_dim(scales, side, 1, False).reshape(CORES, 1, here)
    rows_of = jnp.concatenate([known[:, 2 * XL :], scale], axis=1)
    sides = [(rows_of[0], mine, gathered), (rows_of[1], far_exps, far_gathered)]
    given = head_block(starts, sides, columns_here, columns_here, features, partial)
    from_across = lax.ppermute(given, "xl", SWAP)
    kept = head_block(starts, sides, 0, columns_here, features, shares)
    head_grad = kept.astype(F32) + from_across.astype(F32)
    return hidden_grad.astype(BF16), head_grad.astype(BF16).T


def solution(mesh):
    names = ("z", "core", "xh", "xl", "y")
    fine = Mesh(mesh.devices.reshape(Z, CORES, XH, XL, Y), names)
    by_token, by_column = ("z", "core"), P(None, names)
    return jax.shard_map(
        on_device,
        mesh=fine,
        in_specs=(P(by_token, None), by_column, P(by_token), P(by_token), P(by_token)),
        out_specs=(P(by_token, names[2:]), by_column),
        check_vma=False,
    )
```

```python
import jax
import jax.numpy as jnp
from jax import lax
from jax.experimental import pallas as pl
from jax.experimental.pallas import tpu as pltpu
from jax.sharding import Mesh, PartitionSpec as P

F32 = jnp.float32
BF16 = jnp.bfloat16
Z, CORES, XH, XL, Y = 8, 2, 2, 2, 4
PLANE = XH * XL * Y
SWAP = [(0, 1), (1, 0)]
LANES = 128
STEPS = 7
PARAMS = pltpu.CompilerParams(vmem_limit_bytes=56 << 20)
SMEM = pl.BlockSpec(memory_space=pltpu.SMEM)
VMEM = pl.BlockSpec(memory_space=pltpu.VMEM)
ANY = pl.BlockSpec(memory_space=pl.ANY)


def broadcast_gather(part, axes, count):
    copies = jnp.broadcast_to(part[None], (count,) + part.shape)
    return lax.all_to_all(copies, axes, 0, 0, tiled=True)


def dot(left, right, contract):
    return lax.dot_general(left, right, (contract, ((), ())), preferred_element_type=F32)


def cost(flops, nbytes):
    return pl.CostEstimate(flops=flops, bytes_accessed=nbytes, transcendentals=0)


def matches_of(starts_ref, low, rows, columns_here, ids):
    number = low // columns_here
    row = lax.broadcasted_iota(jnp.int32, (rows, ids.shape[1]), 0) + (low - number * columns_here)
    return row + starts_ref[number] == ids


def logits_and_stats(starts, hidden, weights, columns_here):
    features = weights[0].shape[1]
    count = len(weights)
    sizes = [piece.shape[0] for piece in weights]
    offsets = [sum(sizes[:i]) for i in range(count)]
    columns, tokens = sum(sizes), hidden.shape[0]
    block = features // STEPS
    blocks = columns // columns_here

    def body(starts_ref, h_ref, *refs):
        w_refs = refs[:count]
        *exps_refs, stats_ref, w, h, f, held, exps, sems, out = refs[count:]

        def loads(k):
            span = pl.ds(k * block, block)
            return [pltpu.make_async_copy(h_ref.at[:, span], h.at[k], sems.at[k, count])] + [
                pltpu.make_async_copy(
                    w_refs[i].at[:, span], w.at[k, pl.ds(offsets[i], sizes[i])], sems.at[k, i]
                )
                for i in range(count)
            ]

        copies = [loads(k) for k in range(STEPS)]
        facts_copy = pltpu.make_async_copy(
            h_ref.at[:, pl.ds(features, LANES)], f, sems.at[STEPS, 0]
        )
        for copy in copies[0] + copies[1] + [facts_copy]:
            copy.start()
        for k in range(STEPS):
            for copy in copies[k]:
                copy.wait()
            if k + 2 < STEPS:
                for copy in copies[k + 2]:
                    copy.start()
            part = dot(w[k], h[k], ((1,), (1,)))
            held[...] = part if k == 0 else held[...] + part
        facts_copy.wait()
        facts = f[...].astype(F32).T
        token_id = facts[0:1] * 16384.0 + facts[1:2] * 128.0 + facts[2:3]
        teacher = facts[4:5] + facts[5:6] + facts[6:7]
        ids = token_id.astype(jnp.int32)
        top = jnp.max(held[...], axis=0, keepdims=True)
        total, picked = jnp.zeros_like(top), jnp.zeros_like(top)
        sends = []
        for i in range(blocks):
            low = i * columns_here
            logits = held[low : low + columns_here]
            grown = jnp.exp(logits - top)
            total += jnp.sum(grown, axis=0, keepdims=True)
            exps[low : low + columns_here] = grown.astype(BF16)
            into = exps_refs[2 * i // blocks].at[pl.ds(low % (columns // 2), columns_here)]
            sends.append(
                pltpu.make_async_copy(exps.at[pl.ds(low, columns_here)], into, out.at[i])
            )
            sends[-1].start()
            match = matches_of(starts_ref, low, columns_here, columns_here, ids)
            picked += jnp.sum(jnp.where(match, logits, 0.0), axis=0, keepdims=True)
        zero = jnp.zeros_like(top)
        stats_ref[...] = jnp.concatenate(
            [top, total, picked, facts[3:4], teacher, token_id, zero, zero]
        )
        for send in sends:
            send.wait()

    return pl.pallas_call(
        body,
        in_specs=[SMEM, ANY] + [ANY] * count,
        out_specs=[ANY, ANY, VMEM],
        out_shape=[jax.ShapeDtypeStruct((columns // 2, tokens), BF16)] * 2
        + [jax.ShapeDtypeStruct((8, tokens), F32)],
        scratch_shapes=[
            pltpu.VMEM((STEPS, columns, block), BF16),
            pltpu.VMEM((STEPS, tokens, block), BF16),
            pltpu.VMEM((tokens, LANES), BF16),
            pltpu.VMEM((columns, tokens), F32),
            pltpu.VMEM((columns, tokens), BF16),
            pltpu.SemaphoreType.DMA((STEPS + 1, count + 1)),
            pltpu.SemaphoreType.DMA((blocks,)),
        ],
        compiler_params=PARAMS,
        cost_estimate=cost(
            2 * columns * tokens * features, 2 * features * (columns + tokens) + 2 * columns * tokens
        ),
    )(starts, hidden, *weights)


def merge_stats(parts, own, after):
    lines = own.shape[0] // 8

    def body(parts_ref, own_ref, _, out_ref):
        tops = parts_ref[:, :lines]
        top = jnp.max(tops, axis=0)
        out_ref[:lines] = top
        out_ref[lines : 2 * lines] = jnp.sum(
            parts_ref[:, lines : 2 * lines] * jnp.exp(tops - top[None]), axis=0
        )
        out_ref[2 * lines : 3 * lines] = jnp.sum(parts_ref[:, 2 * lines :], axis=0)
        out_ref[3 * lines : 6 * lines] = own_ref[3 * lines : 6 * lines]
        out_ref[6 * lines :] = own_ref[:lines]

    return pl.pallas_call(
        body,
        in_specs=[VMEM, VMEM, ANY],
        out_specs=VMEM,
        out_shape=jax.ShapeDtypeStruct((7 * lines, LANES), F32),
        compiler_params=PARAMS,
        cost_estimate=cost(0, 4 * parts.size),
    )(parts, own, after)


def change_of(starts_ref, rows_ref, exps, low, columns_here, scaled):
    ids = rows_ref[0:1].astype(jnp.int32)
    match = matches_of(starts_ref, low, exps.shape[0], columns_here, ids)
    change = jnp.where(match, 1.0, 0.0) - exps.astype(F32) * rows_ref[1:2]
    return (change * rows_ref[2:3] if scaled else change).astype(BF16)


def partial_product(starts, token_rows, exps_t, weights, columns_here):
    half, tokens = exps_t[0].shape
    columns = 2 * half
    features = weights[0].shape[1]
    count = len(weights)
    sizes = [piece.shape[0] for piece in weights]
    offsets = [sum(sizes[:i]) for i in range(count)]
    block = features // STEPS

    def body(starts_ref, rows_ref, first_ref, last_ref, *refs):
        w_refs = refs[:count]
        out_ref, exps, w, held, ready, e_sems, w_sems, sems = refs[count:]
        first = [
            pltpu.make_async_copy(ref, exps.at[pl.ds(i * half, half)], e_sems.at[i])
            for i, ref in enumerate((first_ref, last_ref))
        ]
        loads = [
            [
                pltpu.make_async_copy(
                    w_refs[i].at[:, pl.ds(k * block, block)],
                    w.at[k, pl.ds(offsets[i], sizes[i])],
                    w_sems.at[k, i],
                )
                for i in range(count)
            ]
            for k in range(STEPS)
        ]
        for copy in first + loads[0] + loads[1]:
            copy.start()
        for low in range(0, columns, columns_here):
            if low % half == 0:
                first[low // half].wait()
            held[low : low + columns_here] = change_of(
                starts_ref, rows_ref, exps[low : low + columns_here], low, columns_here, False
            )

        def send(k):
            return pltpu.make_async_copy(
                ready.at[k % 2], out_ref.at[:, pl.ds(k * block, block)], sems.at[k % 2]
            )

        for k in range(STEPS):
            for copy in loads[k]:
                copy.wait()
            if k + 2 < STEPS:
                for copy in loads[k + 2]:
                    copy.start()
            out = dot(held[...], w[k], ((0,), (0,)))
            if k >= 2:
                send(k - 2).wait()
            ready[k % 2] = out.astype(BF16)
            send(k).start()
        send(STEPS - 2).wait()
        send(STEPS - 1).wait()

    return pl.pallas_call(
        body,
        in_specs=[SMEM, VMEM, ANY, ANY] + [ANY] * count,
        out_specs=ANY,
        out_shape=jax.ShapeDtypeStruct((tokens, features), BF16),
        scratch_shapes=[
            pltpu.VMEM((columns, tokens), BF16),
            pltpu.VMEM((STEPS, columns, block), BF16),
            pltpu.VMEM((columns, tokens), BF16),
            pltpu.VMEM((2, tokens, block), BF16),
            pltpu.SemaphoreType.DMA((2,)),
            pltpu.SemaphoreType.DMA((STEPS, count)),
            pltpu.SemaphoreType.DMA((2,)),
        ],
        compiler_params=PARAMS,
        cost_estimate=cost(
            2 * columns * tokens * features, 2 * features * (columns + tokens) + 2 * columns * tokens
        ),
    )(starts, token_rows, *exps_t, *weights)


def head_block(starts, sides, low, columns_here, features, after):
    tokens = sides[0][2].shape[0]
    block = features // STEPS
    count = len(sides)

    def body(starts_ref, *refs):
        rows_refs, exps_refs, h_refs = refs[0 : 3 * count : 3], refs[1 : 3 * count : 3], refs[2 : 3 * count : 3]
        out_ref, exps, h, held, ready, e_sems, h_sems, sems = refs[3 * count + 1 :]
        first = [
            pltpu.make_async_copy(ref.at[pl.ds(low, columns_here)], exps.at[i], e_sems.at[i])
            for i, ref in enumerate(exps_refs)
        ]
        loads = [
            [
                pltpu.make_async_copy(
                    ref.at[:, pl.ds(k * block, block)], h.at[k, i], h_sems.at[k, i]
                )
                for i, ref in enumerate(h_refs)
            ]
            for k in range(STEPS)
        ]
        for copy in first + loads[0] + loads[1]:
            copy.start()
        for i in range(count):
            first[i].wait()
            held[i] = change_of(starts_ref, rows_refs[i], exps[i], low, columns_here, True)

        def send(k):
            return pltpu.make_async_copy(
                ready.at[k % 2], out_ref.at[:, pl.ds(k * block, block)], sems.at[k % 2]
            )

        for k in range(STEPS):
            if k + 2 < STEPS:
                for copy in loads[k + 2]:
                    copy.start()
            out = None
            for i in range(count):
                loads[k][i].wait()
                part = dot(held[i], h[k, i], ((1,), (0,)))
                out = part if out is None else out + part
            if k >= 2:
                send(k - 2).wait()
            ready[k % 2] = out.astype(BF16)
            send(k).start()
        send(STEPS - 2).wait()
        send(STEPS - 1).wait()

    return pl.pallas_call(
        body,
        in_specs=[SMEM] + [VMEM, ANY, ANY] * count + [ANY],
        out_specs=ANY,
        out_shape=jax.ShapeDtypeStruct((columns_here, features), BF16),
        scratch_shapes=[
            pltpu.VMEM((count, columns_here, tokens), BF16),
            pltpu.VMEM((STEPS, count, tokens, block), BF16),
            pltpu.VMEM((count, columns_here, tokens), BF16),
            pltpu.VMEM((2, columns_here, block), BF16),
            pltpu.SemaphoreType.DMA((count,)),
            pltpu.SemaphoreType.DMA((STEPS, count)),
            pltpu.SemaphoreType.DMA((2,)),
        ],
        compiler_params=PARAMS,
        cost_estimate=cost(
            2 * count * columns_here * tokens * features, 2 * features * (columns_here + count * tokens)
        ),
    )(starts, *(operand for side in sides for operand in side), after)


def cut_features(values, width):
    rows, features = values.shape
    count = features // width

    def body(in_ref, out_ref):
        values = in_ref[...]
        for i in range(count):
            out_ref[i] = values[:, i * width : (i + 1) * width]

    return pl.pallas_call(
        body,
        in_specs=[VMEM],
        out_specs=VMEM,
        out_shape=jax.ShapeDtypeStruct((count, rows, width), values.dtype),
        compiler_params=PARAMS,
        cost_estimate=cost(0, 4 * rows * features),
    )(values)


def pack_facts(token_ids, response_mask, teacher_logprob):
    high = lax.reduce_precision(teacher_logprob, 8, 7)
    rest = teacher_logprob - high
    middle = lax.reduce_precision(rest, 8, 7)
    fields = [
        token_ids // 16384,
        token_ids // 128 % 128,
        token_ids % 128,
        response_mask,
        high,
        middle,
        rest - middle,
    ]
    fields = jnp.stack([field.astype(F32) for field in fields], axis=1).astype(BF16)
    return jnp.pad(fields, ((0, 0), (0, LANES - fields.shape[1])))


def pick_one(values, *places):
    for place in places:
        values = lax.dynamic_index_in_dim(values, place, 0, False)
    return values


def on_device(hidden, weight, token_ids, response_mask, teacher_logprob):
    own_rows, features = hidden.shape
    columns_here = weight.shape[1]
    core, z = lax.axis_index("core"), lax.axis_index("z")
    xh, side, y = lax.axis_index("xh"), lax.axis_index("xl"), lax.axis_index("y")
    rows = own_rows // 2
    here = Z * rows
    lines = here // LANES
    tokens = own_rows * Z * CORES

    own = weight.T
    across = lax.ppermute(own, "xl", SWAP)
    own_other = lax.ppermute(own, "core", SWAP)
    facts = pack_facts(token_ids, response_mask, teacher_logprob)
    gathered = lax.all_gather(
        lax.dynamic_slice_in_dim(jnp.concatenate([hidden, facts], axis=1), side * rows, rows, 0),
        "z",
        axis=0,
        tiled=True,
    )
    weights = [own, across, own_other, lax.ppermute(across, "core", SWAP)]
    starts = jnp.stack(
        [
            (((z * CORES + c) * XH + xh) * XL + s) * Y * columns_here + y * columns_here
            for c in (core, 1 - core)
            for s in (side, 1 - side)
        ]
    ).astype(jnp.int32)

    mine, theirs, stats = logits_and_stats(starts, gathered, weights, columns_here)
    far_gathered = lax.ppermute(gathered, "core", SWAP)
    far_exps = lax.ppermute(theirs, "core", SWAP)
    stats = stats.reshape(8 * lines, LANES)
    shared = broadcast_gather(stats[: 3 * lines], "z", Z)
    shared = merge_stats(shared, stats, far_gathered)
    shared = broadcast_gather(shared, ("core", "xh", "xl", "y"), CORES * PLANE)
    shared = shared.reshape(CORES, XH, XL, Y, 7, lines, LANES)
    top = jnp.max(shared[:, :, :, :, 0], axis=(1, 3))
    shrink = jnp.exp(shared[:, :, :, :, 0] - top[:, None, :, None])
    total = jnp.sum(shared[:, :, :, :, 1] * shrink, axis=(1, 3))
    picked = jnp.sum(shared[:, :, :, :, 2], axis=(1, 3))
    norms = top + jnp.log(total)
    at_place = lax.dynamic_slice(
        shared, (0, xh, side, y, 5, 0, 0), (CORES, 1, 1, 1, 2, lines, LANES)
    ).reshape(CORES, 2, here)
    own_norms = lax.dynamic_index_in_dim(norms, side, 1, False).reshape(CORES, here)
    token_rows = jnp.stack([at_place[:, 0], jnp.exp(at_place[:, 1] - own_norms)], axis=1)

    partial = partial_product(
        starts, pick_one(token_rows, core), (mine, theirs), weights, columns_here
    )
    summed = lax.psum_scatter(partial, "z", scatter_dimension=0, tiled=True)
    cut = features // PLANE
    shares = cut_features(summed, cut)
    summed = lax.all_to_all(shares, ("xh", "xl", "y"), 0, 0, tiled=True)
    summed = summed.reshape(XH, XL, Y, rows, cut).astype(F32)
    summed = jnp.sum(summed, axis=(0, 2)).reshape(own_rows, cut)

    mask, teacher = shared[:, 0, :, 0, 3], shared[:, 0, :, 0, 4]
    mask, ratio = (
        part.reshape(CORES, XL, Z, rows) for part in (mask, mask * (picked - norms - teacher))
    )
    steps = jnp.arange(rows, dtype=jnp.int32)
    later = (steps[None, :] >= steps[:, None]).astype(F32)
    within = jnp.sum(ratio[..., None, :] * later, axis=-1)
    parts = jnp.sum(ratio, axis=-1).transpose(2, 0, 1).reshape(-1)
    order = jnp.arange(parts.shape[0], dtype=jnp.int32)
    after = (order[None, :] > order[:, None]).astype(F32)
    beyond = jnp.sum(parts[None, :] * after, axis=1).reshape(Z, CORES, XL).transpose(1, 2, 0)
    scales = mask * (within + beyond[..., None]) / float(tokens)

    own_scale = lax.dynamic_index_in_dim(pick_one(scales, core), z, 1, False).reshape(own_rows)
    hidden_grad = summed * own_scale[:, None]

    scale = lax.dynamic_index_in_dim(scales, side, 1, False).reshape(CORES, 1, here)
    rows_of = jnp.concatenate([token_rows, scale], axis=1)
    sides = [
        (pick_one(rows_of, core), mine, gathered),
        (pick_one(rows_of, 1 - core), far_exps, far_gathered),
    ]
    given = head_block(starts, sides, columns_here, columns_here, features, partial)
    from_across = lax.ppermute(given, "xl", SWAP)
    kept = head_block(starts, sides, 0, columns_here, features, shares)
    head_grad = kept.astype(F32) + from_across.astype(F32)
    return hidden_grad.astype(BF16), head_grad.astype(BF16).T


def solution(mesh):
    names = ("z", "core", "xh", "xl", "y")
    fine = Mesh(mesh.devices.reshape(Z, CORES, XH, XL, Y), names)
    by_token, by_column = ("z", "core"), P(None, names)
    return jax.shard_map(
        on_device,
        mesh=fine,
        in_specs=(P(by_token, None), by_column, P(by_token), P(by_token), P(by_token)),
        out_specs=(P(by_token, names[2:]), by_column),
        check_vma=False,
    )
```

```python
import jax
import jax.numpy as jnp
from jax import lax
from jax.experimental import pallas as pl
from jax.experimental.pallas import tpu as pltpu
from jax.sharding import Mesh, PartitionSpec as P

F32 = jnp.float32
BF16 = jnp.bfloat16
Z, CORES, XH, XL, Y = 8, 2, 2, 2, 4
PLANE = XH * XL * Y
SWAP = [(0, 1), (1, 0)]
LANES = 128
STEPS = 7
PARAMS = pltpu.CompilerParams(vmem_limit_bytes=56 << 20)
SMEM = pl.BlockSpec(memory_space=pltpu.SMEM)
VMEM = pl.BlockSpec(memory_space=pltpu.VMEM)
ANY = pl.BlockSpec(memory_space=pl.ANY)


def broadcast_gather(part, axes, count):
    copies = jnp.broadcast_to(part[None], (count,) + part.shape)
    return lax.all_to_all(copies, axes, 0, 0, tiled=True)


def dot(left, right, contract):
    return lax.dot_general(left, right, (contract, ((), ())), preferred_element_type=F32)


def cost(flops, nbytes):
    return pl.CostEstimate(flops=flops, bytes_accessed=nbytes, transcendentals=0)


def matches_of(starts_ref, low, rows, columns_here, ids):
    number = low // columns_here
    row = lax.broadcasted_iota(jnp.int32, (rows, ids.shape[1]), 0) + (low - number * columns_here)
    return row + starts_ref[number] == ids


def logits_and_stats(starts, hidden, weights, columns_here):
    features = weights[0].shape[1]
    count = len(weights)
    sizes = [piece.shape[0] for piece in weights]
    offsets = [sum(sizes[:i]) for i in range(count)]
    columns, tokens = sum(sizes), hidden.shape[0]
    block = features // STEPS
    blocks = columns // columns_here

    def body(starts_ref, h_ref, *refs):
        w_refs = refs[:count]
        *exps_refs, stats_ref, _, w, h, f, held, exps, sems, out = refs[count:]

        def loads(k):
            span = pl.ds(k * block, block)
            return [pltpu.make_async_copy(h_ref.at[:, span], h.at[k], sems.at[k, count])] + [
                pltpu.make_async_copy(
                    w_refs[i].at[:, span], w.at[k, pl.ds(offsets[i], sizes[i])], sems.at[k, i]
                )
                for i in range(count)
            ]

        copies = [loads(k) for k in range(STEPS)]
        facts_copy = pltpu.make_async_copy(
            h_ref.at[:, pl.ds(features, LANES)], f, sems.at[STEPS, 0]
        )
        for copy in copies[0] + copies[1] + [facts_copy]:
            copy.start()
        for k in range(STEPS):
            for copy in copies[k]:
                copy.wait()
            if k + 2 < STEPS:
                for copy in copies[k + 2]:
                    copy.start()
            part = dot(w[k], h[k], ((1,), (1,)))
            held[...] = part if k == 0 else held[...] + part
        facts_copy.wait()
        facts = f[...].astype(F32).T
        token_id = facts[0:1] * 16384.0 + facts[1:2] * 128.0 + facts[2:3]
        teacher = facts[4:5] + facts[5:6] + facts[6:7]
        ids = token_id.astype(jnp.int32)
        top = jnp.max(held[...], axis=0, keepdims=True)
        total, picked = jnp.zeros_like(top), jnp.zeros_like(top)
        sends = []
        for i in range(blocks):
            low = i * columns_here
            logits = held[low : low + columns_here]
            grown = jnp.exp(logits - top)
            total += jnp.sum(grown, axis=0, keepdims=True)
            exps[low : low + columns_here] = grown.astype(BF16)
            into = exps_refs[2 * i // blocks].at[pl.ds(low % (columns // 2), columns_here)]
            sends.append(
                pltpu.make_async_copy(exps.at[pl.ds(low, columns_here)], into, out.at[i])
            )
            sends[-1].start()
            match = matches_of(starts_ref, low, columns_here, columns_here, ids)
            picked += jnp.sum(jnp.where(match, logits, 0.0), axis=0, keepdims=True)
        zero = jnp.zeros_like(top)
        stats_ref[...] = jnp.concatenate(
            [top, total, picked, facts[3:4], teacher, token_id, zero, zero]
        )
        for send in sends:
            send.wait()

    return pl.pallas_call(
        body,
        in_specs=[SMEM, ANY] + [ANY] * count,
        out_specs=[ANY, ANY, VMEM, ANY],
        out_shape=[jax.ShapeDtypeStruct((columns // 2, tokens), BF16)] * 2
        + [
            jax.ShapeDtypeStruct((8, tokens), F32),
            jax.ShapeDtypeStruct(hidden.shape, hidden.dtype),
        ],
        input_output_aliases={1: 3},
        scratch_shapes=[
            pltpu.VMEM((STEPS, columns, block), BF16),
            pltpu.VMEM((STEPS, tokens, block), BF16),
            pltpu.VMEM((tokens, LANES), BF16),
            pltpu.VMEM((columns, tokens), F32),
            pltpu.VMEM((columns, tokens), BF16),
            pltpu.SemaphoreType.DMA((STEPS + 1, count + 1)),
            pltpu.SemaphoreType.DMA((blocks,)),
        ],
        compiler_params=PARAMS,
        cost_estimate=cost(
            2 * columns * tokens * features, 2 * features * (columns + tokens) + 2 * columns * tokens
        ),
    )(starts, hidden, *weights)


def merge_stats(parts, own, after):
    lines = own.shape[0] // 8

    def body(parts_ref, own_ref, _, out_ref):
        tops = parts_ref[:, :lines]
        top = jnp.max(tops, axis=0)
        out_ref[:lines] = top
        out_ref[lines : 2 * lines] = jnp.sum(
            parts_ref[:, lines : 2 * lines] * jnp.exp(tops - top[None]), axis=0
        )
        out_ref[2 * lines : 3 * lines] = jnp.sum(parts_ref[:, 2 * lines :], axis=0)
        out_ref[3 * lines :] = own_ref[3 * lines : 5 * lines]

    return pl.pallas_call(
        body,
        in_specs=[VMEM, VMEM, ANY],
        out_specs=VMEM,
        out_shape=jax.ShapeDtypeStruct((5 * lines, LANES), F32),
        compiler_params=PARAMS,
        cost_estimate=cost(0, 4 * parts.size),
    )(parts, own, after)


def change_of(starts_ref, rows_ref, exps, low, columns_here, scaled):
    ids = rows_ref[0:1].astype(jnp.int32)
    match = matches_of(starts_ref, low, exps.shape[0], columns_here, ids)
    change = jnp.where(match, 1.0, 0.0) - exps.astype(F32) * rows_ref[1:2]
    return (change * rows_ref[2:3] if scaled else change).astype(BF16)


def partial_product(starts, token_rows, exps_t, weights, columns_here):
    half, tokens = exps_t[0].shape
    columns = 2 * half
    features = weights[0].shape[1]
    count = len(weights)
    sizes = [piece.shape[0] for piece in weights]
    offsets = [sum(sizes[:i]) for i in range(count)]
    block = features // STEPS

    def body(starts_ref, rows_ref, first_ref, last_ref, *refs):
        w_refs = refs[:count]
        out_ref, exps, w, held, ready, e_sems, w_sems, sems = refs[count:]
        first = [
            pltpu.make_async_copy(ref, exps.at[pl.ds(i * half, half)], e_sems.at[i])
            for i, ref in enumerate((first_ref, last_ref))
        ]
        loads = [
            [
                pltpu.make_async_copy(
                    w_refs[i].at[:, pl.ds(k * block, block)],
                    w.at[k, pl.ds(offsets[i], sizes[i])],
                    w_sems.at[k, i],
                )
                for i in range(count)
            ]
            for k in range(STEPS)
        ]
        for copy in first + loads[0] + loads[1]:
            copy.start()
        for low in range(0, columns, columns_here):
            if low % half == 0:
                first[low // half].wait()
            held[low : low + columns_here] = change_of(
                starts_ref, rows_ref, exps[low : low + columns_here], low, columns_here, False
            )

        def send(k):
            return pltpu.make_async_copy(
                ready.at[k % 2], out_ref.at[:, pl.ds(k * block, block)], sems.at[k % 2]
            )

        for k in range(STEPS):
            for copy in loads[k]:
                copy.wait()
            if k + 2 < STEPS:
                for copy in loads[k + 2]:
                    copy.start()
            out = dot(held[...], w[k], ((0,), (0,)))
            if k >= 2:
                send(k - 2).wait()
            ready[k % 2] = out.astype(BF16)
            send(k).start()
        send(STEPS - 2).wait()
        send(STEPS - 1).wait()

    return pl.pallas_call(
        body,
        in_specs=[SMEM, VMEM, ANY, ANY] + [ANY] * count,
        out_specs=ANY,
        out_shape=jax.ShapeDtypeStruct((tokens, features), BF16),
        scratch_shapes=[
            pltpu.VMEM((columns, tokens), BF16),
            pltpu.VMEM((STEPS, columns, block), BF16),
            pltpu.VMEM((columns, tokens), BF16),
            pltpu.VMEM((2, tokens, block), BF16),
            pltpu.SemaphoreType.DMA((2,)),
            pltpu.SemaphoreType.DMA((STEPS, count)),
            pltpu.SemaphoreType.DMA((2,)),
        ],
        compiler_params=PARAMS,
        cost_estimate=cost(
            2 * columns * tokens * features, 2 * features * (columns + tokens) + 2 * columns * tokens
        ),
    )(starts, token_rows, *exps_t, *weights)


def head_block(starts, sides, low, columns_here, features, after):
    tokens = sides[0][2].shape[0]
    block = features // STEPS
    count = len(sides)

    def body(starts_ref, *refs):
        rows_refs, exps_refs, h_refs = refs[0 : 3 * count : 3], refs[1 : 3 * count : 3], refs[2 : 3 * count : 3]
        out_ref, exps, h, held, ready, e_sems, h_sems, sems = refs[3 * count + 1 :]
        first = [
            pltpu.make_async_copy(ref.at[pl.ds(low, columns_here)], exps.at[i], e_sems.at[i])
            for i, ref in enumerate(exps_refs)
        ]
        loads = [
            [
                pltpu.make_async_copy(
                    ref.at[:, pl.ds(k * block, block)], h.at[k, i], h_sems.at[k, i]
                )
                for i, ref in enumerate(h_refs)
            ]
            for k in range(STEPS)
        ]
        for copy in first + loads[0] + loads[1]:
            copy.start()
        for i in range(count):
            first[i].wait()
            held[i] = change_of(starts_ref, rows_refs[i], exps[i], low, columns_here, True)

        def send(k):
            return pltpu.make_async_copy(
                ready.at[k % 2], out_ref.at[:, pl.ds(k * block, block)], sems.at[k % 2]
            )

        for k in range(STEPS):
            if k + 2 < STEPS:
                for copy in loads[k + 2]:
                    copy.start()
            out = None
            for i in range(count):
                loads[k][i].wait()
                part = dot(held[i], h[k, i], ((1,), (0,)))
                out = part if out is None else out + part
            if k >= 2:
                send(k - 2).wait()
            ready[k % 2] = out.astype(BF16)
            send(k).start()
        send(STEPS - 2).wait()
        send(STEPS - 1).wait()

    return pl.pallas_call(
        body,
        in_specs=[SMEM] + [VMEM, ANY, ANY] * count + [ANY],
        out_specs=ANY,
        out_shape=jax.ShapeDtypeStruct((columns_here, features), BF16),
        scratch_shapes=[
            pltpu.VMEM((count, columns_here, tokens), BF16),
            pltpu.VMEM((STEPS, count, tokens, block), BF16),
            pltpu.VMEM((count, columns_here, tokens), BF16),
            pltpu.VMEM((2, columns_here, block), BF16),
            pltpu.SemaphoreType.DMA((count,)),
            pltpu.SemaphoreType.DMA((STEPS, count)),
            pltpu.SemaphoreType.DMA((2,)),
        ],
        compiler_params=PARAMS,
        cost_estimate=cost(
            2 * count * columns_here * tokens * features, 2 * features * (columns_here + count * tokens)
        ),
    )(starts, *(operand for side in sides for operand in side), after)


def cut_features(values, width):
    rows, features = values.shape
    count = features // width

    def body(in_ref, out_ref):
        values = in_ref[...]
        for i in range(count):
            out_ref[i] = values[:, i * width : (i + 1) * width]

    return pl.pallas_call(
        body,
        in_specs=[VMEM],
        out_specs=VMEM,
        out_shape=jax.ShapeDtypeStruct((count, rows, width), values.dtype),
        compiler_params=PARAMS,
        cost_estimate=cost(0, 4 * rows * features),
    )(values)


def pack_facts(token_ids, response_mask, teacher_logprob):
    high = lax.reduce_precision(teacher_logprob, 8, 7)
    rest = teacher_logprob - high
    middle = lax.reduce_precision(rest, 8, 7)
    fields = [
        token_ids // 16384,
        token_ids // 128 % 128,
        token_ids % 128,
        response_mask,
        high,
        middle,
        rest - middle,
    ]
    fields = jnp.stack([field.astype(F32) for field in fields], axis=1).astype(BF16)
    return jnp.pad(fields, ((0, 0), (0, LANES - fields.shape[1])))


def pick_one(values, *places):
    for place in places:
        values = lax.dynamic_index_in_dim(values, place, 0, False)
    return values


def on_device(hidden, weight, token_ids, response_mask, teacher_logprob):
    own_rows, features = hidden.shape
    columns_here = weight.shape[1]
    core, z = lax.axis_index("core"), lax.axis_index("z")
    xh, side, y = lax.axis_index("xh"), lax.axis_index("xl"), lax.axis_index("y")
    rows = own_rows // 2
    here = Z * rows
    lines = here // LANES
    tokens = own_rows * Z * CORES

    own = weight.T
    across = lax.ppermute(own, "xl", SWAP)
    own_other = lax.ppermute(own, "core", SWAP)
    facts = pack_facts(token_ids, response_mask, teacher_logprob)
    gathered = lax.all_gather(
        lax.dynamic_slice_in_dim(jnp.concatenate([hidden, facts], axis=1), side * rows, rows, 0),
        "z",
        axis=0,
        tiled=True,
    )
    weights = [own, across, own_other, lax.ppermute(across, "core", SWAP)]
    starts = jnp.stack(
        [
            (((z * CORES + c) * XH + xh) * XL + s) * Y * columns_here + y * columns_here
            for c in (core, 1 - core)
            for s in (side, 1 - side)
        ]
    ).astype(jnp.int32)

    mine, theirs, stats, gathered = logits_and_stats(starts, gathered, weights, columns_here)
    far_gathered = lax.ppermute(gathered, "core", SWAP)
    far_exps = lax.ppermute(theirs, "core", SWAP)
    lined = stats.reshape(8 * lines, LANES)
    shared = merge_stats(broadcast_gather(lined[: 3 * lines], "z", Z), lined, far_gathered)
    shared = broadcast_gather(shared, ("xh", "xl", "y"), PLANE)
    shared = shared.reshape(XH, XL, Y, 5, lines, LANES)
    top = jnp.max(shared[:, :, :, 0], axis=(0, 2))
    shrink = jnp.exp(shared[:, :, :, 0] - top[None, :, None])
    total = jnp.sum(shared[:, :, :, 1] * shrink, axis=(0, 2))
    picked = jnp.sum(shared[:, :, :, 2], axis=(0, 2))
    norms = top + jnp.log(total)
    factor = jnp.exp(stats[0] - pick_one(norms, side).reshape(here))
    token_rows = jnp.stack([stats[5], factor])

    partial = partial_product(starts, token_rows, (mine, theirs), weights, columns_here)
    summed = lax.psum_scatter(partial, "z", scatter_dimension=0, tiled=True)
    cut = features // PLANE
    shares = cut_features(summed, cut)
    summed = lax.all_to_all(shares, ("xh", "xl", "y"), 0, 0, tiled=True)
    summed = summed.reshape(XH, XL, Y, rows, cut).astype(F32)
    summed = jnp.sum(summed, axis=(0, 2)).reshape(own_rows, cut)

    mask, teacher = shared[0, :, 0, 3], shared[0, :, 0, 4]
    ratio = mask * (picked - norms - teacher)
    known = jnp.concatenate([part.reshape(XL, here) for part in (mask, ratio)] + [token_rows])
    known = jnp.stack([known, lax.ppermute(known, "core", SWAP)])
    mask, ratio = (
        part.reshape(CORES, XL, Z, rows) for part in (known[:, :XL], known[:, XL : 2 * XL])
    )
    steps = jnp.arange(rows, dtype=jnp.int32)
    later = (steps[None, :] >= steps[:, None]).astype(F32)
    within = jnp.sum(ratio[..., None, :] * later, axis=-1)
    parts = jnp.sum(ratio, axis=-1).reshape(-1)
    number = jnp.arange(XL * Z, dtype=jnp.int32)
    order = number % Z * (CORES * XL) + number // Z
    order = jnp.concatenate([order + core * XL, order + (1 - core) * XL])
    beyond = jnp.sum(parts[None, :] * (order[None, :] > order[:, None]), axis=1)
    scales = mask * (within + beyond.reshape(CORES, XL, Z, 1)) / float(tokens)

    own_scale = lax.dynamic_index_in_dim(scales[0], z, 1, False).reshape(own_rows)
    hidden_grad = summed * own_scale[:, None]

    scale = lax.dynamic_index_in_dim(scales, side, 1, False).reshape(CORES, 1, here)
    rows_of = jnp.concatenate([known[:, 2 * XL :], scale], axis=1)
    sides = [(rows_of[0], mine, gathered), (rows_of[1], far_exps, far_gathered)]
    given = head_block(starts, sides, columns_here, columns_here, features, partial)
    from_across = lax.ppermute(given, "xl", SWAP)
    kept = head_block(starts, sides, 0, columns_here, features, shares)
    head_grad = kept.astype(F32) + from_across.astype(F32)
    return hidden_grad.astype(BF16), head_grad.astype(BF16).T


def solution(mesh):
    names = ("z", "core", "xh", "xl", "y")
    fine = Mesh(mesh.devices.reshape(Z, CORES, XH, XL, Y), names)
    by_token, by_column = ("z", "core"), P(None, names)
    return jax.shard_map(
        on_device,
        mesh=fine,
        in_specs=(P(by_token, None), by_column, P(by_token), P(by_token), P(by_token)),
        out_specs=(P(by_token, names[2:]), by_column),
        check_vma=False,
    )
```

```python
import jax
import jax.numpy as jnp
from jax import lax
from jax.experimental import pallas as pl
from jax.experimental.pallas import tpu as pltpu
from jax.sharding import Mesh, PartitionSpec as P

F32 = jnp.float32
BF16 = jnp.bfloat16
Z, CORES, XH, XL, Y = 8, 2, 2, 2, 4
PLANE = XH * XL * Y
SWAP = [(0, 1), (1, 0)]
LANES = 128
STEPS = 7
PARAMS = pltpu.CompilerParams(vmem_limit_bytes=56 << 20)
SMEM = pl.BlockSpec(memory_space=pltpu.SMEM)
VMEM = pl.BlockSpec(memory_space=pltpu.VMEM)
ANY = pl.BlockSpec(memory_space=pl.ANY)


def broadcast_gather(part, axes, count):
    copies = jnp.broadcast_to(part[None], (count,) + part.shape)
    return lax.all_to_all(copies, axes, 0, 0, tiled=True)


def dot(left, right, contract):
    return lax.dot_general(left, right, (contract, ((), ())), preferred_element_type=F32)


def cost(flops, nbytes):
    return pl.CostEstimate(flops=flops, bytes_accessed=nbytes, transcendentals=0)


def matches_of(starts_ref, low, rows, columns_here, ids):
    number = low // columns_here
    row = lax.broadcasted_iota(jnp.int32, (rows, ids.shape[1]), 0) + (low - number * columns_here)
    return row + starts_ref[number] == ids


def logits_and_stats(starts, hidden, weights, columns_here):
    features = weights[0].shape[1]
    count = len(weights)
    sizes = [piece.shape[0] for piece in weights]
    offsets = [sum(sizes[:i]) for i in range(count)]
    columns, tokens = sum(sizes), hidden.shape[0]
    block = features // STEPS
    blocks = columns // columns_here

    def body(starts_ref, h_ref, *refs):
        w_refs = refs[:count]
        *exps_refs, stats_ref, _, w, h, f, held, exps, sems, out = refs[count:]

        def loads(k):
            span = pl.ds(k * block, block)
            return [pltpu.make_async_copy(h_ref.at[:, span], h.at[k], sems.at[k, count])] + [
                pltpu.make_async_copy(
                    w_refs[i].at[:, span], w.at[k, pl.ds(offsets[i], sizes[i])], sems.at[k, i]
                )
                for i in range(count)
            ]

        copies = [loads(k) for k in range(STEPS)]
        facts_copy = pltpu.make_async_copy(
            h_ref.at[:, pl.ds(features, LANES)], f, sems.at[STEPS, 0]
        )
        for copy in copies[0] + copies[1] + [facts_copy]:
            copy.start()
        for k in range(STEPS):
            for copy in copies[k]:
                copy.wait()
            if k + 2 < STEPS:
                for copy in copies[k + 2]:
                    copy.start()
            part = dot(w[k], h[k], ((1,), (1,)))
            held[...] = part if k == 0 else held[...] + part
        facts_copy.wait()
        facts = f[...].astype(F32).T
        token_id = facts[0:1] * 16384.0 + facts[1:2] * 128.0 + facts[2:3]
        teacher = facts[4:5] + facts[5:6] + facts[6:7]
        ids = token_id.astype(jnp.int32)
        top = jnp.max(held[...], axis=0, keepdims=True)
        total, picked = jnp.zeros_like(top), jnp.zeros_like(top)
        sends = []
        for i in range(blocks):
            low = i * columns_here
            logits = held[low : low + columns_here]
            grown = jnp.exp(logits - top)
            total += jnp.sum(grown, axis=0, keepdims=True)
            exps[low : low + columns_here] = grown.astype(BF16)
            into = exps_refs[2 * i // blocks].at[pl.ds(low % (columns // 2), columns_here)]
            sends.append(
                pltpu.make_async_copy(exps.at[pl.ds(low, columns_here)], into, out.at[i])
            )
            sends[-1].start()
            match = matches_of(starts_ref, low, columns_here, columns_here, ids)
            picked += jnp.sum(jnp.where(match, logits, 0.0), axis=0, keepdims=True)
        zero = jnp.zeros_like(top)
        stats_ref[...] = jnp.concatenate(
            [top, total, picked, facts[3:4], teacher, token_id, zero, zero]
        )
        for send in sends:
            send.wait()

    return pl.pallas_call(
        body,
        in_specs=[SMEM, ANY] + [ANY] * count,
        out_specs=[ANY, ANY, VMEM, ANY],
        out_shape=[jax.ShapeDtypeStruct((columns // 2, tokens), BF16)] * 2
        + [
            jax.ShapeDtypeStruct((8, tokens), F32),
            jax.ShapeDtypeStruct(hidden.shape, hidden.dtype),
        ],
        input_output_aliases={1: 3},
        scratch_shapes=[
            pltpu.VMEM((STEPS, columns, block), BF16),
            pltpu.VMEM((STEPS, tokens, block), BF16),
            pltpu.VMEM((tokens, LANES), BF16),
            pltpu.VMEM((columns, tokens), F32),
            pltpu.VMEM((columns, tokens), BF16),
            pltpu.SemaphoreType.DMA((STEPS + 1, count + 1)),
            pltpu.SemaphoreType.DMA((blocks,)),
        ],
        compiler_params=PARAMS,
        cost_estimate=cost(
            2 * columns * tokens * features, 2 * features * (columns + tokens) + 2 * columns * tokens
        ),
    )(starts, hidden, *weights)


def merge_stats(parts, own, after):
    lines = own.shape[0] // 8

    def body(parts_ref, own_ref, _, out_ref):
        def field(number):
            return own_ref[number * lines : (number + 1) * lines]

        tops = parts_ref[:, :lines]
        top = jnp.max(tops, axis=0)
        sums = parts_ref[:, lines : 2 * lines] * jnp.exp(tops - top[None])
        norm = top + jnp.log(jnp.sum(sums, axis=0))
        picked = jnp.sum(parts_ref[:, 2 * lines :], axis=0)
        mask = field(3)
        out_ref[:lines] = field(5)
        out_ref[lines : 2 * lines] = jnp.exp(field(0) - norm)
        out_ref[2 * lines : 3 * lines] = mask
        out_ref[3 * lines :] = mask * (picked - norm - field(4))

    return pl.pallas_call(
        body,
        in_specs=[VMEM, VMEM, ANY],
        out_specs=VMEM,
        out_shape=jax.ShapeDtypeStruct((4 * lines, LANES), F32),
        compiler_params=PARAMS,
        cost_estimate=cost(0, 4 * parts.size),
    )(parts, own, after)


def change_of(starts_ref, rows_ref, exps, low, columns_here, scaled):
    ids = rows_ref[0:1].astype(jnp.int32)
    match = matches_of(starts_ref, low, exps.shape[0], columns_here, ids)
    change = jnp.where(match, 1.0, 0.0) - exps.astype(F32) * rows_ref[1:2]
    return (change * rows_ref[2:3] if scaled else change).astype(BF16)


def partial_product(starts, token_rows, exps_t, weights, columns_here):
    half, tokens = exps_t[0].shape
    columns = 2 * half
    features = weights[0].shape[1]
    count = len(weights)
    sizes = [piece.shape[0] for piece in weights]
    offsets = [sum(sizes[:i]) for i in range(count)]
    block = features // STEPS

    def body(starts_ref, rows_ref, first_ref, last_ref, *refs):
        w_refs = refs[:count]
        out_ref, exps, w, held, ready, e_sems, w_sems, sems = refs[count:]
        first = [
            pltpu.make_async_copy(ref, exps.at[pl.ds(i * half, half)], e_sems.at[i])
            for i, ref in enumerate((first_ref, last_ref))
        ]
        loads = [
            [
                pltpu.make_async_copy(
                    w_refs[i].at[:, pl.ds(k * block, block)],
                    w.at[k, pl.ds(offsets[i], sizes[i])],
                    w_sems.at[k, i],
                )
                for i in range(count)
            ]
            for k in range(STEPS)
        ]
        for copy in first + loads[0] + loads[1]:
            copy.start()
        for low in range(0, columns, columns_here):
            if low % half == 0:
                first[low // half].wait()
            held[low : low + columns_here] = change_of(
                starts_ref, rows_ref, exps[low : low + columns_here], low, columns_here, False
            )

        def send(k):
            return pltpu.make_async_copy(
                ready.at[k % 2], out_ref.at[:, pl.ds(k * block, block)], sems.at[k % 2]
            )

        for k in range(STEPS):
            for copy in loads[k]:
                copy.wait()
            if k + 2 < STEPS:
                for copy in loads[k + 2]:
                    copy.start()
            out = dot(held[...], w[k], ((0,), (0,)))
            if k >= 2:
                send(k - 2).wait()
            ready[k % 2] = out.astype(BF16)
            send(k).start()
        send(STEPS - 2).wait()
        send(STEPS - 1).wait()

    return pl.pallas_call(
        body,
        in_specs=[SMEM, VMEM, ANY, ANY] + [ANY] * count,
        out_specs=ANY,
        out_shape=jax.ShapeDtypeStruct((tokens, features), BF16),
        scratch_shapes=[
            pltpu.VMEM((columns, tokens), BF16),
            pltpu.VMEM((STEPS, columns, block), BF16),
            pltpu.VMEM((columns, tokens), BF16),
            pltpu.VMEM((2, tokens, block), BF16),
            pltpu.SemaphoreType.DMA((2,)),
            pltpu.SemaphoreType.DMA((STEPS, count)),
            pltpu.SemaphoreType.DMA((2,)),
        ],
        compiler_params=PARAMS,
        cost_estimate=cost(
            2 * columns * tokens * features, 2 * features * (columns + tokens) + 2 * columns * tokens
        ),
    )(starts, token_rows, *exps_t, *weights)


def head_block(starts, sides, low, columns_here, features, after):
    tokens = sides[0][2].shape[0]
    block = features // STEPS
    count = len(sides)

    def body(starts_ref, *refs):
        rows_refs, exps_refs, h_refs = refs[0 : 3 * count : 3], refs[1 : 3 * count : 3], refs[2 : 3 * count : 3]
        out_ref, exps, h, held, ready, e_sems, h_sems, sems = refs[3 * count + 1 :]
        first = [
            pltpu.make_async_copy(ref.at[pl.ds(low, columns_here)], exps.at[i], e_sems.at[i])
            for i, ref in enumerate(exps_refs)
        ]
        loads = [
            [
                pltpu.make_async_copy(
                    ref.at[:, pl.ds(k * block, block)], h.at[k, i], h_sems.at[k, i]
                )
                for i, ref in enumerate(h_refs)
            ]
            for k in range(STEPS)
        ]
        for copy in first + loads[0] + loads[1]:
            copy.start()
        for i in range(count):
            first[i].wait()
            held[i] = change_of(starts_ref, rows_refs[i], exps[i], low, columns_here, True)

        def send(k):
            return pltpu.make_async_copy(
                ready.at[k % 2], out_ref.at[:, pl.ds(k * block, block)], sems.at[k % 2]
            )

        for k in range(STEPS):
            if k + 2 < STEPS:
                for copy in loads[k + 2]:
                    copy.start()
            out = None
            for i in range(count):
                loads[k][i].wait()
                part = dot(held[i], h[k, i], ((1,), (0,)))
                out = part if out is None else out + part
            if k >= 2:
                send(k - 2).wait()
            ready[k % 2] = out.astype(BF16)
            send(k).start()
        send(STEPS - 2).wait()
        send(STEPS - 1).wait()

    return pl.pallas_call(
        body,
        in_specs=[SMEM] + [VMEM, ANY, ANY] * count + [ANY],
        out_specs=ANY,
        out_shape=jax.ShapeDtypeStruct((columns_here, features), BF16),
        scratch_shapes=[
            pltpu.VMEM((count, columns_here, tokens), BF16),
            pltpu.VMEM((STEPS, count, tokens, block), BF16),
            pltpu.VMEM((count, columns_here, tokens), BF16),
            pltpu.VMEM((2, columns_here, block), BF16),
            pltpu.SemaphoreType.DMA((count,)),
            pltpu.SemaphoreType.DMA((STEPS, count)),
            pltpu.SemaphoreType.DMA((2,)),
        ],
        compiler_params=PARAMS,
        cost_estimate=cost(
            2 * count * columns_here * tokens * features, 2 * features * (columns_here + count * tokens)
        ),
    )(starts, *(operand for side in sides for operand in side), after)


def cut_features(values, width):
    rows, features = values.shape
    count = features // width

    def body(in_ref, out_ref):
        values = in_ref[...]
        for i in range(count):
            out_ref[i] = values[:, i * width : (i + 1) * width]

    return pl.pallas_call(
        body,
        in_specs=[VMEM],
        out_specs=VMEM,
        out_shape=jax.ShapeDtypeStruct((count, rows, width), values.dtype),
        compiler_params=PARAMS,
        cost_estimate=cost(0, 4 * rows * features),
    )(values)


def pack_facts(token_ids, response_mask, teacher_logprob):
    high = lax.reduce_precision(teacher_logprob, 8, 7)
    rest = teacher_logprob - high
    middle = lax.reduce_precision(rest, 8, 7)
    fields = [
        token_ids // 16384,
        token_ids // 128 % 128,
        token_ids % 128,
        response_mask,
        high,
        middle,
        rest - middle,
    ]
    fields = jnp.stack([field.astype(F32) for field in fields], axis=1).astype(BF16)
    return jnp.pad(fields, ((0, 0), (0, LANES - fields.shape[1])))


def pick_one(values, *places):
    for place in places:
        values = lax.dynamic_index_in_dim(values, place, 0, False)
    return values


def on_device(hidden, weight, token_ids, response_mask, teacher_logprob):
    own_rows, features = hidden.shape
    columns_here = weight.shape[1]
    core, z = lax.axis_index("core"), lax.axis_index("z")
    xh, side, y = lax.axis_index("xh"), lax.axis_index("xl"), lax.axis_index("y")
    rows = own_rows // 2
    here = Z * rows
    lines = here // LANES
    tokens = own_rows * Z * CORES

    own = weight.T
    across = lax.ppermute(own, "xl", SWAP)
    own_other = lax.ppermute(own, "core", SWAP)
    facts = pack_facts(token_ids, response_mask, teacher_logprob)
    gathered = lax.all_gather(
        lax.dynamic_slice_in_dim(jnp.concatenate([hidden, facts], axis=1), side * rows, rows, 0),
        "z",
        axis=0,
        tiled=True,
    )
    weights = [own, across, own_other, lax.ppermute(across, "core", SWAP)]
    starts = jnp.stack(
        [
            (((z * CORES + c) * XH + xh) * XL + s) * Y * columns_here + y * columns_here
            for c in (core, 1 - core)
            for s in (side, 1 - side)
        ]
    ).astype(jnp.int32)

    mine, theirs, stats, gathered = logits_and_stats(starts, gathered, weights, columns_here)
    far_gathered = lax.ppermute(gathered, "core", SWAP)
    far_exps = lax.ppermute(theirs, "core", SWAP)
    lined = stats.reshape(8 * lines, LANES)
    shared = broadcast_gather(lined[: 3 * lines], ("z", "xh", "y"), Z * XH * Y)
    known = merge_stats(shared, lined, far_gathered).reshape(4, here)

    partial = partial_product(starts, known, (mine, theirs), weights, columns_here)
    summed = lax.psum_scatter(partial, "z", scatter_dimension=0, tiled=True)
    cut = features // PLANE
    shares = cut_features(summed, cut)
    summed = lax.all_to_all(shares, ("xh", "xl", "y"), 0, 0, tiled=True)
    summed = summed.reshape(XH, XL, Y, rows, cut).astype(F32)
    summed = jnp.sum(summed, axis=(0, 2)).reshape(own_rows, cut)

    known = jnp.stack([known, lax.ppermute(known, "core", SWAP)])
    mask, ratio = (
        part.reshape(CORES, XL, Z, rows)
        for part in jnp.stack([known[:, 2:], lax.ppermute(known[:, 2:], "xl", SWAP)], axis=1).transpose(2, 0, 1, 3)
    )
    steps = jnp.arange(rows, dtype=jnp.int32)
    later = (steps[None, :] >= steps[:, None]).astype(F32)
    within = jnp.sum(ratio[..., None, :] * later, axis=-1)
    parts = jnp.sum(ratio, axis=-1).reshape(-1)
    order = jnp.arange(Z, dtype=jnp.int32) * (CORES * XL)
    order = jnp.concatenate(
        [order + (c * XL + s) for c in (core, 1 - core) for s in (side, 1 - side)]
    )
    beyond = jnp.sum(parts[None, :] * (order[None, :] > order[:, None]), axis=1)
    scales = mask * (within + beyond.reshape(CORES, XL, Z, 1)) / float(tokens)

    own_scale = lax.dynamic_index_in_dim(scales[0], z, 1, False)
    own_scale = jnp.where(side == 0, own_scale, own_scale[::-1]).reshape(own_rows)
    hidden_grad = summed * own_scale[:, None]

    rows_of = jnp.concatenate([known[:, :2], scales[:, 0].reshape(CORES, 1, here)], axis=1)
    sides = [(rows_of[0], mine, gathered), (rows_of[1], far_exps, far_gathered)]
    given = head_block(starts, sides, columns_here, columns_here, features, partial)
    from_across = lax.ppermute(given, "xl", SWAP)
    kept = head_block(starts, sides, 0, columns_here, features, shares)
    head_grad = kept.astype(F32) + from_across.astype(F32)
    return hidden_grad.astype(BF16), head_grad.astype(BF16).T


def solution(mesh):
    names = ("z", "core", "xh", "xl", "y")
    fine = Mesh(mesh.devices.reshape(Z, CORES, XH, XL, Y), names)
    by_token, by_column = ("z", "core"), P(None, names)
    return jax.shard_map(
        on_device,
        mesh=fine,
        in_specs=(P(by_token, None), by_column, P(by_token), P(by_token), P(by_token)),
        out_specs=(P(by_token, names[2:]), by_column),
        check_vma=False,
    )
```

```python
import jax
import jax.numpy as jnp
from jax import lax
from jax.experimental import pallas as pl
from jax.experimental.pallas import tpu as pltpu
from jax.sharding import Mesh, PartitionSpec as P

F32 = jnp.float32
BF16 = jnp.bfloat16
Z, CORES, XH, XL, Y = 8, 2, 2, 2, 4
PLANE = XH * XL * Y
SWAP = [(0, 1), (1, 0)]
LANES = 128
STEPS = 7
PARAMS = pltpu.CompilerParams(vmem_limit_bytes=56 << 20)
SMEM = pl.BlockSpec(memory_space=pltpu.SMEM)
VMEM = pl.BlockSpec(memory_space=pltpu.VMEM)
ANY = pl.BlockSpec(memory_space=pl.ANY)


def broadcast_gather(part, axes, count):
    copies = jnp.broadcast_to(part[None], (count,) + part.shape)
    return lax.all_to_all(copies, axes, 0, 0, tiled=True)


def dot(left, right, contract):
    return lax.dot_general(left, right, (contract, ((), ())), preferred_element_type=F32)


def cost(flops, nbytes):
    return pl.CostEstimate(flops=flops, bytes_accessed=nbytes, transcendentals=0)


def matches_of(starts_ref, low, rows, columns_here, ids):
    number = low // columns_here
    row = lax.broadcasted_iota(jnp.int32, (rows, ids.shape[1]), 0) + (low - number * columns_here)
    return row + starts_ref[number] == ids


def logits_and_stats(starts, hidden, weights, columns_here):
    features = weights[0].shape[1]
    count = len(weights)
    sizes = [piece.shape[0] for piece in weights]
    offsets = [sum(sizes[:i]) for i in range(count)]
    columns, tokens = sum(sizes), hidden.shape[0]
    block = features // STEPS
    blocks = columns // columns_here

    def body(starts_ref, h_ref, *refs):
        w_refs = refs[:count]
        *exps_refs, stats_ref, _, w, h, f, held, exps, sems, out = refs[count:]

        def loads(k):
            span = pl.ds(k * block, block)
            return [pltpu.make_async_copy(h_ref.at[:, span], h.at[k], sems.at[k, count])] + [
                pltpu.make_async_copy(
                    w_refs[i].at[:, span], w.at[k, pl.ds(offsets[i], sizes[i])], sems.at[k, i]
                )
                for i in range(count)
            ]

        copies = [loads(k) for k in range(STEPS)]
        facts_copy = pltpu.make_async_copy(
            h_ref.at[:, pl.ds(features, LANES)], f, sems.at[STEPS, 0]
        )
        for copy in copies[0] + copies[1] + [facts_copy]:
            copy.start()
        for k in range(STEPS):
            for copy in copies[k]:
                copy.wait()
            if k + 2 < STEPS:
                for copy in copies[k + 2]:
                    copy.start()
            part = dot(w[k], h[k], ((1,), (1,)))
            held[...] = part if k == 0 else held[...] + part
        facts_copy.wait()
        facts = f[...].astype(F32).T
        token_id = facts[0:1] * 16384.0 + facts[1:2] * 128.0 + facts[2:3]
        teacher = facts[4:5] + facts[5:6] + facts[6:7]
        ids = token_id.astype(jnp.int32)
        top = jnp.max(held[...], axis=0, keepdims=True)
        total, picked = jnp.zeros_like(top), jnp.zeros_like(top)
        sends = []
        for i in range(blocks):
            low = i * columns_here
            logits = held[low : low + columns_here]
            grown = jnp.exp(logits - top)
            total += jnp.sum(grown, axis=0, keepdims=True)
            exps[low : low + columns_here] = grown.astype(BF16)
            into = exps_refs[2 * i // blocks].at[pl.ds(low % (columns // 2), columns_here)]
            sends.append(
                pltpu.make_async_copy(exps.at[pl.ds(low, columns_here)], into, out.at[i])
            )
            sends[-1].start()
            match = matches_of(starts_ref, low, columns_here, columns_here, ids)
            picked += jnp.sum(jnp.where(match, logits, 0.0), axis=0, keepdims=True)
        zero = jnp.zeros_like(top)
        stats_ref[...] = jnp.concatenate(
            [top, total, picked, facts[3:4], teacher, token_id, zero, zero]
        )
        for send in sends:
            send.wait()

    return pl.pallas_call(
        body,
        in_specs=[SMEM, ANY] + [ANY] * count,
        out_specs=[ANY, ANY, VMEM, ANY],
        out_shape=[jax.ShapeDtypeStruct((columns // 2, tokens), BF16)] * 2
        + [
            jax.ShapeDtypeStruct((8, tokens), F32),
            jax.ShapeDtypeStruct(hidden.shape, hidden.dtype),
        ],
        input_output_aliases={1: 3},
        scratch_shapes=[
            pltpu.VMEM((STEPS, columns, block), BF16),
            pltpu.VMEM((STEPS, tokens, block), BF16),
            pltpu.VMEM((tokens, LANES), BF16),
            pltpu.VMEM((columns, tokens), F32),
            pltpu.VMEM((columns, tokens), BF16),
            pltpu.SemaphoreType.DMA((STEPS + 1, count + 1)),
            pltpu.SemaphoreType.DMA((blocks,)),
        ],
        compiler_params=PARAMS,
        cost_estimate=cost(
            2 * columns * tokens * features, 2 * features * (columns + tokens) + 2 * columns * tokens
        ),
    )(starts, hidden, *weights)


def merge_stats(parts, own, after):
    lines = own.shape[0] // 8

    def body(parts_ref, own_ref, _, __, out_ref):
        tops = parts_ref[:, :lines]
        top = jnp.max(tops, axis=0)
        out_ref[:lines] = top
        out_ref[lines : 2 * lines] = jnp.sum(
            parts_ref[:, lines : 2 * lines] * jnp.exp(tops - top[None]), axis=0
        )
        out_ref[2 * lines : 3 * lines] = jnp.sum(parts_ref[:, 2 * lines :], axis=0)
        out_ref[3 * lines :] = own_ref[3 * lines : 5 * lines]

    return pl.pallas_call(
        body,
        in_specs=[VMEM, VMEM, ANY, ANY],
        out_specs=VMEM,
        out_shape=jax.ShapeDtypeStruct((5 * lines, LANES), F32),
        compiler_params=PARAMS,
        cost_estimate=cost(0, 4 * parts.size),
    )(parts, own, *after)


def change_of(starts_ref, rows_ref, exps, low, columns_here, scaled):
    ids = rows_ref[0:1].astype(jnp.int32)
    match = matches_of(starts_ref, low, exps.shape[0], columns_here, ids)
    change = jnp.where(match, 1.0, 0.0) - exps.astype(F32) * rows_ref[1:2]
    return (change * rows_ref[2:3] if scaled else change).astype(BF16)


def partial_product(starts, token_rows, exps_t, weights, columns_here):
    half, tokens = exps_t[0].shape
    columns = 2 * half
    features = weights[0].shape[1]
    count = len(weights)
    sizes = [piece.shape[0] for piece in weights]
    offsets = [sum(sizes[:i]) for i in range(count)]
    block = features // STEPS

    def body(starts_ref, rows_ref, first_ref, last_ref, *refs):
        w_refs = refs[:count]
        out_ref, exps, w, held, ready, e_sems, w_sems, sems = refs[count:]
        first = [
            pltpu.make_async_copy(ref, exps.at[pl.ds(i * half, half)], e_sems.at[i])
            for i, ref in enumerate((first_ref, last_ref))
        ]
        loads = [
            [
                pltpu.make_async_copy(
                    w_refs[i].at[:, pl.ds(k * block, block)],
                    w.at[k, pl.ds(offsets[i], sizes[i])],
                    w_sems.at[k, i],
                )
                for i in range(count)
            ]
            for k in range(STEPS)
        ]
        for copy in first + loads[0] + loads[1]:
            copy.start()
        for low in range(0, columns, columns_here):
            if low % half == 0:
                first[low // half].wait()
            held[low : low + columns_here] = change_of(
                starts_ref, rows_ref, exps[low : low + columns_here], low, columns_here, False
            )

        def send(k):
            return pltpu.make_async_copy(
                ready.at[k % 2], out_ref.at[:, pl.ds(k * block, block)], sems.at[k % 2]
            )

        for k in range(STEPS):
            for copy in loads[k]:
                copy.wait()
            if k + 2 < STEPS:
                for copy in loads[k + 2]:
                    copy.start()
            out = dot(held[...], w[k], ((0,), (0,)))
            if k >= 2:
                send(k - 2).wait()
            ready[k % 2] = out.astype(BF16)
            send(k).start()
        send(STEPS - 2).wait()
        send(STEPS - 1).wait()

    return pl.pallas_call(
        body,
        in_specs=[SMEM, VMEM, ANY, ANY] + [ANY] * count,
        out_specs=ANY,
        out_shape=jax.ShapeDtypeStruct((tokens, features), BF16),
        scratch_shapes=[
            pltpu.VMEM((columns, tokens), BF16),
            pltpu.VMEM((STEPS, columns, block), BF16),
            pltpu.VMEM((columns, tokens), BF16),
            pltpu.VMEM((2, tokens, block), BF16),
            pltpu.SemaphoreType.DMA((2,)),
            pltpu.SemaphoreType.DMA((STEPS, count)),
            pltpu.SemaphoreType.DMA((2,)),
        ],
        compiler_params=PARAMS,
        cost_estimate=cost(
            2 * columns * tokens * features, 2 * features * (columns + tokens) + 2 * columns * tokens
        ),
    )(starts, token_rows, *exps_t, *weights)


def head_block(starts, sides, low, columns_here, features, after):
    tokens = sides[0][2].shape[0]
    block = features // STEPS
    count = len(sides)

    def body(starts_ref, *refs):
        rows_refs, exps_refs, h_refs = refs[0 : 3 * count : 3], refs[1 : 3 * count : 3], refs[2 : 3 * count : 3]
        out_ref, exps, h, held, ready, e_sems, h_sems, sems = refs[3 * count + 1 :]
        first = [
            pltpu.make_async_copy(ref.at[pl.ds(low, columns_here)], exps.at[i], e_sems.at[i])
            for i, ref in enumerate(exps_refs)
        ]
        loads = [
            [
                pltpu.make_async_copy(
                    ref.at[:, pl.ds(k * block, block)], h.at[k, i], h_sems.at[k, i]
                )
                for i, ref in enumerate(h_refs)
            ]
            for k in range(STEPS)
        ]
        for copy in first + loads[0] + loads[1]:
            copy.start()
        for i in range(count):
            first[i].wait()
            held[i] = change_of(starts_ref, rows_refs[i], exps[i], low, columns_here, True)

        def send(k):
            return pltpu.make_async_copy(
                ready.at[k % 2], out_ref.at[:, pl.ds(k * block, block)], sems.at[k % 2]
            )

        for k in range(STEPS):
            if k + 2 < STEPS:
                for copy in loads[k + 2]:
                    copy.start()
            out = None
            for i in range(count):
                loads[k][i].wait()
                part = dot(held[i], h[k, i], ((1,), (0,)))
                out = part if out is None else out + part
            if k >= 2:
                send(k - 2).wait()
            ready[k % 2] = out.astype(BF16)
            send(k).start()
        send(STEPS - 2).wait()
        send(STEPS - 1).wait()

    return pl.pallas_call(
        body,
        in_specs=[SMEM] + [VMEM, ANY, ANY] * count + [ANY],
        out_specs=ANY,
        out_shape=jax.ShapeDtypeStruct((columns_here, features), BF16),
        scratch_shapes=[
            pltpu.VMEM((count, columns_here, tokens), BF16),
            pltpu.VMEM((STEPS, count, tokens, block), BF16),
            pltpu.VMEM((count, columns_here, tokens), BF16),
            pltpu.VMEM((2, columns_here, block), BF16),
            pltpu.SemaphoreType.DMA((count,)),
            pltpu.SemaphoreType.DMA((STEPS, count)),
            pltpu.SemaphoreType.DMA((2,)),
        ],
        compiler_params=PARAMS,
        cost_estimate=cost(
            2 * count * columns_here * tokens * features, 2 * features * (columns_here + count * tokens)
        ),
    )(starts, *(operand for side in sides for operand in side), after)


def cut_features(values, width):
    rows, features = values.shape
    count = features // width

    def body(in_ref, out_ref):
        values = in_ref[...]
        for i in range(count):
            out_ref[i] = values[:, i * width : (i + 1) * width]

    return pl.pallas_call(
        body,
        in_specs=[VMEM],
        out_specs=VMEM,
        out_shape=jax.ShapeDtypeStruct((count, rows, width), values.dtype),
        compiler_params=PARAMS,
        cost_estimate=cost(0, 4 * rows * features),
    )(values)


def pack_facts(token_ids, response_mask, teacher_logprob):
    high = lax.reduce_precision(teacher_logprob, 8, 7)
    rest = teacher_logprob - high
    middle = lax.reduce_precision(rest, 8, 7)
    fields = [
        token_ids // 16384,
        token_ids // 128 % 128,
        token_ids % 128,
        response_mask,
        high,
        middle,
        rest - middle,
        jnp.zeros_like(high),
    ]
    return jnp.stack([field.astype(F32) for field in fields])


def half_shard(side, hidden, facts):
    own_rows, features = hidden.shape
    rows = own_rows // 2

    def body(side_ref, hidden_ref, facts_ref, out_ref, sem):
        first = pl.multiple_of(side_ref[0] * rows, rows)
        copy = pltpu.make_async_copy(
            hidden_ref.at[pl.ds(first, rows)], out_ref.at[:, pl.ds(0, features)], sem
        )
        copy.start()
        facts = facts_ref[...]
        facts = jnp.concatenate([facts, jnp.zeros((LANES - facts.shape[0], own_rows), F32)]).T
        facts = jnp.where(side_ref[0] == 0, facts[:rows], facts[rows:])
        out_ref[:, features:] = facts.astype(BF16)
        copy.wait()

    return pl.pallas_call(
        body,
        in_specs=[SMEM, ANY, VMEM],
        out_specs=VMEM,
        out_shape=jax.ShapeDtypeStruct((rows, features + LANES), BF16),
        scratch_shapes=[pltpu.SemaphoreType.DMA],
        compiler_params=PARAMS,
        cost_estimate=cost(0, 4 * rows * features),
    )(side, hidden, facts)


def add_parts(kept, got, after):
    rows, features = kept.shape
    block = features // 4

    def body(kept_ref, got_ref, _, out_ref):
        out_ref[...] = (kept_ref[...].astype(F32) + got_ref[...].astype(F32)).astype(BF16)

    spec = pl.BlockSpec((rows, block), lambda k: (0, k))
    return pl.pallas_call(
        body,
        grid=(4,),
        in_specs=[spec, spec, ANY],
        out_specs=spec,
        out_shape=jax.ShapeDtypeStruct((rows, features), BF16),
        compiler_params=pltpu.CompilerParams(vmem_limit_bytes=16 << 20),
        cost_estimate=cost(0, 6 * rows * features),
    )(kept, got, after)


def pick_one(values, *places):
    for place in places:
        values = lax.dynamic_index_in_dim(values, place, 0, False)
    return values


def on_device(hidden, weight, token_ids, response_mask, teacher_logprob):
    own_rows, features = hidden.shape
    columns_here = weight.shape[1]
    core, z = lax.axis_index("core"), lax.axis_index("z")
    xh, side, y = lax.axis_index("xh"), lax.axis_index("xl"), lax.axis_index("y")
    rows = own_rows // 2
    here = Z * rows
    lines = here // LANES
    tokens = own_rows * Z * CORES

    own = weight.T
    across = lax.ppermute(own, "xl", SWAP)
    own_other = lax.ppermute(own, "core", SWAP)
    facts = pack_facts(token_ids, response_mask, teacher_logprob)
    gathered = lax.all_gather(
        half_shard(side.astype(jnp.int32).reshape(1), hidden, facts), "z", axis=0, tiled=True
    )
    weights = [own, across, own_other, lax.ppermute(across, "core", SWAP)]
    starts = jnp.stack(
        [
            (((z * CORES + c) * XH + xh) * XL + s) * Y * columns_here + y * columns_here
            for c in (core, 1 - core)
            for s in (side, 1 - side)
        ]
    ).astype(jnp.int32)

    mine, theirs, stats, gathered = logits_and_stats(starts, gathered, weights, columns_here)
    far_gathered = lax.ppermute(gathered, "core", SWAP)
    far_exps = lax.ppermute(theirs, "core", SWAP)
    lined = stats.reshape(8 * lines, LANES)
    shared = merge_stats(broadcast_gather(lined[: 3 * lines], "z", Z), lined, (far_gathered, far_exps))
    shared = broadcast_gather(shared, ("xh", "xl", "y"), PLANE)
    shared = shared.reshape(XH, XL, Y, 5, lines, LANES)
    top = jnp.max(shared[:, :, :, 0], axis=(0, 2))
    shrink = jnp.exp(shared[:, :, :, 0] - top[None, :, None])
    total = jnp.sum(shared[:, :, :, 1] * shrink, axis=(0, 2))
    picked = jnp.sum(shared[:, :, :, 2], axis=(0, 2))
    norms = top + jnp.log(total)
    factor = jnp.exp(stats[0] - pick_one(norms, side).reshape(here))
    token_rows = jnp.stack([stats[5], factor])

    partial = partial_product(starts, token_rows, (mine, theirs), weights, columns_here)
    summed = lax.psum_scatter(partial, "z", scatter_dimension=0, tiled=True)
    cut = features // PLANE
    shares = cut_features(summed, cut)
    summed = lax.all_to_all(shares, ("xh", "xl", "y"), 0, 0, tiled=True)
    summed = summed.reshape(XH, XL, Y, rows, cut).astype(F32)
    summed = jnp.sum(summed, axis=(0, 2)).reshape(own_rows, cut)

    mask, teacher = shared[0, :, 0, 3], shared[0, :, 0, 4]
    ratio = mask * (picked - norms - teacher)
    known = jnp.concatenate([part.reshape(XL, here) for part in (mask, ratio)] + [token_rows])
    known = jnp.stack([known, lax.ppermute(known, "core", SWAP)])
    mask, ratio = (
        part.reshape(CORES, XL, Z, rows) for part in (known[:, :XL], known[:, XL : 2 * XL])
    )
    steps = jnp.arange(rows, dtype=jnp.int32)
    later = (steps[None, :] >= steps[:, None]).astype(F32)
    within = jnp.sum(ratio[..., None, :] * later, axis=-1)
    parts = jnp.sum(ratio, axis=-1).reshape(-1)
    number = jnp.arange(XL * Z, dtype=jnp.int32)
    order = number % Z * (CORES * XL) + number // Z
    order = jnp.concatenate([order + core * XL, order + (1 - core) * XL])
    beyond = jnp.sum(parts[None, :] * (order[None, :] > order[:, None]), axis=1)
    scales = mask * (within + beyond.reshape(CORES, XL, Z, 1)) / float(tokens)

    own_scale = lax.dynamic_index_in_dim(scales[0], z, 1, False).reshape(own_rows)
    hidden_grad = (summed * own_scale[:, None]).astype(BF16)

    scale = lax.dynamic_index_in_dim(scales, side, 1, False).reshape(CORES, 1, here)
    rows_of = jnp.concatenate([known[:, 2 * XL :], scale], axis=1)
    sides = [(rows_of[0], mine, gathered), (rows_of[1], far_exps, far_gathered)]
    given = head_block(starts, sides, columns_here, columns_here, features, partial)
    from_across = lax.ppermute(given, "xl", SWAP)
    kept = head_block(starts, sides, 0, columns_here, features, shares)
    head_grad = add_parts(kept, from_across, hidden_grad)
    return hidden_grad, head_grad.T


def solution(mesh):
    names = ("z", "core", "xh", "xl", "y")
    fine = Mesh(mesh.devices.reshape(Z, CORES, XH, XL, Y), names)
    by_token, by_column = ("z", "core"), P(None, names)
    return jax.shard_map(
        on_device,
        mesh=fine,
        in_specs=(P(by_token, None), by_column, P(by_token), P(by_token), P(by_token)),
        out_specs=(P(by_token, names[2:]), by_column),
        check_vma=False,
    )
```

```python
import jax
import jax.numpy as jnp
from jax import lax
from jax.experimental import pallas as pl
from jax.experimental.pallas import tpu as pltpu
from jax.sharding import Mesh, PartitionSpec as P

F32 = jnp.float32
BF16 = jnp.bfloat16
Z, CORES, XH, XL, Y = 8, 2, 2, 2, 4
PLANE = XH * XL * Y
SWAP = [(0, 1), (1, 0)]
LANES = 128
STEPS = 7
PARAMS = pltpu.CompilerParams(vmem_limit_bytes=56 << 20)
SMEM = pl.BlockSpec(memory_space=pltpu.SMEM)
VMEM = pl.BlockSpec(memory_space=pltpu.VMEM)
ANY = pl.BlockSpec(memory_space=pl.ANY)


def dot(left, right, contract):
    return lax.dot_general(left, right, (contract, ((), ())), preferred_element_type=F32)


def cost(flops, nbytes):
    return pl.CostEstimate(flops=flops, bytes_accessed=nbytes, transcendentals=0)


def matches_of(starts_ref, low, rows, columns_here, ids):
    number = low // columns_here
    row = lax.broadcasted_iota(jnp.int32, (rows, ids.shape[1]), 0) + (low - number * columns_here)
    return row + starts_ref[number] == ids


def as_lines(row):
    return [row[:, at : at + LANES] for at in range(0, row.shape[1], LANES)]


def logits_and_stats(starts, hidden, weights, columns_here):
    features = weights[0].shape[1]
    count = len(weights)
    sizes = [piece.shape[0] for piece in weights]
    offsets = [sum(sizes[:i]) for i in range(count)]
    columns, tokens = sum(sizes), hidden.shape[0]
    block = features // STEPS
    blocks = columns // columns_here

    def body(starts_ref, h_ref, *refs):
        w_refs = refs[:count]
        *exps_refs, stats_ref, copies_ref, lines_ref, _, w, h, f, held, exps, sems, out = refs[count:]

        def loads(k):
            span = pl.ds(k * block, block)
            return [pltpu.make_async_copy(h_ref.at[:, span], h.at[k], sems.at[k, count])] + [
                pltpu.make_async_copy(
                    w_refs[i].at[:, span], w.at[k, pl.ds(offsets[i], sizes[i])], sems.at[k, i]
                )
                for i in range(count)
            ]

        copies = [loads(k) for k in range(STEPS)]
        facts_copy = pltpu.make_async_copy(
            h_ref.at[:, pl.ds(features, LANES)], f, sems.at[STEPS, 0]
        )
        for copy in copies[0] + copies[1] + [facts_copy]:
            copy.start()
        for k in range(STEPS):
            for copy in copies[k]:
                copy.wait()
            if k + 2 < STEPS:
                for copy in copies[k + 2]:
                    copy.start()
            part = dot(w[k], h[k], ((1,), (1,)))
            held[...] = part if k == 0 else held[...] + part
        facts_copy.wait()
        facts = f[...].astype(F32).T
        token_id = facts[0:1] * 16384.0 + facts[1:2] * 128.0 + facts[2:3]
        teacher = facts[4:5] + facts[5:6] + facts[6:7]
        ids = token_id.astype(jnp.int32)
        top = jnp.max(held[...], axis=0, keepdims=True)
        total, picked = jnp.zeros_like(top), jnp.zeros_like(top)
        sends = []
        for i in range(blocks):
            low = i * columns_here
            logits = held[low : low + columns_here]
            grown = jnp.exp(logits - top)
            total += jnp.sum(grown, axis=0, keepdims=True)
            exps[low : low + columns_here] = grown.astype(BF16)
            into = exps_refs[2 * i // blocks].at[pl.ds(low % (columns // 2), columns_here)]
            sends.append(
                pltpu.make_async_copy(exps.at[pl.ds(low, columns_here)], into, out.at[i])
            )
            sends[-1].start()
            match = matches_of(starts_ref, low, columns_here, columns_here, ids)
            picked += jnp.sum(jnp.where(match, logits, 0.0), axis=0, keepdims=True)
        zero = jnp.zeros_like(top)
        stats_ref[...] = jnp.concatenate(
            [top, total, picked, facts[3:4], teacher, token_id, zero, zero]
        )
        lined = jnp.concatenate(as_lines(top) + as_lines(total) + as_lines(picked))
        copies_ref[...] = jnp.broadcast_to(lined[None], copies_ref.shape)
        lines_ref[...] = jnp.concatenate(as_lines(facts[3:4]) + as_lines(teacher))
        for send in sends:
            send.wait()

    return pl.pallas_call(
        body,
        in_specs=[SMEM, ANY] + [ANY] * count,
        out_specs=[ANY, ANY, VMEM, VMEM, VMEM, ANY],
        out_shape=[jax.ShapeDtypeStruct((columns // 2, tokens), BF16)] * 2
        + [
            jax.ShapeDtypeStruct((8, tokens), F32),
            jax.ShapeDtypeStruct((Z, 3 * tokens // LANES, LANES), F32),
            jax.ShapeDtypeStruct((2 * tokens // LANES, LANES), F32),
            jax.ShapeDtypeStruct(hidden.shape, hidden.dtype),
        ],
        input_output_aliases={1: 5},
        scratch_shapes=[
            pltpu.VMEM((STEPS, columns, block), BF16),
            pltpu.VMEM((STEPS, tokens, block), BF16),
            pltpu.VMEM((tokens, LANES), BF16),
            pltpu.VMEM((columns, tokens), F32),
            pltpu.VMEM((columns, tokens), BF16),
            pltpu.SemaphoreType.DMA((STEPS + 1, count + 1)),
            pltpu.SemaphoreType.DMA((blocks,)),
        ],
        compiler_params=PARAMS,
        cost_estimate=cost(
            2 * columns * tokens * features, 2 * features * (columns + tokens) + 2 * columns * tokens
        ),
    )(starts, hidden, *weights)


def merge_stats(parts, own, after):
    lines = parts.shape[1] // 3

    def body(parts_ref, own_ref, _, __, out_ref):
        tops = parts_ref[:, :lines]
        top = jnp.max(tops, axis=0)
        total = jnp.sum(parts_ref[:, lines : 2 * lines] * jnp.exp(tops - top[None]), axis=0)
        picked = jnp.sum(parts_ref[:, 2 * lines :], axis=0)
        merged = jnp.concatenate([top, total, picked, own_ref[...]])
        out_ref[...] = jnp.broadcast_to(merged[None], out_ref.shape)

    return pl.pallas_call(
        body,
        in_specs=[VMEM, VMEM, ANY, ANY],
        out_specs=VMEM,
        out_shape=jax.ShapeDtypeStruct((PLANE, 5 * lines, LANES), F32),
        compiler_params=PARAMS,
        cost_estimate=cost(0, 4 * parts.size),
    )(parts, own, *after)


def change_of(starts_ref, rows_ref, exps, low, columns_here, scaled):
    ids = rows_ref[0:1].astype(jnp.int32)
    match = matches_of(starts_ref, low, exps.shape[0], columns_here, ids)
    change = jnp.where(match, 1.0, 0.0) - exps.astype(F32) * rows_ref[1:2]
    return (change * rows_ref[2:3] if scaled else change).astype(BF16)


def partial_product(starts, token_rows, exps_t, weights, columns_here):
    half, tokens = exps_t[0].shape
    columns = 2 * half
    features = weights[0].shape[1]
    count = len(weights)
    sizes = [piece.shape[0] for piece in weights]
    offsets = [sum(sizes[:i]) for i in range(count)]
    block = features // STEPS

    def body(starts_ref, rows_ref, first_ref, last_ref, *refs):
        w_refs = refs[:count]
        out_ref, exps, w, held, ready, e_sems, w_sems, sems = refs[count:]
        first = [
            pltpu.make_async_copy(ref, exps.at[pl.ds(i * half, half)], e_sems.at[i])
            for i, ref in enumerate((first_ref, last_ref))
        ]
        loads = [
            [
                pltpu.make_async_copy(
                    w_refs[i].at[:, pl.ds(k * block, block)],
                    w.at[k, pl.ds(offsets[i], sizes[i])],
                    w_sems.at[k, i],
                )
                for i in range(count)
            ]
            for k in range(STEPS)
        ]
        for copy in first + loads[0] + loads[1]:
            copy.start()
        for low in range(0, columns, columns_here):
            if low % half == 0:
                first[low // half].wait()
            held[low : low + columns_here] = change_of(
                starts_ref, rows_ref, exps[low : low + columns_here], low, columns_here, False
            )

        def send(k):
            return pltpu.make_async_copy(
                ready.at[k % 2], out_ref.at[:, pl.ds(k * block, block)], sems.at[k % 2]
            )

        for k in range(STEPS):
            for copy in loads[k]:
                copy.wait()
            if k + 2 < STEPS:
                for copy in loads[k + 2]:
                    copy.start()
            out = dot(held[...], w[k], ((0,), (0,)))
            if k >= 2:
                send(k - 2).wait()
            ready[k % 2] = out.astype(BF16)
            send(k).start()
        send(STEPS - 2).wait()
        send(STEPS - 1).wait()

    return pl.pallas_call(
        body,
        in_specs=[SMEM, VMEM, ANY, ANY] + [ANY] * count,
        out_specs=ANY,
        out_shape=jax.ShapeDtypeStruct((tokens, features), BF16),
        scratch_shapes=[
            pltpu.VMEM((columns, tokens), BF16),
            pltpu.VMEM((STEPS, columns, block), BF16),
            pltpu.VMEM((columns, tokens), BF16),
            pltpu.VMEM((2, tokens, block), BF16),
            pltpu.SemaphoreType.DMA((2,)),
            pltpu.SemaphoreType.DMA((STEPS, count)),
            pltpu.SemaphoreType.DMA((2,)),
        ],
        compiler_params=PARAMS,
        cost_estimate=cost(
            2 * columns * tokens * features, 2 * features * (columns + tokens) + 2 * columns * tokens
        ),
    )(starts, token_rows, *exps_t, *weights)


def head_block(starts, sides, low, columns_here, features, after):
    tokens = sides[0][2].shape[0]
    block = features // STEPS
    count = len(sides)

    def body(starts_ref, *refs):
        rows_refs, exps_refs, h_refs = refs[0 : 3 * count : 3], refs[1 : 3 * count : 3], refs[2 : 3 * count : 3]
        out_ref, exps, h, held, ready, e_sems, h_sems, sems = refs[3 * count + 1 :]
        first = [
            pltpu.make_async_copy(ref.at[pl.ds(low, columns_here)], exps.at[i], e_sems.at[i])
            for i, ref in enumerate(exps_refs)
        ]
        loads = [
            [
                pltpu.make_async_copy(
                    ref.at[:, pl.ds(k * block, block)], h.at[k, i], h_sems.at[k, i]
                )
                for i, ref in enumerate(h_refs)
            ]
            for k in range(STEPS)
        ]
        for copy in first + loads[0] + loads[1]:
            copy.start()
        for i in range(count):
            first[i].wait()
            held[i] = change_of(starts_ref, rows_refs[i], exps[i], low, columns_here, True)

        def send(k):
            return pltpu.make_async_copy(
                ready.at[k % 2], out_ref.at[:, pl.ds(k * block, block)], sems.at[k % 2]
            )

        for k in range(STEPS):
            if k + 2 < STEPS:
                for copy in loads[k + 2]:
                    copy.start()
            out = None
            for i in range(count):
                loads[k][i].wait()
                part = dot(held[i], h[k, i], ((1,), (0,)))
                out = part if out is None else out + part
            if k >= 2:
                send(k - 2).wait()
            ready[k % 2] = out.astype(BF16)
            send(k).start()
        send(STEPS - 2).wait()
        send(STEPS - 1).wait()

    return pl.pallas_call(
        body,
        in_specs=[SMEM] + [VMEM, ANY, ANY] * count + [ANY],
        out_specs=ANY,
        out_shape=jax.ShapeDtypeStruct((columns_here, features), BF16),
        scratch_shapes=[
            pltpu.VMEM((count, columns_here, tokens), BF16),
            pltpu.VMEM((STEPS, count, tokens, block), BF16),
            pltpu.VMEM((count, columns_here, tokens), BF16),
            pltpu.VMEM((2, columns_here, block), BF16),
            pltpu.SemaphoreType.DMA((count,)),
            pltpu.SemaphoreType.DMA((STEPS, count)),
            pltpu.SemaphoreType.DMA((2,)),
        ],
        compiler_params=PARAMS,
        cost_estimate=cost(
            2 * count * columns_here * tokens * features, 2 * features * (columns_here + count * tokens)
        ),
    )(starts, *(operand for side in sides for operand in side), after)


def cut_features(values, width):
    rows, features = values.shape
    count = features // width

    def body(in_ref, out_ref):
        values = in_ref[...]
        for i in range(count):
            out_ref[i] = values[:, i * width : (i + 1) * width]

    return pl.pallas_call(
        body,
        in_specs=[VMEM],
        out_specs=VMEM,
        out_shape=jax.ShapeDtypeStruct((count, rows, width), values.dtype),
        compiler_params=PARAMS,
        cost_estimate=cost(0, 4 * rows * features),
    )(values)


def pack_facts(token_ids, response_mask, teacher_logprob):
    high = lax.reduce_precision(teacher_logprob, 8, 7)
    rest = teacher_logprob - high
    middle = lax.reduce_precision(rest, 8, 7)
    fields = [
        token_ids // 16384,
        token_ids // 128 % 128,
        token_ids % 128,
        response_mask,
        high,
        middle,
        rest - middle,
    ]
    fields = jnp.stack([field.astype(F32) for field in fields], axis=1).astype(BF16)
    return jnp.pad(fields, ((0, 0), (0, LANES - fields.shape[1])))


def pick_one(values, *places):
    for place in places:
        values = lax.dynamic_index_in_dim(values, place, 0, False)
    return values


def on_device(hidden, weight, token_ids, response_mask, teacher_logprob):
    own_rows, features = hidden.shape
    columns_here = weight.shape[1]
    core, z = lax.axis_index("core"), lax.axis_index("z")
    xh, side, y = lax.axis_index("xh"), lax.axis_index("xl"), lax.axis_index("y")
    rows = own_rows // 2
    here = Z * rows
    lines = here // LANES
    tokens = own_rows * Z * CORES

    own = weight.T
    across = lax.ppermute(own, "xl", SWAP)
    own_other = lax.ppermute(own, "core", SWAP)
    facts = pack_facts(token_ids, response_mask, teacher_logprob)
    gathered = lax.all_gather(
        lax.dynamic_slice_in_dim(jnp.concatenate([hidden, facts], axis=1), side * rows, rows, 0),
        "z",
        axis=0,
        tiled=True,
    )
    weights = [own, across, own_other, lax.ppermute(across, "core", SWAP)]
    starts = jnp.stack(
        [
            (((z * CORES + c) * XH + xh) * XL + s) * Y * columns_here + y * columns_here
            for c in (core, 1 - core)
            for s in (side, 1 - side)
        ]
    ).astype(jnp.int32)

    mine, theirs, stats, copies, lined, gathered = logits_and_stats(starts, gathered, weights, columns_here)
    far_gathered = lax.ppermute(gathered, "core", SWAP)
    far_exps = lax.ppermute(theirs, "core", SWAP)
    shared = lax.all_to_all(copies, "z", 0, 0, tiled=True)
    shared = merge_stats(shared, lined, (far_gathered, far_exps))
    shared = lax.all_to_all(shared, ("xh", "xl", "y"), 0, 0, tiled=True)
    shared = shared.reshape(XH, XL, Y, 5, lines, LANES)
    top = jnp.max(shared[:, :, :, 0], axis=(0, 2))
    shrink = jnp.exp(shared[:, :, :, 0] - top[None, :, None])
    total = jnp.sum(shared[:, :, :, 1] * shrink, axis=(0, 2))
    picked = jnp.sum(shared[:, :, :, 2], axis=(0, 2))
    norms = top + jnp.log(total)
    factor = jnp.exp(stats[0] - pick_one(norms, side).reshape(here))
    token_rows = jnp.stack([stats[5], factor])

    partial = partial_product(starts, token_rows, (mine, theirs), weights, columns_here)
    summed = lax.psum_scatter(partial, "z", scatter_dimension=0, tiled=True)
    cut = features // PLANE
    shares = cut_features(summed, cut)
    summed = lax.all_to_all(shares, ("xh", "xl", "y"), 0, 0, tiled=True)
    summed = summed.reshape(XH, XL, Y, rows, cut).astype(F32)
    summed = jnp.sum(summed, axis=(0, 2)).reshape(own_rows, cut)

    mask, teacher = shared[0, :, 0, 3], shared[0, :, 0, 4]
    ratio = mask * (picked - norms - teacher)
    known = jnp.concatenate([part.reshape(XL, here) for part in (mask, ratio)] + [token_rows])
    known = jnp.stack([known, lax.ppermute(known, "core", SWAP)])
    mask, ratio = (
        part.reshape(CORES, XL, Z, rows) for part in (known[:, :XL], known[:, XL : 2 * XL])
    )
    steps = jnp.arange(rows, dtype=jnp.int32)
    later = (steps[None, :] >= steps[:, None]).astype(F32)
    within = jnp.sum(ratio[..., None, :] * later, axis=-1)
    parts = jnp.sum(ratio, axis=-1).reshape(-1)
    number = jnp.arange(XL * Z, dtype=jnp.int32)
    order = number % Z * (CORES * XL) + number // Z
    order = jnp.concatenate([order + core * XL, order + (1 - core) * XL])
    beyond = jnp.sum(parts[None, :] * (order[None, :] > order[:, None]), axis=1)
    scales = mask * (within + beyond.reshape(CORES, XL, Z, 1)) / float(tokens)

    own_scale = lax.dynamic_index_in_dim(scales[0], z, 1, False).reshape(own_rows)
    hidden_grad = summed * own_scale[:, None]

    scale = lax.dynamic_index_in_dim(scales, side, 1, False).reshape(CORES, 1, here)
    rows_of = jnp.concatenate([known[:, 2 * XL :], scale], axis=1)
    sides = [(rows_of[0], mine, gathered), (rows_of[1], far_exps, far_gathered)]
    given = head_block(starts, sides, columns_here, columns_here, features, partial)
    from_across = lax.ppermute(given, "xl", SWAP)
    kept = head_block(starts, sides, 0, columns_here, features, shares)
    head_grad = kept.astype(F32) + from_across.astype(F32)
    return hidden_grad.astype(BF16), head_grad.astype(BF16).T


def solution(mesh):
    names = ("z", "core", "xh", "xl", "y")
    fine = Mesh(mesh.devices.reshape(Z, CORES, XH, XL, Y), names)
    by_token, by_column = ("z", "core"), P(None, names)
    return jax.shard_map(
        on_device,
        mesh=fine,
        in_specs=(P(by_token, None), by_column, P(by_token), P(by_token), P(by_token)),
        out_specs=(P(by_token, names[2:]), by_column),
        check_vma=False,
    )
```

```python
import jax
import jax.numpy as jnp
from jax import lax
from jax.experimental import pallas as pl
from jax.experimental.pallas import tpu as pltpu
from jax.sharding import Mesh, PartitionSpec as P

F32 = jnp.float32
BF16 = jnp.bfloat16
Z, CORES, XH, XL, Y = 8, 2, 2, 2, 4
PLANE = XH * XL * Y
SWAP = [(0, 1), (1, 0)]
LANES = 128
STEPS = 7
PARAMS = pltpu.CompilerParams(vmem_limit_bytes=56 << 20)
SMEM = pl.BlockSpec(memory_space=pltpu.SMEM)
VMEM = pl.BlockSpec(memory_space=pltpu.VMEM)
ANY = pl.BlockSpec(memory_space=pl.ANY)


def dot(left, right, contract):
    return lax.dot_general(left, right, (contract, ((), ())), preferred_element_type=F32)


def cost(flops, nbytes):
    return pl.CostEstimate(flops=flops, bytes_accessed=nbytes, transcendentals=0)


def matches_of(starts_ref, low, rows, columns_here, ids):
    number = low // columns_here
    row = lax.broadcasted_iota(jnp.int32, (rows, ids.shape[1]), 0) + (low - number * columns_here)
    return row + starts_ref[number] == ids


def as_lines(row):
    return [row[:, at : at + LANES] for at in range(0, row.shape[1], LANES)]


def logits_and_stats(starts, hidden, weights, columns_here):
    features = weights[0].shape[1]
    count = len(weights)
    sizes = [piece.shape[0] for piece in weights]
    offsets = [sum(sizes[:i]) for i in range(count)]
    columns, tokens = sum(sizes), hidden.shape[0]
    block = features // STEPS
    blocks = columns // columns_here

    def body(starts_ref, h_ref, *refs):
        w_refs = refs[:count]
        *exps_refs, stats_ref, copies_ref, lines_ref, _, w, h, f, held, exps, sems, out = refs[count:]

        def loads(k):
            span = pl.ds(k * block, block)
            return [pltpu.make_async_copy(h_ref.at[:, span], h.at[k], sems.at[k, count])] + [
                pltpu.make_async_copy(
                    w_refs[i].at[:, span], w.at[k, pl.ds(offsets[i], sizes[i])], sems.at[k, i]
                )
                for i in range(count)
            ]

        copies = [loads(k) for k in range(STEPS)]
        facts_copy = pltpu.make_async_copy(
            h_ref.at[:, pl.ds(features, LANES)], f, sems.at[STEPS, 0]
        )
        for copy in copies[0] + copies[1] + [facts_copy]:
            copy.start()
        for k in range(STEPS):
            for copy in copies[k]:
                copy.wait()
            if k + 2 < STEPS:
                for copy in copies[k + 2]:
                    copy.start()
            part = dot(w[k], h[k], ((1,), (1,)))
            held[...] = part if k == 0 else held[...] + part
        facts_copy.wait()
        facts = f[...].astype(F32).T
        token_id = facts[0:1] * 16384.0 + facts[1:2] * 128.0 + facts[2:3]
        teacher = facts[4:5] + facts[5:6] + facts[6:7]
        ids = token_id.astype(jnp.int32)
        top = jnp.max(held[...], axis=0, keepdims=True)
        total, picked = jnp.zeros_like(top), jnp.zeros_like(top)
        sends = []
        for i in range(blocks):
            low = i * columns_here
            logits = held[low : low + columns_here]
            grown = jnp.exp(logits - top)
            total += jnp.sum(grown, axis=0, keepdims=True)
            exps[low : low + columns_here] = grown.astype(BF16)
            into = exps_refs[2 * i // blocks].at[pl.ds(low % (columns // 2), columns_here)]
            sends.append(
                pltpu.make_async_copy(exps.at[pl.ds(low, columns_here)], into, out.at[i])
            )
            sends[-1].start()
            match = matches_of(starts_ref, low, columns_here, columns_here, ids)
            picked += jnp.sum(jnp.where(match, logits, 0.0), axis=0, keepdims=True)
        zero = jnp.zeros_like(top)
        stats_ref[...] = jnp.concatenate(
            [top, total, picked, facts[3:4], teacher, token_id, zero, zero]
        )
        lined = jnp.concatenate(as_lines(top) + as_lines(total) + as_lines(picked))
        copies_ref[...] = jnp.broadcast_to(lined[None], copies_ref.shape)
        lines_ref[...] = jnp.concatenate(as_lines(facts[3:4]) + as_lines(teacher))
        for send in sends:
            send.wait()

    return pl.pallas_call(
        body,
        in_specs=[SMEM, ANY] + [ANY] * count,
        out_specs=[ANY, ANY, VMEM, VMEM, VMEM, ANY],
        out_shape=[jax.ShapeDtypeStruct((columns // 2, tokens), BF16)] * 2
        + [
            jax.ShapeDtypeStruct((8, tokens), F32),
            jax.ShapeDtypeStruct((Z, 3 * tokens // LANES, LANES), F32),
            jax.ShapeDtypeStruct((2 * tokens // LANES, LANES), F32),
            jax.ShapeDtypeStruct(hidden.shape, hidden.dtype),
        ],
        input_output_aliases={1: 5},
        scratch_shapes=[
            pltpu.VMEM((STEPS, columns, block), BF16),
            pltpu.VMEM((STEPS, tokens, block), BF16),
            pltpu.VMEM((tokens, LANES), BF16),
            pltpu.VMEM((columns, tokens), F32),
            pltpu.VMEM((columns, tokens), BF16),
            pltpu.SemaphoreType.DMA((STEPS + 1, count + 1)),
            pltpu.SemaphoreType.DMA((blocks,)),
        ],
        compiler_params=PARAMS,
        cost_estimate=cost(
            2 * columns * tokens * features, 2 * features * (columns + tokens) + 2 * columns * tokens
        ),
    )(starts, hidden, *weights)


def merge_stats(parts, own, after):
    lines = parts.shape[1] // 3

    def body(parts_ref, own_ref, _, __, out_ref):
        tops = parts_ref[:, :lines]
        top = jnp.max(tops, axis=0)
        total = jnp.sum(parts_ref[:, lines : 2 * lines] * jnp.exp(tops - top[None]), axis=0)
        picked = jnp.sum(parts_ref[:, 2 * lines :], axis=0)
        merged = jnp.concatenate([top, total, picked, own_ref[...]])
        out_ref[...] = jnp.broadcast_to(merged[None], out_ref.shape)

    return pl.pallas_call(
        body,
        in_specs=[VMEM, VMEM, ANY, ANY],
        out_specs=VMEM,
        out_shape=jax.ShapeDtypeStruct((PLANE, 5 * lines, LANES), F32),
        compiler_params=pltpu.CompilerParams(vmem_limit_bytes=8 << 20),
        cost_estimate=cost(0, 4 * parts.size),
    )(parts, own, *after)


def change_of(starts_ref, rows_ref, exps, low, columns_here, scaled):
    ids = rows_ref[0:1].astype(jnp.int32)
    match = matches_of(starts_ref, low, exps.shape[0], columns_here, ids)
    change = jnp.where(match, 1.0, 0.0) - exps.astype(F32) * rows_ref[1:2]
    return (change * rows_ref[2:3] if scaled else change).astype(BF16)


def partial_product(starts, token_rows, exps_t, weights, columns_here):
    half, tokens = exps_t[0].shape
    columns = 2 * half
    features = weights[0].shape[1]
    count = len(weights)
    sizes = [piece.shape[0] for piece in weights]
    offsets = [sum(sizes[:i]) for i in range(count)]
    block = features // STEPS

    def body(starts_ref, rows_ref, first_ref, last_ref, *refs):
        w_refs = refs[:count]
        out_ref, exps, w, held, ready, e_sems, w_sems, sems = refs[count:]
        first = [
            pltpu.make_async_copy(ref, exps.at[pl.ds(i * half, half)], e_sems.at[i])
            for i, ref in enumerate((first_ref, last_ref))
        ]
        loads = [
            [
                pltpu.make_async_copy(
                    w_refs[i].at[:, pl.ds(k * block, block)],
                    w.at[k, pl.ds(offsets[i], sizes[i])],
                    w_sems.at[k, i],
                )
                for i in range(count)
            ]
            for k in range(STEPS)
        ]
        for copy in first + loads[0] + loads[1]:
            copy.start()
        for low in range(0, columns, columns_here):
            if low % half == 0:
                first[low // half].wait()
            held[low : low + columns_here] = change_of(
                starts_ref, rows_ref, exps[low : low + columns_here], low, columns_here, False
            )

        def send(k):
            return pltpu.make_async_copy(
                ready.at[k % 2], out_ref.at[:, pl.ds(k * block, block)], sems.at[k % 2]
            )

        for k in range(STEPS):
            for copy in loads[k]:
                copy.wait()
            if k + 2 < STEPS:
                for copy in loads[k + 2]:
                    copy.start()
            out = dot(held[...], w[k], ((0,), (0,)))
            if k >= 2:
                send(k - 2).wait()
            ready[k % 2] = out.astype(BF16)
            send(k).start()
        send(STEPS - 2).wait()
        send(STEPS - 1).wait()

    return pl.pallas_call(
        body,
        in_specs=[SMEM, VMEM, ANY, ANY] + [ANY] * count,
        out_specs=ANY,
        out_shape=jax.ShapeDtypeStruct((tokens, features), BF16),
        scratch_shapes=[
            pltpu.VMEM((columns, tokens), BF16),
            pltpu.VMEM((STEPS, columns, block), BF16),
            pltpu.VMEM((columns, tokens), BF16),
            pltpu.VMEM((2, tokens, block), BF16),
            pltpu.SemaphoreType.DMA((2,)),
            pltpu.SemaphoreType.DMA((STEPS, count)),
            pltpu.SemaphoreType.DMA((2,)),
        ],
        compiler_params=PARAMS,
        cost_estimate=cost(
            2 * columns * tokens * features, 2 * features * (columns + tokens) + 2 * columns * tokens
        ),
    )(starts, token_rows, *exps_t, *weights)


def head_block(starts, sides, low, columns_here, features, after):
    tokens = sides[0][2].shape[0]
    block = features // STEPS
    count = len(sides)

    def body(starts_ref, *refs):
        rows_refs, exps_refs, h_refs = refs[0 : 3 * count : 3], refs[1 : 3 * count : 3], refs[2 : 3 * count : 3]
        out_ref, exps, h, held, ready, e_sems, h_sems, sems = refs[3 * count + 1 :]
        first = [
            pltpu.make_async_copy(ref.at[pl.ds(low, columns_here)], exps.at[i], e_sems.at[i])
            for i, ref in enumerate(exps_refs)
        ]
        loads = [
            [
                pltpu.make_async_copy(
                    ref.at[:, pl.ds(k * block, block)], h.at[k, i], h_sems.at[k, i]
                )
                for i, ref in enumerate(h_refs)
            ]
            for k in range(STEPS)
        ]
        for copy in first + loads[0] + loads[1]:
            copy.start()
        for i in range(count):
            first[i].wait()
            held[i] = change_of(starts_ref, rows_refs[i], exps[i], low, columns_here, True)

        def send(k):
            return pltpu.make_async_copy(
                ready.at[k % 2], out_ref.at[:, pl.ds(k * block, block)], sems.at[k % 2]
            )

        for k in range(STEPS):
            if k + 2 < STEPS:
                for copy in loads[k + 2]:
                    copy.start()
            out = None
            for i in range(count):
                loads[k][i].wait()
                part = dot(held[i], h[k, i], ((1,), (0,)))
                out = part if out is None else out + part
            if k >= 2:
                send(k - 2).wait()
            ready[k % 2] = out.astype(BF16)
            send(k).start()
        send(STEPS - 2).wait()
        send(STEPS - 1).wait()

    return pl.pallas_call(
        body,
        in_specs=[SMEM] + [VMEM, ANY, ANY] * count + [ANY],
        out_specs=ANY,
        out_shape=jax.ShapeDtypeStruct((columns_here, features), BF16),
        scratch_shapes=[
            pltpu.VMEM((count, columns_here, tokens), BF16),
            pltpu.VMEM((STEPS, count, tokens, block), BF16),
            pltpu.VMEM((count, columns_here, tokens), BF16),
            pltpu.VMEM((2, columns_here, block), BF16),
            pltpu.SemaphoreType.DMA((count,)),
            pltpu.SemaphoreType.DMA((STEPS, count)),
            pltpu.SemaphoreType.DMA((2,)),
        ],
        compiler_params=PARAMS,
        cost_estimate=cost(
            2 * count * columns_here * tokens * features, 2 * features * (columns_here + count * tokens)
        ),
    )(starts, *(operand for side in sides for operand in side), after)


def cut_features(values, width):
    rows, features = values.shape
    count = features // width

    def body(in_ref, out_ref):
        values = in_ref[...]
        for i in range(count):
            out_ref[i] = values[:, i * width : (i + 1) * width]

    return pl.pallas_call(
        body,
        in_specs=[VMEM],
        out_specs=VMEM,
        out_shape=jax.ShapeDtypeStruct((count, rows, width), values.dtype),
        compiler_params=PARAMS,
        cost_estimate=cost(0, 4 * rows * features),
    )(values)


def pack_facts(token_ids, response_mask, teacher_logprob):
    high = lax.reduce_precision(teacher_logprob, 8, 7)
    rest = teacher_logprob - high
    middle = lax.reduce_precision(rest, 8, 7)
    fields = [
        token_ids // 16384,
        token_ids // 128 % 128,
        token_ids % 128,
        response_mask,
        high,
        middle,
        rest - middle,
    ]
    fields = jnp.stack([field.astype(F32) for field in fields], axis=1).astype(BF16)
    return jnp.pad(fields, ((0, 0), (0, LANES - fields.shape[1])))


def pick_one(values, *places):
    for place in places:
        values = lax.dynamic_index_in_dim(values, place, 0, False)
    return values


def on_device(hidden, weight, token_ids, response_mask, teacher_logprob):
    own_rows, features = hidden.shape
    columns_here = weight.shape[1]
    core, z = lax.axis_index("core"), lax.axis_index("z")
    xh, side, y = lax.axis_index("xh"), lax.axis_index("xl"), lax.axis_index("y")
    rows = own_rows // 2
    here = Z * rows
    lines = here // LANES
    tokens = own_rows * Z * CORES

    own = weight.T
    across = lax.ppermute(own, "xl", SWAP)
    own_other = lax.ppermute(own, "core", SWAP)
    facts = pack_facts(token_ids, response_mask, teacher_logprob)
    gathered = lax.all_gather(
        lax.dynamic_slice_in_dim(jnp.concatenate([hidden, facts], axis=1), side * rows, rows, 0),
        "z",
        axis=0,
        tiled=True,
    )
    weights = [own, across, own_other, lax.ppermute(across, "core", SWAP)]
    starts = jnp.stack(
        [
            (((z * CORES + c) * XH + xh) * XL + s) * Y * columns_here + y * columns_here
            for c in (core, 1 - core)
            for s in (side, 1 - side)
        ]
    ).astype(jnp.int32)

    mine, theirs, stats, copies, lined, gathered = logits_and_stats(starts, gathered, weights, columns_here)
    far_gathered = lax.ppermute(gathered, "core", SWAP)
    far_exps = lax.ppermute(theirs, "core", SWAP)
    shared = lax.all_to_all(copies, "z", 0, 0, tiled=True)
    shared = merge_stats(shared, lined, (far_gathered, far_exps))
    shared = lax.all_to_all(shared, ("xh", "xl", "y"), 0, 0, tiled=True)
    shared = shared.reshape(XH, XL, Y, 5, lines, LANES)
    top = jnp.max(shared[:, :, :, 0], axis=(0, 2))
    shrink = jnp.exp(shared[:, :, :, 0] - top[None, :, None])
    total = jnp.sum(shared[:, :, :, 1] * shrink, axis=(0, 2))
    picked = jnp.sum(shared[:, :, :, 2], axis=(0, 2))
    norms = top + jnp.log(total)
    factor = jnp.exp(stats[0] - pick_one(norms, side).reshape(here))
    token_rows = jnp.stack([stats[5], factor])

    partial = partial_product(starts, token_rows, (mine, theirs), weights, columns_here)
    summed = lax.psum_scatter(partial, "z", scatter_dimension=0, tiled=True)
    cut = features // PLANE
    shares = cut_features(summed, cut)
    summed = lax.all_to_all(shares, ("xh", "xl", "y"), 0, 0, tiled=True)
    summed = summed.reshape(XH, XL, Y, rows, cut).astype(F32)
    summed = jnp.sum(summed, axis=(0, 2)).reshape(own_rows, cut)

    mask, teacher = shared[0, :, 0, 3], shared[0, :, 0, 4]
    ratio = mask * (picked - norms - teacher)
    known = jnp.concatenate([part.reshape(XL, here) for part in (mask, ratio)] + [token_rows])
    known = jnp.stack([known, lax.ppermute(known, "core", SWAP)])
    mask, ratio = (
        part.reshape(CORES, XL, Z, rows) for part in (known[:, :XL], known[:, XL : 2 * XL])
    )
    steps = jnp.arange(rows, dtype=jnp.int32)
    later = (steps[None, :] >= steps[:, None]).astype(F32)
    within = jnp.sum(ratio[..., None, :] * later, axis=-1)
    parts = jnp.sum(ratio, axis=-1).reshape(-1)
    number = jnp.arange(XL * Z, dtype=jnp.int32)
    order = number % Z * (CORES * XL) + number // Z
    order = jnp.concatenate([order + core * XL, order + (1 - core) * XL])
    beyond = jnp.sum(parts[None, :] * (order[None, :] > order[:, None]), axis=1)
    scales = mask * (within + beyond.reshape(CORES, XL, Z, 1)) / float(tokens)

    own_scale = lax.dynamic_index_in_dim(scales[0], z, 1, False).reshape(own_rows)
    hidden_grad = summed * own_scale[:, None]

    scale = lax.dynamic_index_in_dim(scales, side, 1, False).reshape(CORES, 1, here)
    rows_of = jnp.concatenate([known[:, 2 * XL :], scale], axis=1)
    sides = [(rows_of[0], mine, gathered), (rows_of[1], far_exps, far_gathered)]
    given = head_block(starts, sides, columns_here, columns_here, features, partial)
    from_across = lax.ppermute(given, "xl", SWAP)
    kept = head_block(starts, sides, 0, columns_here, features, shares)
    head_grad = kept.astype(F32) + from_across.astype(F32)
    return hidden_grad.astype(BF16), head_grad.astype(BF16).T


def solution(mesh):
    names = ("z", "core", "xh", "xl", "y")
    fine = Mesh(mesh.devices.reshape(Z, CORES, XH, XL, Y), names)
    by_token, by_column = ("z", "core"), P(None, names)
    return jax.shard_map(
        on_device,
        mesh=fine,
        in_specs=(P(by_token, None), by_column, P(by_token), P(by_token), P(by_token)),
        out_specs=(P(by_token, names[2:]), by_column),
        check_vma=False,
    )
```

```python
import jax
import jax.numpy as jnp
from jax import lax
from jax.experimental import pallas as pl
from jax.experimental.pallas import tpu as pltpu
from jax.sharding import Mesh, PartitionSpec as P

F32 = jnp.float32
BF16 = jnp.bfloat16
Z, CORES, XH, XL, Y = 8, 2, 2, 2, 4
PLANE = XH * XL * Y
SWAP = [(0, 1), (1, 0)]
LANES = 128
STEPS = 7
AHEAD = 3
PARAMS = pltpu.CompilerParams(vmem_limit_bytes=56 << 20)
SMEM = pl.BlockSpec(memory_space=pltpu.SMEM)
VMEM = pl.BlockSpec(memory_space=pltpu.VMEM)
ANY = pl.BlockSpec(memory_space=pl.ANY)


def dot(left, right, contract):
    return lax.dot_general(left, right, (contract, ((), ())), preferred_element_type=F32)


def cost(flops, nbytes):
    return pl.CostEstimate(flops=flops, bytes_accessed=nbytes, transcendentals=0)


def matches_of(starts_ref, low, rows, columns_here, ids):
    number = low // columns_here
    row = lax.broadcasted_iota(jnp.int32, (rows, ids.shape[1]), 0) + (low - number * columns_here)
    return row + starts_ref[number] == ids


def as_lines(row):
    return [row[:, at : at + LANES] for at in range(0, row.shape[1], LANES)]


def logits_and_stats(starts, hidden, weights, columns_here):
    features = weights[0].shape[1]
    count = len(weights)
    sizes = [piece.shape[0] for piece in weights]
    offsets = [sum(sizes[:i]) for i in range(count)]
    columns, tokens = sum(sizes), hidden.shape[0]
    block = features // STEPS
    blocks = columns // columns_here

    def body(starts_ref, h_ref, *refs):
        w_refs = refs[:count]
        *exps_refs, stats_ref, copies_ref, lines_ref, _, w, h, f, held, exps, sems, out = refs[count:]

        def loads(k):
            span = pl.ds(k * block, block)
            return [pltpu.make_async_copy(h_ref.at[:, span], h.at[k], sems.at[k, count])] + [
                pltpu.make_async_copy(
                    w_refs[i].at[:, span], w.at[k, pl.ds(offsets[i], sizes[i])], sems.at[k, i]
                )
                for i in range(count)
            ]

        copies = [loads(k) for k in range(STEPS)]
        facts_copy = pltpu.make_async_copy(
            h_ref.at[:, pl.ds(features, LANES)], f, sems.at[STEPS, 0]
        )
        for copy in sum(copies[:AHEAD], []) + [facts_copy]:
            copy.start()
        for k in range(STEPS):
            for copy in copies[k]:
                copy.wait()
            if k + AHEAD < STEPS:
                for copy in copies[k + AHEAD]:
                    copy.start()
            part = dot(w[k], h[k], ((1,), (1,)))
            held[...] = part if k == 0 else held[...] + part
        facts_copy.wait()
        facts = f[...].astype(F32).T
        token_id = facts[0:1] * 16384.0 + facts[1:2] * 128.0 + facts[2:3]
        teacher = facts[4:5] + facts[5:6] + facts[6:7]
        ids = token_id.astype(jnp.int32)
        top = jnp.max(held[...], axis=0, keepdims=True)
        total, picked = jnp.zeros_like(top), jnp.zeros_like(top)
        sends = []
        for i in range(blocks):
            low = i * columns_here
            logits = held[low : low + columns_here]
            grown = jnp.exp(logits - top)
            total += jnp.sum(grown, axis=0, keepdims=True)
            exps[low : low + columns_here] = grown.astype(BF16)
            into = exps_refs[2 * i // blocks].at[pl.ds(low % (columns // 2), columns_here)]
            sends.append(
                pltpu.make_async_copy(exps.at[pl.ds(low, columns_here)], into, out.at[i])
            )
            sends[-1].start()
            match = matches_of(starts_ref, low, columns_here, columns_here, ids)
            picked += jnp.sum(jnp.where(match, logits, 0.0), axis=0, keepdims=True)
        zero = jnp.zeros_like(top)
        stats_ref[...] = jnp.concatenate(
            [top, total, picked, facts[3:4], teacher, token_id, zero, zero]
        )
        lined = jnp.concatenate(as_lines(top) + as_lines(total) + as_lines(picked))
        copies_ref[...] = jnp.broadcast_to(lined[None], copies_ref.shape)
        lines_ref[...] = jnp.concatenate(as_lines(facts[3:4]) + as_lines(teacher))
        for send in sends:
            send.wait()

    return pl.pallas_call(
        body,
        in_specs=[SMEM, ANY] + [ANY] * count,
        out_specs=[ANY, ANY, VMEM, VMEM, VMEM, ANY],
        out_shape=[jax.ShapeDtypeStruct((columns // 2, tokens), BF16)] * 2
        + [
            jax.ShapeDtypeStruct((8, tokens), F32),
            jax.ShapeDtypeStruct((Z, 3 * tokens // LANES, LANES), F32),
            jax.ShapeDtypeStruct((2 * tokens // LANES, LANES), F32),
            jax.ShapeDtypeStruct(hidden.shape, hidden.dtype),
        ],
        input_output_aliases={1: 5},
        scratch_shapes=[
            pltpu.VMEM((STEPS, columns, block), BF16),
            pltpu.VMEM((STEPS, tokens, block), BF16),
            pltpu.VMEM((tokens, LANES), BF16),
            pltpu.VMEM((columns, tokens), F32),
            pltpu.VMEM((columns, tokens), BF16),
            pltpu.SemaphoreType.DMA((STEPS + 1, count + 1)),
            pltpu.SemaphoreType.DMA((blocks,)),
        ],
        compiler_params=PARAMS,
        cost_estimate=cost(
            2 * columns * tokens * features, 2 * features * (columns + tokens) + 2 * columns * tokens
        ),
    )(starts, hidden, *weights)


def merge_stats(parts, own, after):
    lines = parts.shape[1] // 3

    def body(parts_ref, own_ref, _, __, out_ref):
        tops = parts_ref[:, :lines]
        top = jnp.max(tops, axis=0)
        total = jnp.sum(parts_ref[:, lines : 2 * lines] * jnp.exp(tops - top[None]), axis=0)
        picked = jnp.sum(parts_ref[:, 2 * lines :], axis=0)
        merged = jnp.concatenate([top, total, picked, own_ref[...]])
        out_ref[...] = jnp.broadcast_to(merged[None], out_ref.shape)

    return pl.pallas_call(
        body,
        in_specs=[VMEM, VMEM, ANY, ANY],
        out_specs=VMEM,
        out_shape=jax.ShapeDtypeStruct((PLANE, 5 * lines, LANES), F32),
        compiler_params=pltpu.CompilerParams(vmem_limit_bytes=8 << 20),
        cost_estimate=cost(0, 4 * parts.size),
    )(parts, own, *after)


def change_of(starts_ref, rows_ref, exps, low, columns_here, scaled):
    ids = rows_ref[0:1].astype(jnp.int32)
    match = matches_of(starts_ref, low, exps.shape[0], columns_here, ids)
    change = jnp.where(match, 1.0, 0.0) - exps.astype(F32) * rows_ref[1:2]
    return (change * rows_ref[2:3] if scaled else change).astype(BF16)


def partial_product(starts, token_rows, exps_t, weights, columns_here):
    half, tokens = exps_t[0].shape
    columns = 2 * half
    features = weights[0].shape[1]
    count = len(weights)
    sizes = [piece.shape[0] for piece in weights]
    offsets = [sum(sizes[:i]) for i in range(count)]
    block = features // STEPS

    def body(starts_ref, rows_ref, first_ref, last_ref, *refs):
        w_refs = refs[:count]
        out_ref, exps, w, held, ready, e_sems, w_sems, sems = refs[count:]
        first = [
            pltpu.make_async_copy(ref, exps.at[pl.ds(i * half, half)], e_sems.at[i])
            for i, ref in enumerate((first_ref, last_ref))
        ]
        loads = [
            [
                pltpu.make_async_copy(
                    w_refs[i].at[:, pl.ds(k * block, block)],
                    w.at[k, pl.ds(offsets[i], sizes[i])],
                    w_sems.at[k, i],
                )
                for i in range(count)
            ]
            for k in range(STEPS)
        ]
        for copy in first + sum(loads[:AHEAD], []):
            copy.start()
        for low in range(0, columns, columns_here):
            if low % half == 0:
                first[low // half].wait()
            held[low : low + columns_here] = change_of(
                starts_ref, rows_ref, exps[low : low + columns_here], low, columns_here, False
            )

        def send(k):
            return pltpu.make_async_copy(
                ready.at[k % 2], out_ref.at[:, pl.ds(k * block, block)], sems.at[k % 2]
            )

        for k in range(STEPS):
            for copy in loads[k]:
                copy.wait()
            if k + AHEAD < STEPS:
                for copy in loads[k + AHEAD]:
                    copy.start()
            out = dot(held[...], w[k], ((0,), (0,)))
            if k >= 2:
                send(k - 2).wait()
            ready[k % 2] = out.astype(BF16)
            send(k).start()
        send(STEPS - 2).wait()
        send(STEPS - 1).wait()

    return pl.pallas_call(
        body,
        in_specs=[SMEM, VMEM, ANY, ANY] + [ANY] * count,
        out_specs=ANY,
        out_shape=jax.ShapeDtypeStruct((tokens, features), BF16),
        scratch_shapes=[
            pltpu.VMEM((columns, tokens), BF16),
            pltpu.VMEM((STEPS, columns, block), BF16),
            pltpu.VMEM((columns, tokens), BF16),
            pltpu.VMEM((2, tokens, block), BF16),
            pltpu.SemaphoreType.DMA((2,)),
            pltpu.SemaphoreType.DMA((STEPS, count)),
            pltpu.SemaphoreType.DMA((2,)),
        ],
        compiler_params=PARAMS,
        cost_estimate=cost(
            2 * columns * tokens * features, 2 * features * (columns + tokens) + 2 * columns * tokens
        ),
    )(starts, token_rows, *exps_t, *weights)


def head_block(starts, sides, low, columns_here, features, after):
    tokens = sides[0][2].shape[0]
    block = features // STEPS
    count = len(sides)

    def body(starts_ref, *refs):
        rows_refs, exps_refs, h_refs = refs[0 : 3 * count : 3], refs[1 : 3 * count : 3], refs[2 : 3 * count : 3]
        out_ref, exps, h, held, ready, e_sems, h_sems, sems = refs[3 * count + 1 :]
        first = [
            pltpu.make_async_copy(ref.at[pl.ds(low, columns_here)], exps.at[i], e_sems.at[i])
            for i, ref in enumerate(exps_refs)
        ]
        loads = [
            [
                pltpu.make_async_copy(
                    ref.at[:, pl.ds(k * block, block)], h.at[k, i], h_sems.at[k, i]
                )
                for i, ref in enumerate(h_refs)
            ]
            for k in range(STEPS)
        ]
        for copy in first + sum(loads[:AHEAD], []):
            copy.start()
        for i in range(count):
            first[i].wait()
            held[i] = change_of(starts_ref, rows_refs[i], exps[i], low, columns_here, True)

        def send(k):
            return pltpu.make_async_copy(
                ready.at[k % 2], out_ref.at[:, pl.ds(k * block, block)], sems.at[k % 2]
            )

        for k in range(STEPS):
            if k + AHEAD < STEPS:
                for copy in loads[k + AHEAD]:
                    copy.start()
            out = None
            for i in range(count):
                loads[k][i].wait()
                part = dot(held[i], h[k, i], ((1,), (0,)))
                out = part if out is None else out + part
            if k >= 2:
                send(k - 2).wait()
            ready[k % 2] = out.astype(BF16)
            send(k).start()
        send(STEPS - 2).wait()
        send(STEPS - 1).wait()

    return pl.pallas_call(
        body,
        in_specs=[SMEM] + [VMEM, ANY, ANY] * count + [ANY],
        out_specs=ANY,
        out_shape=jax.ShapeDtypeStruct((columns_here, features), BF16),
        scratch_shapes=[
            pltpu.VMEM((count, columns_here, tokens), BF16),
            pltpu.VMEM((STEPS, count, tokens, block), BF16),
            pltpu.VMEM((count, columns_here, tokens), BF16),
            pltpu.VMEM((2, columns_here, block), BF16),
            pltpu.SemaphoreType.DMA((count,)),
            pltpu.SemaphoreType.DMA((STEPS, count)),
            pltpu.SemaphoreType.DMA((2,)),
        ],
        compiler_params=PARAMS,
        cost_estimate=cost(
            2 * count * columns_here * tokens * features, 2 * features * (columns_here + count * tokens)
        ),
    )(starts, *(operand for side in sides for operand in side), after)


def cut_features(values, width):
    rows, features = values.shape
    count = features // width

    def body(in_ref, out_ref):
        values = in_ref[...]
        for i in range(count):
            out_ref[i] = values[:, i * width : (i + 1) * width]

    return pl.pallas_call(
        body,
        in_specs=[VMEM],
        out_specs=VMEM,
        out_shape=jax.ShapeDtypeStruct((count, rows, width), values.dtype),
        compiler_params=PARAMS,
        cost_estimate=cost(0, 4 * rows * features),
    )(values)


def pack_facts(token_ids, response_mask, teacher_logprob):
    high = lax.reduce_precision(teacher_logprob, 8, 7)
    rest = teacher_logprob - high
    middle = lax.reduce_precision(rest, 8, 7)
    fields = [
        token_ids // 16384,
        token_ids // 128 % 128,
        token_ids % 128,
        response_mask,
        high,
        middle,
        rest - middle,
    ]
    fields = jnp.stack([field.astype(F32) for field in fields], axis=1).astype(BF16)
    return jnp.pad(fields, ((0, 0), (0, LANES - fields.shape[1])))


def pick_one(values, *places):
    for place in places:
        values = lax.dynamic_index_in_dim(values, place, 0, False)
    return values


def on_device(hidden, weight, token_ids, response_mask, teacher_logprob):
    own_rows, features = hidden.shape
    columns_here = weight.shape[1]
    core, z = lax.axis_index("core"), lax.axis_index("z")
    xh, side, y = lax.axis_index("xh"), lax.axis_index("xl"), lax.axis_index("y")
    rows = own_rows // 2
    here = Z * rows
    lines = here // LANES
    tokens = own_rows * Z * CORES

    own = weight.T
    across = lax.ppermute(own, "xl", SWAP)
    own_other = lax.ppermute(own, "core", SWAP)
    facts = pack_facts(token_ids, response_mask, teacher_logprob)
    gathered = lax.all_gather(
        lax.dynamic_slice_in_dim(jnp.concatenate([hidden, facts], axis=1), side * rows, rows, 0),
        "z",
        axis=0,
        tiled=True,
    )
    weights = [own, across, own_other, lax.ppermute(across, "core", SWAP)]
    starts = jnp.stack(
        [
            (((z * CORES + c) * XH + xh) * XL + s) * Y * columns_here + y * columns_here
            for c in (core, 1 - core)
            for s in (side, 1 - side)
        ]
    ).astype(jnp.int32)

    mine, theirs, stats, copies, lined, gathered = logits_and_stats(starts, gathered, weights, columns_here)
    far_gathered = lax.ppermute(gathered, "core", SWAP)
    far_exps = lax.ppermute(theirs, "core", SWAP)
    shared = lax.all_to_all(copies, "z", 0, 0, tiled=True)
    shared = merge_stats(shared, lined, (far_gathered, far_exps))
    shared = lax.all_to_all(shared, ("xh", "xl", "y"), 0, 0, tiled=True)
    shared = shared.reshape(XH, XL, Y, 5, lines, LANES)
    top = jnp.max(shared[:, :, :, 0], axis=(0, 2))
    shrink = jnp.exp(shared[:, :, :, 0] - top[None, :, None])
    total = jnp.sum(shared[:, :, :, 1] * shrink, axis=(0, 2))
    picked = jnp.sum(shared[:, :, :, 2], axis=(0, 2))
    norms = top + jnp.log(total)
    factor = jnp.exp(stats[0] - pick_one(norms, side).reshape(here))
    token_rows = jnp.stack([stats[5], factor])

    partial = partial_product(starts, token_rows, (mine, theirs), weights, columns_here)
    summed = lax.psum_scatter(partial, "z", scatter_dimension=0, tiled=True)
    cut = features // PLANE
    shares = cut_features(summed, cut)
    summed = lax.all_to_all(shares, ("xh", "xl", "y"), 0, 0, tiled=True)
    summed = summed.reshape(XH, XL, Y, rows, cut).astype(F32)
    summed = jnp.sum(summed, axis=(0, 2)).reshape(own_rows, cut)

    mask, teacher = shared[0, :, 0, 3], shared[0, :, 0, 4]
    ratio = mask * (picked - norms - teacher)
    known = jnp.concatenate([part.reshape(XL, here) for part in (mask, ratio)] + [token_rows])
    known = jnp.stack([known, lax.ppermute(known, "core", SWAP)])
    mask, ratio = (
        part.reshape(CORES, XL, Z, rows) for part in (known[:, :XL], known[:, XL : 2 * XL])
    )
    steps = jnp.arange(rows, dtype=jnp.int32)
    later = (steps[None, :] >= steps[:, None]).astype(F32)
    within = jnp.sum(ratio[..., None, :] * later, axis=-1)
    parts = jnp.sum(ratio, axis=-1).reshape(-1)
    number = jnp.arange(XL * Z, dtype=jnp.int32)
    order = number % Z * (CORES * XL) + number // Z
    order = jnp.concatenate([order + core * XL, order + (1 - core) * XL])
    beyond = jnp.sum(parts[None, :] * (order[None, :] > order[:, None]), axis=1)
    scales = mask * (within + beyond.reshape(CORES, XL, Z, 1)) / float(tokens)

    own_scale = lax.dynamic_index_in_dim(scales[0], z, 1, False).reshape(own_rows)
    hidden_grad = summed * own_scale[:, None]

    scale = lax.dynamic_index_in_dim(scales, side, 1, False).reshape(CORES, 1, here)
    rows_of = jnp.concatenate([known[:, 2 * XL :], scale], axis=1)
    sides = [(rows_of[0], mine, gathered), (rows_of[1], far_exps, far_gathered)]
    given = head_block(starts, sides, columns_here, columns_here, features, partial)
    from_across = lax.ppermute(given, "xl", SWAP)
    kept = head_block(starts, sides, 0, columns_here, features, shares)
    head_grad = kept.astype(F32) + from_across.astype(F32)
    return hidden_grad.astype(BF16), head_grad.astype(BF16).T


def solution(mesh):
    names = ("z", "core", "xh", "xl", "y")
    fine = Mesh(mesh.devices.reshape(Z, CORES, XH, XL, Y), names)
    by_token, by_column = ("z", "core"), P(None, names)
    return jax.shard_map(
        on_device,
        mesh=fine,
        in_specs=(P(by_token, None), by_column, P(by_token), P(by_token), P(by_token)),
        out_specs=(P(by_token, names[2:]), by_column),
        check_vma=False,
    )
```

```python
import jax
import jax.numpy as jnp
from jax import lax
from jax.experimental import pallas as pl
from jax.experimental.pallas import tpu as pltpu
from jax.sharding import Mesh, PartitionSpec as P

F32 = jnp.float32
BF16 = jnp.bfloat16
Z, CORES, XH, XL, Y = 8, 2, 2, 2, 4
PLANE = XH * XL * Y
SWAP = [(0, 1), (1, 0)]
LANES = 128
STEPS = 7
PARAMS = pltpu.CompilerParams(vmem_limit_bytes=56 << 20)
SMEM = pl.BlockSpec(memory_space=pltpu.SMEM)
VMEM = pl.BlockSpec(memory_space=pltpu.VMEM)
ANY = pl.BlockSpec(memory_space=pl.ANY)


def dot(left, right, contract):
    return lax.dot_general(left, right, (contract, ((), ())), preferred_element_type=F32)


def cost(flops, nbytes):
    return pl.CostEstimate(flops=flops, bytes_accessed=nbytes, transcendentals=0)


def matches_of(starts_ref, low, rows, columns_here, ids):
    number = low // columns_here
    row = lax.broadcasted_iota(jnp.int32, (rows, ids.shape[1]), 0) + (low - number * columns_here)
    return row + starts_ref[number] == ids


def as_lines(row):
    return [row[:, at : at + LANES] for at in range(0, row.shape[1], LANES)]


def logits_and_stats(starts, hidden, weights, columns_here):
    features = weights[0].shape[1]
    count = len(weights)
    sizes = [piece.shape[0] for piece in weights]
    offsets = [sum(sizes[:i]) for i in range(count)]
    columns, tokens = sum(sizes), hidden.shape[0]
    block = features // STEPS
    blocks = columns // columns_here

    def body(starts_ref, h_ref, *refs):
        w_refs = refs[:count]
        *exps_refs, stats_ref, copies_ref, lines_ref, _, w, h, f, held, exps, sems, out = refs[count:]

        def loads(k):
            span = pl.ds(k * block, block)
            return [pltpu.make_async_copy(h_ref.at[:, span], h.at[k], sems.at[k, count])] + [
                pltpu.make_async_copy(
                    w_refs[i].at[:, span], w.at[k, pl.ds(offsets[i], sizes[i])], sems.at[k, i]
                )
                for i in range(count)
            ]

        copies = [loads(k) for k in range(STEPS)]
        facts_copy = pltpu.make_async_copy(
            h_ref.at[:, pl.ds(features, LANES)], f, sems.at[STEPS, 0]
        )
        for copy in copies[0] + copies[1] + [facts_copy]:
            copy.start()
        for k in range(STEPS):
            for copy in copies[k]:
                copy.wait()
            if k + 2 < STEPS:
                for copy in copies[k + 2]:
                    copy.start()
            part = dot(w[k], h[k], ((1,), (1,)))
            held[...] = part if k == 0 else held[...] + part
        facts_copy.wait()
        facts = f[...].astype(F32).T
        token_id = facts[0:1] * 16384.0 + facts[1:2] * 128.0 + facts[2:3]
        teacher = facts[4:5] + facts[5:6] + facts[6:7]
        ids = token_id.astype(jnp.int32)
        top = jnp.max(held[...], axis=0, keepdims=True)
        total, picked = jnp.zeros_like(top), jnp.zeros_like(top)
        sends = []
        for i in range(blocks):
            low = i * columns_here
            logits = held[low : low + columns_here]
            grown = jnp.exp(logits - top)
            total += jnp.sum(grown, axis=0, keepdims=True)
            exps[low : low + columns_here] = grown.astype(BF16)
            into = exps_refs[2 * i // blocks].at[pl.ds(low % (columns // 2), columns_here)]
            sends.append(
                pltpu.make_async_copy(exps.at[pl.ds(low, columns_here)], into, out.at[i])
            )
            sends[-1].start()
            match = matches_of(starts_ref, low, columns_here, columns_here, ids)
            picked += jnp.sum(jnp.where(match, logits, 0.0), axis=0, keepdims=True)
        zero = jnp.zeros_like(top)
        stats_ref[...] = jnp.concatenate(
            [top, total, picked, facts[3:4], teacher, token_id, zero, zero]
        )
        lined = jnp.concatenate(as_lines(top) + as_lines(total) + as_lines(picked))
        copies_ref[...] = jnp.broadcast_to(lined[None], copies_ref.shape)
        lines_ref[...] = jnp.concatenate(as_lines(facts[3:4]) + as_lines(teacher))
        for send in sends:
            send.wait()

    return pl.pallas_call(
        body,
        in_specs=[SMEM, ANY] + [ANY] * count,
        out_specs=[ANY, ANY, VMEM, VMEM, VMEM, ANY],
        out_shape=[jax.ShapeDtypeStruct((columns // 2, tokens), BF16)] * 2
        + [
            jax.ShapeDtypeStruct((8, tokens), F32),
            jax.ShapeDtypeStruct((Z, 3 * tokens // LANES, LANES), F32),
            jax.ShapeDtypeStruct((2 * tokens // LANES, LANES), F32),
            jax.ShapeDtypeStruct(hidden.shape, hidden.dtype),
        ],
        input_output_aliases={1: 5},
        scratch_shapes=[
            pltpu.VMEM((STEPS, columns, block), BF16),
            pltpu.VMEM((STEPS, tokens, block), BF16),
            pltpu.VMEM((tokens, LANES), BF16),
            pltpu.VMEM((columns, tokens), F32),
            pltpu.VMEM((columns, tokens), BF16),
            pltpu.SemaphoreType.DMA((STEPS + 1, count + 1)),
            pltpu.SemaphoreType.DMA((blocks,)),
        ],
        compiler_params=PARAMS,
        cost_estimate=cost(
            2 * columns * tokens * features, 2 * features * (columns + tokens) + 2 * columns * tokens
        ),
    )(starts, hidden, *weights)


def merge_stats(parts, own, after):
    lines = parts.shape[1] // 3

    def body(parts_ref, own_ref, _, __, out_ref):
        tops = parts_ref[:, :lines]
        top = jnp.max(tops, axis=0)
        total = jnp.sum(parts_ref[:, lines : 2 * lines] * jnp.exp(tops - top[None]), axis=0)
        picked = jnp.sum(parts_ref[:, 2 * lines :], axis=0)
        merged = jnp.concatenate([top, total, picked])
        out_ref[...] = jnp.broadcast_to(merged[None], out_ref.shape)

    return pl.pallas_call(
        body,
        in_specs=[VMEM, VMEM, ANY, ANY],
        out_specs=VMEM,
        out_shape=jax.ShapeDtypeStruct((XH * Y, 3 * lines, LANES), F32),
        compiler_params=pltpu.CompilerParams(vmem_limit_bytes=8 << 20),
        cost_estimate=cost(0, 4 * parts.size),
    )(parts, own, *after)


def change_of(starts_ref, rows_ref, exps, low, columns_here, scaled):
    ids = rows_ref[0:1].astype(jnp.int32)
    match = matches_of(starts_ref, low, exps.shape[0], columns_here, ids)
    change = jnp.where(match, 1.0, 0.0) - exps.astype(F32) * rows_ref[1:2]
    return (change * rows_ref[2:3] if scaled else change).astype(BF16)


def partial_product(starts, token_rows, exps_t, weights, columns_here):
    half, tokens = exps_t[0].shape
    columns = 2 * half
    features = weights[0].shape[1]
    count = len(weights)
    sizes = [piece.shape[0] for piece in weights]
    offsets = [sum(sizes[:i]) for i in range(count)]
    block = features // STEPS

    def body(starts_ref, rows_ref, first_ref, last_ref, *refs):
        w_refs = refs[:count]
        out_ref, exps, w, held, ready, e_sems, w_sems, sems = refs[count:]
        first = [
            pltpu.make_async_copy(ref, exps.at[pl.ds(i * half, half)], e_sems.at[i])
            for i, ref in enumerate((first_ref, last_ref))
        ]
        loads = [
            [
                pltpu.make_async_copy(
                    w_refs[i].at[:, pl.ds(k * block, block)],
                    w.at[k, pl.ds(offsets[i], sizes[i])],
                    w_sems.at[k, i],
                )
                for i in range(count)
            ]
            for k in range(STEPS)
        ]
        for copy in first + loads[0] + loads[1]:
            copy.start()
        for low in range(0, columns, columns_here):
            if low % half == 0:
                first[low // half].wait()
            held[low : low + columns_here] = change_of(
                starts_ref, rows_ref, exps[low : low + columns_here], low, columns_here, False
            )

        def send(k):
            return pltpu.make_async_copy(
                ready.at[k % 2], out_ref.at[:, pl.ds(k * block, block)], sems.at[k % 2]
            )

        for k in range(STEPS):
            for copy in loads[k]:
                copy.wait()
            if k + 2 < STEPS:
                for copy in loads[k + 2]:
                    copy.start()
            out = dot(held[...], w[k], ((0,), (0,)))
            if k >= 2:
                send(k - 2).wait()
            ready[k % 2] = out.astype(BF16)
            send(k).start()
        send(STEPS - 2).wait()
        send(STEPS - 1).wait()

    return pl.pallas_call(
        body,
        in_specs=[SMEM, VMEM, ANY, ANY] + [ANY] * count,
        out_specs=ANY,
        out_shape=jax.ShapeDtypeStruct((tokens, features), BF16),
        scratch_shapes=[
            pltpu.VMEM((columns, tokens), BF16),
            pltpu.VMEM((STEPS, columns, block), BF16),
            pltpu.VMEM((columns, tokens), BF16),
            pltpu.VMEM((2, tokens, block), BF16),
            pltpu.SemaphoreType.DMA((2,)),
            pltpu.SemaphoreType.DMA((STEPS, count)),
            pltpu.SemaphoreType.DMA((2,)),
        ],
        compiler_params=PARAMS,
        cost_estimate=cost(
            2 * columns * tokens * features, 2 * features * (columns + tokens) + 2 * columns * tokens
        ),
    )(starts, token_rows, *exps_t, *weights)


def head_block(starts, sides, low, columns_here, features, after):
    tokens = sides[0][2].shape[0]
    block = features // STEPS
    count = len(sides)

    def body(starts_ref, *refs):
        rows_refs, exps_refs, h_refs = refs[0 : 3 * count : 3], refs[1 : 3 * count : 3], refs[2 : 3 * count : 3]
        out_ref, exps, h, held, ready, e_sems, h_sems, sems = refs[3 * count + 1 :]
        first = [
            pltpu.make_async_copy(ref.at[pl.ds(low, columns_here)], exps.at[i], e_sems.at[i])
            for i, ref in enumerate(exps_refs)
        ]
        loads = [
            [
                pltpu.make_async_copy(
                    ref.at[:, pl.ds(k * block, block)], h.at[k, i], h_sems.at[k, i]
                )
                for i, ref in enumerate(h_refs)
            ]
            for k in range(STEPS)
        ]
        for copy in first + loads[0] + loads[1]:
            copy.start()
        for i in range(count):
            first[i].wait()
            held[i] = change_of(starts_ref, rows_refs[i], exps[i], low, columns_here, True)

        def send(k):
            return pltpu.make_async_copy(
                ready.at[k % 2], out_ref.at[:, pl.ds(k * block, block)], sems.at[k % 2]
            )

        for k in range(STEPS):
            if k + 2 < STEPS:
                for copy in loads[k + 2]:
                    copy.start()
            out = None
            for i in range(count):
                loads[k][i].wait()
                part = dot(held[i], h[k, i], ((1,), (0,)))
                out = part if out is None else out + part
            if k >= 2:
                send(k - 2).wait()
            ready[k % 2] = out.astype(BF16)
            send(k).start()
        send(STEPS - 2).wait()
        send(STEPS - 1).wait()

    return pl.pallas_call(
        body,
        in_specs=[SMEM] + [VMEM, ANY, ANY] * count + [ANY],
        out_specs=ANY,
        out_shape=jax.ShapeDtypeStruct((columns_here, features), BF16),
        scratch_shapes=[
            pltpu.VMEM((count, columns_here, tokens), BF16),
            pltpu.VMEM((STEPS, count, tokens, block), BF16),
            pltpu.VMEM((count, columns_here, tokens), BF16),
            pltpu.VMEM((2, columns_here, block), BF16),
            pltpu.SemaphoreType.DMA((count,)),
            pltpu.SemaphoreType.DMA((STEPS, count)),
            pltpu.SemaphoreType.DMA((2,)),
        ],
        compiler_params=PARAMS,
        cost_estimate=cost(
            2 * count * columns_here * tokens * features, 2 * features * (columns_here + count * tokens)
        ),
    )(starts, *(operand for side in sides for operand in side), after)


def cut_features(values, width):
    rows, features = values.shape
    count = features // width

    def body(in_ref, out_ref):
        values = in_ref[...]
        for i in range(count):
            out_ref[i] = values[:, i * width : (i + 1) * width]

    return pl.pallas_call(
        body,
        in_specs=[VMEM],
        out_specs=VMEM,
        out_shape=jax.ShapeDtypeStruct((count, rows, width), values.dtype),
        compiler_params=PARAMS,
        cost_estimate=cost(0, 4 * rows * features),
    )(values)


def pack_facts(token_ids, response_mask, teacher_logprob):
    high = lax.reduce_precision(teacher_logprob, 8, 7)
    rest = teacher_logprob - high
    middle = lax.reduce_precision(rest, 8, 7)
    fields = [
        token_ids // 16384,
        token_ids // 128 % 128,
        token_ids % 128,
        response_mask,
        high,
        middle,
        rest - middle,
    ]
    fields = jnp.stack([field.astype(F32) for field in fields], axis=1).astype(BF16)
    return jnp.pad(fields, ((0, 0), (0, LANES - fields.shape[1])))


def pick_one(values, *places):
    for place in places:
        values = lax.dynamic_index_in_dim(values, place, 0, False)
    return values


def on_device(hidden, weight, token_ids, response_mask, teacher_logprob):
    own_rows, features = hidden.shape
    columns_here = weight.shape[1]
    core, z = lax.axis_index("core"), lax.axis_index("z")
    xh, side, y = lax.axis_index("xh"), lax.axis_index("xl"), lax.axis_index("y")
    rows = own_rows // 2
    here = Z * rows
    lines = here // LANES
    tokens = own_rows * Z * CORES

    own = weight.T
    across = lax.ppermute(own, "xl", SWAP)
    own_other = lax.ppermute(own, "core", SWAP)
    facts = pack_facts(token_ids, response_mask, teacher_logprob)
    gathered = lax.all_gather(
        lax.dynamic_slice_in_dim(jnp.concatenate([hidden, facts], axis=1), side * rows, rows, 0),
        "z",
        axis=0,
        tiled=True,
    )
    weights = [own, across, own_other, lax.ppermute(across, "core", SWAP)]
    starts = jnp.stack(
        [
            (((z * CORES + c) * XH + xh) * XL + s) * Y * columns_here + y * columns_here
            for c in (core, 1 - core)
            for s in (side, 1 - side)
        ]
    ).astype(jnp.int32)

    mine, theirs, stats, copies, lined, gathered = logits_and_stats(starts, gathered, weights, columns_here)
    far_gathered = lax.ppermute(gathered, "core", SWAP)
    far_exps = lax.ppermute(theirs, "core", SWAP)
    shared = lax.all_to_all(copies, "z", 0, 0, tiled=True)
    shared = merge_stats(shared, lined, (far_gathered, far_exps))
    shared = lax.all_to_all(shared, ("xh", "y"), 0, 0, tiled=True)
    shared = shared.reshape(XH * Y, 3, lines, LANES)
    top = jnp.max(shared[:, 0], axis=0)
    total = jnp.sum(shared[:, 1] * jnp.exp(shared[:, 0] - top[None]), axis=0)
    norms = (top + jnp.log(total)).reshape(here)
    ratio = stats[3] * (jnp.sum(shared[:, 2], axis=0).reshape(here) - norms - stats[4])
    known = jnp.stack([stats[5], jnp.exp(stats[0] - norms), stats[3], ratio])

    partial = partial_product(starts, known, (mine, theirs), weights, columns_here)
    summed = lax.psum_scatter(partial, "z", scatter_dimension=0, tiled=True)
    cut = features // PLANE
    shares = cut_features(summed, cut)
    summed = lax.all_to_all(shares, ("xh", "xl", "y"), 0, 0, tiled=True)
    summed = summed.reshape(XH, XL, Y, rows, cut).astype(F32)
    summed = jnp.sum(summed, axis=(0, 2)).reshape(own_rows, cut)

    far = lax.ppermute(known, "core", SWAP)
    beside = lax.ppermute(known[2:], "xl", SWAP)
    opposite = lax.ppermute(known[2:], ("core", "xl"), [(i, 3 - i) for i in range(4)])
    mask, ratio = jnp.stack([known[2:], beside, far[2:], opposite], axis=1).reshape(
        2, CORES, XL, Z, rows
    )
    steps = jnp.arange(rows, dtype=jnp.int32)
    later = (steps[None, :] >= steps[:, None]).astype(F32)
    within = jnp.sum(ratio[..., None, :] * later, axis=-1)
    parts = jnp.sum(ratio, axis=-1).reshape(-1)
    order = jnp.arange(Z, dtype=jnp.int32) * (CORES * XL)
    order = jnp.concatenate(
        [order + (c * XL + s) for c in (core, 1 - core) for s in (side, 1 - side)]
    )
    beyond = jnp.sum(parts[None, :] * (order[None, :] > order[:, None]), axis=1)
    scales = mask * (within + beyond.reshape(CORES, XL, Z, 1)) / float(tokens)

    own_scale = lax.dynamic_index_in_dim(scales[0], z, 1, False)
    own_scale = jnp.where(side == 0, own_scale, own_scale[::-1]).reshape(own_rows)
    hidden_grad = summed * own_scale[:, None]

    scale = scales[:, 0].reshape(CORES, 1, here)
    rows_of = jnp.concatenate([jnp.stack([known[:2], far[:2]]), scale], axis=1)
    sides = [(rows_of[0], mine, gathered), (rows_of[1], far_exps, far_gathered)]
    given = head_block(starts, sides, columns_here, columns_here, features, partial)
    from_across = lax.ppermute(given, "xl", SWAP)
    kept = head_block(starts, sides, 0, columns_here, features, shares)
    head_grad = kept.astype(F32) + from_across.astype(F32)
    return hidden_grad.astype(BF16), head_grad.astype(BF16).T


def solution(mesh):
    names = ("z", "core", "xh", "xl", "y")
    fine = Mesh(mesh.devices.reshape(Z, CORES, XH, XL, Y), names)
    by_token, by_column = ("z", "core"), P(None, names)
    return jax.shard_map(
        on_device,
        mesh=fine,
        in_specs=(P(by_token, None), by_column, P(by_token), P(by_token), P(by_token)),
        out_specs=(P(by_token, names[2:]), by_column),
        check_vma=False,
    )
```
